256 devices in a mesh: span: 8 (over z_lo, core), dom: 32 (over x, y, z_hi).
Axes of the slice: x: 4, y: 4, z: 8 (z_hi: 2, z_lo: 4; z = z_hi * 4 + z_lo), core: 2. Of those that a mesh axis runs over, the one named last changes fastest.
Arguments:
- velocity_modes: float32 [3, 512, 20736], P(None, 'span', 'dom'), may hold values from -1.4 to 1.4
- metric: float32 [4, 20736], P(None, 'dom'), may hold values from -0.375 to 0.375
- pair_table: int32 [320, 4], P('dom'), may hold values from 0 to 7, as said below
- bound_table: int32 [256, 2], P('dom'), may hold values from 0 to 7, as said below
Outputs:
- advection: float32 [3, 512, 20736], P(None, 'span', 'dom')
The draws below stay inside these ranges and needn't reach their ends.
Inputs may be any that keep to these rules, and one draw needn't show every extreme that they name: Each partition's elements form a patch of 4 x 2 elements; every edge between two elements of the patch is listed once, with local element numbers, and no edge is listed twice in pair_table and bound_table together. `bound_table`: local element numbers and edge numbers.
All inputs are finite; a program needn't handle non-finite values.
Results may differ from the reference program's by a relative error of at most 0.00014.
Values sent between devices are 32-bit elements; how exact they have to be, the bound alone decides.
No kernel may reach another device: no remote copies, remote signals or barrier semaphores. Data moves between devices by JAX's collectives and lax.ppermute only.
A program may use at most 64 MiB of HBM per device.

```python
import math
import jax
import jax.numpy as jnp
import numpy as np
from jax import lax

NZ = 512
ER = 4
EC = 2
EL_DEV = 8
NE = 256
PAIRS = 10
N_DOM = 32


def mesh_tables(key):
    partitions = NE // (ER * EC)
    part_keys = jax.random.split(key, partitions)

    def one_part(part_key):
        order_key, turn_key = jax.random.split(part_key)
        numbering = jax.random.permutation(order_key, ER * EC).astype(jnp.int32)
        turning = jax.random.randint(turn_key, (ER * EC,), 0, 4, dtype=jnp.int32)
        across = (jnp.arange(ER, dtype=jnp.int32)[:, None] * EC + jnp.arange(EC - 1, dtype=jnp.int32)[None, :]).reshape(-1)
        radial = (jnp.arange(ER - 1, dtype=jnp.int32)[:, None] * EC + jnp.arange(EC, dtype=jnp.int32)[None, :]).reshape(-1)
        first_pos = jnp.concatenate([across, radial])
        second_pos = jnp.concatenate([across + 1, radial + EC])
        first_dir = jnp.concatenate([jnp.full(across.shape, 1, jnp.int32), jnp.full(radial.shape, 2, jnp.int32)])
        second_dir = jnp.concatenate([jnp.full(across.shape, 3, jnp.int32), jnp.full(radial.shape, 0, jnp.int32)])
        pair_rows = jnp.stack([numbering[first_pos], (first_dir + turning[first_pos]) % 4, numbering[second_pos], (second_dir + turning[second_pos]) % 4], -1)
        lower_pos = jnp.arange(ER, dtype=jnp.int32) * EC
        upper_pos = lower_pos + EC - 1
        bounds = jnp.stack([jnp.concatenate([numbering[lower_pos], numbering[upper_pos]]), jnp.concatenate([(3 + turning[lower_pos]) % 4, (1 + turning[upper_pos]) % 4])], -1)
        return (pair_rows, bounds)
    return jax.vmap(one_part)(part_keys)


def draw_pair_table(key, part):
    pair_rows, bounds = mesh_tables(key)
    return pair_rows.reshape(-1, 4).astype(jnp.int32)


def draw_bound_table(key, part):
    pair_rows, bounds = mesh_tables(key)
    return bounds.reshape(-1, 2).astype(jnp.int32)


def draw_velocity_modes(key, part):
    key = jax.random.fold_in(key, 11)
    slot_ids = jnp.arange(NZ, dtype=jnp.int32)[:, None]
    spread = 0.35 / (1.0 + (slot_ids // 2).astype(jnp.float32) / 8.0)
    base = jax.random.truncated_normal(key, -4.0, 4.0, (3, NZ, NE * 81), jnp.float32)
    return (base * spread).astype(jnp.float32)


def steps_of(own_key, shape, pieces, smallest, largest):
    factor_of, own = 1.0, jax.random.fold_in(own_key, 6)
    for position, parts in pieces:
        steps = jnp.exp(jax.random.uniform(jax.random.fold_in(own, position), (parts,), jnp.float32, smallest / len(pieces), largest / len(pieces)))
        factor_of = factor_of * jnp.repeat(steps, shape[position] // parts).reshape([-1 if axis == position else 1 for axis in range(len(shape))])
    return factor_of


def bell_draw(own_key, shape, deviation, most, pieces=(), kind=jnp.bfloat16):
    values = deviation * jax.random.normal(own_key, shape, jnp.float32)
    if pieces:
        values = values * steps_of(own_key, shape, pieces, -0.22, 0.18)
    return jnp.clip(values, -most, most).astype(kind)


def setup_inputs(seed: int = 0) -> dict:
    keys = jax.random.split(jax.random.key(seed), 5)
    velocity_modes = draw_velocity_modes(jax.random.fold_in(keys[4], 71), 0)
    metric = bell_draw(keys[1], (4, NE * 81), 0.06, 0.375, ((1, 32),), jnp.float32)
    pair_table = draw_pair_table(jax.random.fold_in(keys[4], 71), 0)
    bound_table = draw_bound_table(jax.random.fold_in(keys[4], 71), 0)
    return dict(velocity_modes=velocity_modes, metric=metric, pair_table=pair_table, bound_table=bound_table)


SPAN_RATE = 1.0 / 32.0


def legendre_rows(abscissa, node_count):
    legendre = np.zeros((node_count, node_count))
    legendre[:, 0] = 1.0
    legendre[:, 1] = abscissa
    for degree in range(2, node_count):
        legendre[:, degree] = ((2 * degree - 1) * abscissa * legendre[:, degree - 1] - (degree - 1) * legendre[:, degree - 2]) / degree
    return legendre


def lobatto_matrix(order):
    node_count = order + 1
    abscissa = -np.cos(np.pi * np.arange(node_count) / order)
    for iteration in range(60):
        legendre = legendre_rows(abscissa, node_count)
        abscissa = abscissa - (abscissa * legendre[:, order] - legendre[:, order - 1]) / (node_count * legendre[:, order])
    legendre = legendre_rows(abscissa, node_count)
    end_values = legendre[:, order]
    spacing = abscissa[:, None] - abscissa[None, :] + np.eye(node_count)
    matrix = end_values[:, None] / (end_values[None, :] * spacing)
    matrix = matrix * (1.0 - np.eye(node_count))
    matrix[0, 0] = -order * node_count / 4.0
    matrix[order, order] = order * node_count / 4.0
    return matrix


def grad_table():
    lobatto = lobatto_matrix(8)
    return np.concatenate([np.kron(np.eye(9), lobatto).T, np.kron(lobatto, np.eye(9)).T], axis=1)


def edge_table():
    positions = np.arange(9)
    outline = [positions, positions * 9 + 8, 72 + (8 - positions), (8 - positions) * 9]
    return np.stack(outline)[:, 1:8]


def spectral_tables(length):
    plane_ids = jnp.arange(length, dtype=jnp.int32)[:, None]
    slot_ids = jnp.arange(length, dtype=jnp.int32)[None, :]
    wavenum = jnp.where(slot_ids == 1, length // 2, slot_ids // 2)
    phases = (plane_ids * wavenum) % length
    angles = phases.astype(jnp.float32) * (2.0 * math.pi / length)
    sine_slot = (slot_ids % 2 == 1) & (slot_ids > 1)
    inverse_table = jnp.where(sine_slot, jnp.sin(angles), jnp.cos(angles))
    wave_rate = jnp.where(slot_ids == 1, 0, wavenum).astype(jnp.float32) * SPAN_RATE
    slope_table = wave_rate * jnp.where(sine_slot, jnp.cos(angles), -jnp.sin(angles))
    weight = jnp.where(slot_ids <= 1, 1.0 / length, 2.0 / length)
    forward_table = (inverse_table * weight).T
    return inverse_table, slope_table, forward_table


def plane_gradients(signal, metric):
    components, extent, points = signal.shape
    elements = points // 81
    flat_rows = signal.reshape(components * extent * elements, 81)
    table = jnp.asarray(grad_table(), jnp.float32)
    pair_grad = jnp.dot(flat_rows, table, precision=lax.Precision.HIGHEST)
    pair_grad = pair_grad.reshape(components, extent, elements, 162)
    along_xi = pair_grad[..., :81]
    along_eta = pair_grad[..., 81:]
    metrics = metric.reshape(4, 1, 1, elements, 81)
    dudx = metrics[0] * along_xi + metrics[2] * along_eta
    dudy = metrics[1] * along_xi + metrics[3] * along_eta
    return jnp.concatenate([dudx, dudy], 0).reshape(2 * components, extent, points)


def edge_inner(elements, edges):
    inner = jnp.asarray(edge_table(), jnp.int32)
    return (elements[:, None] * 81 + jnp.take(inner, edges, axis=0)).astype(jnp.int32)


def average_pairs(signal, first_side, second_side):
    own_side = signal[..., first_side]
    far_side = signal[..., second_side]
    average = (own_side + far_side) * 0.5
    return signal.at[..., first_side].set(average).at[..., second_side].set(average)


def reference(velocity_modes, metric, pair_table, bound_table):
    offsets = (jnp.arange(N_DOM * PAIRS, dtype=jnp.int32) // PAIRS) * EL_DEV
    first_side = edge_inner(offsets + pair_table[:, 0], pair_table[:, 1])
    second_side = edge_inner(offsets + pair_table[:, 2], pair_table[:, 3])[:, ::-1]
    side_rows = bound_table.reshape(N_DOM, 2, ER, 2)
    part_base = (jnp.arange(N_DOM, dtype=jnp.int32) * EL_DEV)[:, None]
    lower_side = edge_inner((part_base + side_rows[:, 0, :, 0]).reshape(-1), side_rows[:, 0, :, 1].reshape(-1))
    upper_side = edge_inner((part_base + side_rows[:, 1, :, 0]).reshape(-1), side_rows[:, 1, :, 1].reshape(-1))
    upper_prior = jnp.roll(upper_side.reshape(N_DOM, ER, 7), 1, axis=0).reshape(-1, 7)[:, ::-1]
    first_all = jnp.concatenate([first_side, lower_side], 0)
    second_all = jnp.concatenate([second_side, upper_prior], 0)
    gradient = average_pairs(plane_gradients(velocity_modes, metric), first_all, second_all)
    inverse_table, slope_table, forward_table = spectral_tables(NZ)
    highest = lax.Precision.HIGHEST
    physical = jnp.einsum("zm,fmp->fzp", inverse_table, velocity_modes, precision=highest)
    span_slope = jnp.einsum("zm,fmp->fzp", slope_table, velocity_modes, precision=highest)
    physical_grad = jnp.einsum("zm,fmp->fzp", inverse_table, gradient, precision=highest)
    advect = physical[0] * physical_grad[0:3] + physical[1] * physical_grad[3:6] + physical[2] * span_slope
    spectra = jnp.einsum("mz,fzp->fmp", forward_table, advect, precision=highest)
    return average_pairs(spectra, first_all, second_all)
```

```python
import jax
import jax.numpy as jnp
import ml_dtypes
import numpy as np
from jax import lax
from jax.experimental import pallas as pl
from jax.experimental.pallas import tpu as pltpu
from jax.sharding import PartitionSpec as P

NZ = 512
PTS = 81
ELEMS = 8
ROWS = 4
PAIRS = 10
SPAN = 8
MODES = NZ // SPAN
SPAN_RATE = 1.0 / 32.0
BF = jnp.bfloat16
F32 = jnp.float32
LIMIT = 48 * 1024 * 1024


def legendre_rows(abscissa, node_count):
    legendre = np.zeros((node_count, node_count))
    legendre[:, 0] = 1.0
    legendre[:, 1] = abscissa
    for degree in range(2, node_count):
        legendre[:, degree] = (
            (2 * degree - 1) * abscissa * legendre[:, degree - 1]
            - (degree - 1) * legendre[:, degree - 2]
        ) / degree
    return legendre


def lobatto_matrix(order):
    node_count = order + 1
    abscissa = -np.cos(np.pi * np.arange(node_count) / order)
    for _ in range(60):
        legendre = legendre_rows(abscissa, node_count)
        abscissa = abscissa - (abscissa * legendre[:, order] - legendre[:, order - 1]) / (
            node_count * legendre[:, order]
        )
    legendre = legendre_rows(abscissa, node_count)
    end_values = legendre[:, order]
    spacing = abscissa[:, None] - abscissa[None, :] + np.eye(node_count)
    matrix = end_values[:, None] / (end_values[None, :] * spacing)
    matrix = matrix * (1.0 - np.eye(node_count))
    matrix[0, 0] = -order * node_count / 4.0
    matrix[order, order] = order * node_count / 4.0
    return matrix


def edge_points():
    positions = np.arange(9)
    outline = [positions, positions * 9 + 8, 72 + (8 - positions), (8 - positions) * 9]
    return np.stack(outline)[:, 1:8]


def halves(table):
    high = table.astype(np.float32).astype(ml_dtypes.bfloat16)
    low = (table - high.astype(np.float64)).astype(np.float32).astype(ml_dtypes.bfloat16)
    return high, low


def span_tables():
    planes = np.arange(NZ)[None, :]
    slots = np.arange(NZ)[:, None]
    waves = np.where(slots == 1, NZ // 2, slots // 2)
    angles = (planes * waves % NZ) * (2.0 * np.pi / NZ)
    sine = (slots % 2 == 1) & (slots > 1)
    value = np.where(sine, np.sin(angles), np.cos(angles))
    rate = np.where(slots == 1, 0, waves) * SPAN_RATE
    slope = rate * np.where(sine, np.cos(angles), -np.sin(angles))
    return value, slope


def point_matrices():
    lobatto = lobatto_matrix(8)
    return np.kron(np.eye(9), lobatto), np.kron(lobatto, np.eye(9))


def gradient_table():
    along_xi, along_eta = point_matrices()
    table = np.zeros((176, 96))
    table[:81, :81] = along_xi
    table[88:169, :81] = along_eta
    return table


def edge_tables():
    edges = edge_points()
    mats = point_matrices()
    table = np.zeros((256, 1024))
    pick = np.zeros((256, 512))
    for s in range(4):
        for t in range(3):
            for c in range(3):
                for xy in range(2):
                    for i in range(7):
                        lane = s * 128 + t * 42 + c * 14 + xy * 7 + i
                        for h in range(2):
                            table[c * 81 : c * 81 + 81, h * 512 + lane] = mats[h][edges[s, i]]
                        pick[xy * 128 + edges[s, i], lane] = 1.0
    return table, pick


def settle_tables():
    edges = edge_points()
    take = np.zeros((256, 128))
    give = np.zeros((128, 256))
    where = np.zeros((8, 256))
    for s in range(4):
        for c in range(3):
            for i in range(7):
                lane = s * 21 + c * 7 + i
                take[c * 81 + edges[s, 6 - i], lane] = 1.0
                give[lane, c * 81 + edges[s, i]] = 0.5
                where[s, c * 81 + edges[s, i]] = 0.5
    return take, give, where


def row_of(place, part):
    return (place & 1) * ROWS + ((place >> 1) ^ (3 * (part & 1)))


def split(x):
    high = x.astype(BF)
    return high, (x - high.astype(F32)).astype(BF)


def dot(a, b, dims=((1,), (0,))):
    return lax.dot_general(a, b, (dims, ((), ())), preferred_element_type=F32)


def edge_start(edge):
    base = jnp.where(edge == 0, 1, jnp.where(edge == 1, 17, jnp.where(edge == 2, 79, 63)))
    step = jnp.where(edge == 0, 1, jnp.where(edge == 1, 9, jnp.where(edge == 2, -1, -9)))
    return base, step


def list_pairs(pair, count, own, other, other_edge):
    for e in range(ELEMS):
        count[e] = 0
    for n in range(ELEMS * 4):
        own[n] = -1
        other[n] = 0
        other_edge[n] = 0
    for row in range(PAIRS):
        for first, second in ((0, 2), (2, 0)):
            e = pair[row, first]
            slot = e * 4 + count[e]
            own[slot] = pair[row, first + 1]
            other[slot] = pair[row, second]
            other_edge[slot] = pair[row, second + 1]
            count[e] = count[e] + 1


def pack_kernel(bound, v, packed, *outs):
    me, part = lax.axis_index("span"), lax.axis_index("dom")
    for e in range(ELEMS):
        for c in range(3):
            packed[e, :, c * 81 : c * 81 + 81] = v[c, :, e * 81 : e * 81 + 81]
        packed[e, :, 243:256] = jnp.zeros((MODES, 13), F32)
    for k in range(SPAN):
        outs[k][...] = packed[bound[row_of(me ^ k, part), 0]]


def edge_kernel(bound, pair, packed, metric, high, low, pick, columns, *rest):
    outs = rest[:SPAN]
    grads, rows, lines, square, count, own, other, other_edge = rest[SPAN:]
    me, part = lax.axis_index("span"), lax.axis_index("dom")
    list_pairs(pair, count, own, other, other_edge)
    rows[...] = jnp.zeros((16, 256), F32)
    for e in range(ELEMS):
        for j in range(4):
            at = e + 8 * (j // 2)
            lane = 128 * (j % 2)
            rows[at : at + 1, lane : lane + 81] = metric[j : j + 1, e * 81 : e * 81 + 81]
    rows_high, rows_low = split(rows[...])
    scale = dot(rows_high, pick[...]) + dot(rows_low, pick[...])
    values_high, values_low = split(packed[...].reshape(ELEMS * MODES, 256))
    for s in range(4):
        lanes = pl.ds(s * 128, 128)
        parts = []
        for h in range(2):
            at = pl.ds(h * 512 + s * 128, 128)
            parts.append(
                dot(values_high, high[:, at])
                + dot(values_low, high[:, at])
                + dot(values_high, low[:, at])
            )
        for e in range(ELEMS):
            span = slice(e * MODES, (e + 1) * MODES)
            grads[e, s] = (
                parts[0][span] * scale[e : e + 1, s * 128 : s * 128 + 128]
                + parts[1][span] * scale[8 + e : 9 + e, s * 128 : s * 128 + 128]
            )
    lane = lax.broadcasted_iota(jnp.int32, (MODES, 128), 1)
    for k in range(SPAN):
        e = bound[row_of(me ^ k, part), 0]
        picked = [grads[other[e * 4 + t], other_edge[e * 4 + t]] for t in range(3)]
        outs[k][...] = jnp.where(lane < 42, picked[0], jnp.where(lane < 84, picked[1], picked[2]))
    mine = bound[row_of(me, part), 0]
    for n in range(16):
        lines[n] = rows[n : n + 1, :]
    square[...] = jnp.zeros((128, 128), F32)
    for j in range(4):
        line = lines[mine + 8 * (j // 2)]
        square[j : j + 1, :] = line[:, 128 * (j % 2) : 128 * (j % 2) + 128]
    columns[...] = square[...].T


def element_kernel(bound, *rest):
    blocks = rest[:SPAN]
    columns, th, tl, dh, dl, gh, gl = rest[SPAN : SPAN + 7]
    send, mine, u, q, g, modes, value, slope, fields = rest[SPAN + 7 :]
    me, part = lax.axis_index("span"), lax.axis_index("dom")
    for k in range(SPAN):
        modes[pl.ds(pl.multiple_of((me ^ k) * MODES, MODES), MODES), :] = blocks[k][...]
    vh, vl = split(modes[...].T)
    value[0:256] = dot(vh, th[...]) + dot(vl, th[...]) + dot(vh, tl[...])
    slope[0:256] = dot(vh, dh[...]) + dot(vl, dh[...]) + dot(vh, dl[...])
    value[256:264] = jnp.zeros((8, NZ), F32)
    slope[256:264] = jnp.zeros((8, NZ), F32)
    third = value[162:250]
    for c in range(3):
        uh, ul = split(value[81 * c : 81 * c + 96])
        both = dot(gh[...], uh) + dot(gh[...], ul) + dot(gl[...], uh)
        fx, fe = both[:88], both[88:]
        g[c] = columns[0:88, 0:1] * fx + columns[0:88, 2:3] * fe
        g[3 + c] = columns[0:88, 1:2] * fx + columns[0:88, 3:4] * fe
        u[c] = value[81 * c : 81 * c + 88]
        q[c] = third * slope[81 * c : 81 * c + 88]
    base, step = edge_start(bound[row_of(me, part), 1])
    send[...] = jnp.zeros((88, NZ), F32)
    mine[...] = jnp.zeros((88, NZ), F32)
    order = [(g, f) for f in range(6)] + [(u, 0), (u, 1)] + [(q, c) for c in range(3)]
    for f, (ref, at) in enumerate(order):
        for i in range(7):
            line = ref[at, pl.ds(base + step * i, 1), :]
            mine[f * 8 + i : f * 8 + i + 1, :] = line
            send[f * 8 + 6 - i : f * 8 + 7 - i, :] = line


def term_kernel(bound, pair, *rest):
    blocks = rest[:SPAN]
    th, tl, u, q, g, term, modes, count, own, other, other_edge = rest[SPAN:]
    me, part = lax.axis_index("span"), lax.axis_index("dom")
    list_pairs(pair, count, own, other, other_edge)
    for k in range(SPAN):
        modes[pl.ds(pl.multiple_of((me ^ k) * MODES, MODES), MODES), :] = blocks[k][...]
    eh, el = split(modes[...].T)
    planes = dot(eh, th[...]) + dot(el, th[...]) + dot(eh, tl[...])
    ph, pw = split(planes)
    e = bound[row_of(me, part), 0]
    lane = lax.broadcasted_iota(jnp.int32, (88, 128), 1)
    point = lax.broadcasted_iota(jnp.int32, (88, 128), 0)
    slot = jnp.where(lane < 42, 0, jnp.where(lane < 84, 1, 2))
    starts = []
    for t in range(3):
        edge = own[e * 4 + t]
        base, step = edge_start(edge)
        starts.append((jnp.where(edge < 0, -1000, base), step))
    base = jnp.where(slot == 0, starts[0][0], jnp.where(slot == 1, starts[1][0], starts[2][0]))
    step = jnp.where(slot == 0, starts[0][1], jnp.where(slot == 1, starts[1][1], starts[2][1]))
    place = lane - slot * 42
    takes = []
    for f in range(6):
        xy, c = f // 3, f % 3
        i = 6 - (place - (c * 14 + xy * 7))
        hit = (i >= 0) & (i <= 6) & (lane < 126) & (point == base + step * i)
        takes.append(jnp.where(hit, 0.5, 0.0))
    keep = 1.0 - jnp.sum(takes[0], axis=1, keepdims=True)
    take = jnp.concatenate(takes, axis=0).astype(BF)
    far = dot(take, ph) + dot(take, pw)
    for c in range(3):
        value = (
            u[0] * (g[c] * keep + far[c * 88 : c * 88 + 88])
            + u[1] * (g[3 + c] * keep + far[(3 + c) * 88 : (3 + c) * 88 + 88])
            + q[c]
        )
        term[81 * c : 81 * c + 81, :] = value[:81]
    term[243:256, :] = jnp.zeros((13, NZ), F32)


def spectra_kernel(bound, term, mine, other, th, tl, *rest):
    outs = rest[:SPAN]
    work, spec = rest[SPAN:]
    me, part = lax.axis_index("span"), lax.axis_index("dom")
    work[...] = term[...]
    m = [mine[f * 8 : f * 8 + 8, :] for f in range(11)]
    r = [other[f * 8 : f * 8 + 8, :] for f in range(11)]
    base, step = edge_start(bound[row_of(me, part), 1])
    for c in range(3):
        gx = (m[c] + r[c]) * 0.5
        gy = (m[3 + c] + r[3 + c]) * 0.5
        value = (
            (m[6] * gx + m[7] * gy + m[8 + c]) + (r[6] * gx + r[7] * gy + r[8 + c])
        ) * 0.5
        for i in range(7):
            work[pl.ds(81 * c + base + step * i, 1), :] = value[i : i + 1, :]
    wh, wl = split(work[...])
    along = ((1,), (1,))
    total = dot(th[...], wh, along) + dot(th[...], wl, along) + dot(tl[...], wh, along)
    slot = lax.broadcasted_iota(jnp.int32, (NZ, 256), 0)
    spec[...] = total * jnp.where(slot < 2, 1.0 / NZ, 2.0 / NZ)
    for k in range(SPAN):
        outs[k][...] = spec[pl.ds(pl.multiple_of((me ^ k) * MODES, MODES), MODES), :]


def settle_kernel(bound, pair, *rest):
    blocks = rest[:SPAN]
    take, give, where, out, packed, edges, far, count, own, other, other_edge = rest[SPAN:]
    me, part = lax.axis_index("span"), lax.axis_index("dom")
    list_pairs(pair, count, own, other, other_edge)
    for k in range(SPAN):
        packed[bound[row_of(me ^ k, part), 0]] = blocks[k][...]
    ph, pw = split(packed[...].reshape(ELEMS * MODES, 256))
    edges[...] = (dot(ph, take[...]) + dot(pw, take[...])).reshape(ELEMS, MODES, 128)
    lane = lax.broadcasted_iota(jnp.int32, (MODES, 128), 1)
    for e in range(ELEMS):
        total = jnp.zeros((MODES, 128), F32)
        for t in range(3):
            edge = own[e * 4 + t]
            shift = (21 * (edge - other_edge[e * 4 + t]) + 128) & 127
            turned = pltpu.roll(edges[other[e * 4 + t]], shift, 1)
            low = edge * 21
            total = jnp.where((lane >= low) & (lane < low + 21) & (edge >= 0), turned, total)
        far[e] = total
    fh, fl = split(far[...].reshape(ELEMS * MODES, 128))
    given = dot(fh, give[...]) + dot(fl, give[...])
    for e in range(ELEMS):
        keep = jnp.ones((1, 256), F32)
        for t in range(3):
            edge = own[e * 4 + t]
            row = where[pl.ds(jnp.maximum(edge, 0), 1), :]
            keep = keep - jnp.where(edge >= 0, row, 0.0)
        done = packed[e] * keep + given[e * MODES : (e + 1) * MODES]
        for c in range(3):
            out[c, :, e * 81 : e * 81 + 81] = done[:, c * 81 : c * 81 + 81]


def spec_of(space):
    return pl.BlockSpec(memory_space=space)


def call(kernel, name, scalars, arrays, outs, scratch=()):
    shapes = [jax.ShapeDtypeStruct(shape, F32) for shape in outs]
    return pl.pallas_call(
        kernel,
        out_shape=shapes,
        in_specs=[spec_of(pltpu.SMEM)] * len(scalars) + [spec_of(pltpu.VMEM)] * len(arrays),
        out_specs=[spec_of(pltpu.VMEM)] * len(outs),
        scratch_shapes=list(scratch),
        compiler_params=pltpu.CompilerParams(vmem_limit_bytes=LIMIT),
        name=name,
    )(*scalars, *arrays)


def pair_scratch():
    return [pltpu.SMEM((n,), jnp.int32) for n in (ELEMS, ELEMS * 4, ELEMS * 4, ELEMS * 4)]


def exchange(blocks):
    return [blocks[0]] + [
        lax.ppermute(blocks[k], "span", [(s, s ^ k) for s in range(SPAN)])
        for k in range(1, SPAN)
    ]


def side_swap(block, parts):
    def device(part, row, side):
        return ((row ^ (3 * (part & 1))) * 2 + side) * parts + part

    perm = []
    for part in range(parts):
        before = (part - 1) % parts
        for row in range(ROWS):
            perm.append((device(part, row, 0), device(before, row, 1)))
            perm.append((device(before, row, 1), device(part, row, 0)))
    return lax.ppermute(block, ("span", "dom"), perm)


def on_device(velocity_modes, metric, pair_table, bound_table):
    value, slope = span_tables()
    th, tl = halves(value)
    dh, dl = halves(slope)
    gh, gl = halves(gradient_table())
    edge_values, edge_pick = edge_tables()
    ah, al = halves(edge_values)
    pick = halves(edge_pick)[0]
    take, give, where = settle_tables()
    block, edge_block = (MODES, 256), (MODES, 128)

    packed, *blocks = call(
        pack_kernel, "pack", [bound_table], [velocity_modes], [(ELEMS, MODES, 256)] + [block] * SPAN
    )
    blocks = exchange(blocks)
    columns, *edge_blocks = call(
        edge_kernel,
        "edges",
        [bound_table, pair_table],
        [packed, metric, ah, al, pick],
        [(128, 128)] + [edge_block] * SPAN,
        [pltpu.VMEM((ELEMS, 4, MODES, 128), F32), pltpu.VMEM((16, 256), F32), pltpu.VMEM((16, 1, 256), F32), pltpu.VMEM((128, 128), F32)]
        + pair_scratch(),
    )
    edge_blocks = exchange(edge_blocks)
    send, mine, u, q, g = call(
        element_kernel,
        "element",
        [bound_table],
        [*blocks, columns, th, tl, dh, dl, gh, gl],
        [(88, NZ), (88, NZ), (3, 88, NZ), (3, 88, NZ), (6, 88, NZ)],
        [pltpu.VMEM((NZ, 256), F32), pltpu.VMEM((264, NZ), F32), pltpu.VMEM((264, NZ), F32), pltpu.VMEM((8, NZ), F32)],
    )
    other = side_swap(send, lax.axis_size("dom"))
    (term,) = call(
        term_kernel,
        "term",
        [bound_table, pair_table],
        [*edge_blocks, th, tl, u, q, g],
        [(256, NZ)],
        [pltpu.VMEM((NZ, 128), F32)] + pair_scratch(),
    )
    blocks = call(
        spectra_kernel,
        "spectra",
        [bound_table],
        [term, mine, other, th, tl],
        [block] * SPAN,
        [pltpu.VMEM((256, NZ), F32), pltpu.VMEM((NZ, 256), F32)],
    )
    blocks = exchange(blocks)
    (out,) = call(
        settle_kernel,
        "settle",
        [bound_table, pair_table],
        [*blocks, halves(take)[0], halves(give)[0], where.astype(np.float32)],
        [(3, MODES, ELEMS * PTS)],
        [pltpu.VMEM((ELEMS, MODES, 256), F32), pltpu.VMEM((ELEMS, MODES, 128), F32), pltpu.VMEM((ELEMS, MODES, 128), F32)]
        + pair_scratch(),
    )
    return out


def solution(mesh):
    return jax.shard_map(
        on_device,
        mesh=mesh,
        in_specs=(P(None, "span", "dom"), P(None, "dom"), P("dom", None), P("dom", None)),
        out_specs=P(None, "span", "dom"),
        check_vma=False,
    )
```

```python
import jax
import jax.numpy as jnp
import ml_dtypes
import numpy as np
from jax import lax
from jax.experimental import pallas as pl
from jax.experimental.pallas import tpu as pltpu
from jax.sharding import PartitionSpec as P

NZ = 512
PTS = 81
ELEMS = 8
ROWS = 4
PAIRS = 10
SPAN = 8
MODES = NZ // SPAN
SPAN_RATE = 1.0 / 32.0
BF = jnp.bfloat16
F32 = jnp.float32
LIMIT = 48 * 1024 * 1024


def legendre_rows(abscissa, node_count):
    legendre = np.zeros((node_count, node_count))
    legendre[:, 0] = 1.0
    legendre[:, 1] = abscissa
    for degree in range(2, node_count):
        legendre[:, degree] = (
            (2 * degree - 1) * abscissa * legendre[:, degree - 1]
            - (degree - 1) * legendre[:, degree - 2]
        ) / degree
    return legendre


def lobatto_matrix(order):
    node_count = order + 1
    abscissa = -np.cos(np.pi * np.arange(node_count) / order)
    for _ in range(60):
        legendre = legendre_rows(abscissa, node_count)
        abscissa = abscissa - (abscissa * legendre[:, order] - legendre[:, order - 1]) / (
            node_count * legendre[:, order]
        )
    legendre = legendre_rows(abscissa, node_count)
    end_values = legendre[:, order]
    spacing = abscissa[:, None] - abscissa[None, :] + np.eye(node_count)
    matrix = end_values[:, None] / (end_values[None, :] * spacing)
    matrix = matrix * (1.0 - np.eye(node_count))
    matrix[0, 0] = -order * node_count / 4.0
    matrix[order, order] = order * node_count / 4.0
    return matrix


def edge_points():
    positions = np.arange(9)
    outline = [positions, positions * 9 + 8, 72 + (8 - positions), (8 - positions) * 9]
    return np.stack(outline)[:, 1:8]


def halves(table):
    high = table.astype(np.float32).astype(ml_dtypes.bfloat16)
    low = (table - high.astype(np.float64)).astype(np.float32).astype(ml_dtypes.bfloat16)
    return high, low


def span_tables():
    planes = np.arange(NZ)[None, :]
    slots = np.arange(NZ)[:, None]
    waves = np.where(slots == 1, NZ // 2, slots // 2)
    angles = (planes * waves % NZ) * (2.0 * np.pi / NZ)
    sine = (slots % 2 == 1) & (slots > 1)
    value = np.where(sine, np.sin(angles), np.cos(angles))
    rate = np.where(slots == 1, 0, waves) * SPAN_RATE
    slope = rate * np.where(sine, np.cos(angles), -np.sin(angles))
    return value, slope


def point_matrices():
    lobatto = lobatto_matrix(8)
    return np.kron(np.eye(9), lobatto), np.kron(lobatto, np.eye(9))


def gradient_table():
    along_xi, along_eta = point_matrices()
    table = np.zeros((176, 96))
    table[:81, :81] = along_xi
    table[88:169, :81] = along_eta
    return table


def edge_tables():
    edges = edge_points()
    mats = point_matrices()
    table = np.zeros((256, 1024))
    pick = np.zeros((256, 512))
    for s in range(4):
        for t in range(3):
            for c in range(3):
                for xy in range(2):
                    for i in range(7):
                        lane = s * 128 + t * 42 + c * 14 + xy * 7 + i
                        for h in range(2):
                            table[c * 81 : c * 81 + 81, h * 512 + lane] = mats[h][edges[s, i]]
                        pick[xy * 128 + edges[s, i], lane] = 1.0
    high, low = halves(table)
    pick = halves(pick)[0]
    lanes = [slice(s * 128, s * 128 + 128) for s in range(4)]
    later = [slice(512 + s * 128, 640 + s * 128) for s in range(4)]
    return np.stack(
        [
            np.concatenate([high[:, n], high[:, m], low[:, n], low[:, m]], axis=1)
            for n, m in zip(lanes, later)
        ]
    ), pick


def settle_tables():
    edges = edge_points()
    take = np.zeros((256, 128))
    give = np.zeros((128, 256))
    where = np.zeros((8, 256))
    put = np.zeros((4, 32, 256))
    for s in range(4):
        for c in range(3):
            for i in range(7):
                lane = s * 21 + c * 7 + i
                take[c * 81 + edges[s, 6 - i], lane] = 1.0
                give[lane, c * 81 + edges[s, i]] = 0.5
                where[s, c * 81 + edges[s, i]] = 0.5
                put[s, c * 8 + i, c * 81 + edges[s, i]] = 1.0
    return take, give, where, put


def row_of(place, part):
    return (place & 1) * ROWS + ((place >> 1) ^ (3 * (part & 1)))


def split(x):
    high = x.astype(BF)
    return high, (x - high.astype(F32)).astype(BF)


def dot(a, b, dims=((1,), (0,))):
    return lax.dot_general(a, b, (dims, ((), ())), preferred_element_type=F32)


def edge_start(edge):
    base = jnp.where(edge == 0, 1, jnp.where(edge == 1, 17, jnp.where(edge == 2, 79, 63)))
    step = jnp.where(edge == 0, 1, jnp.where(edge == 1, 9, jnp.where(edge == 2, -1, -9)))
    return base, step


def list_pairs(pair, count, own, other, other_edge):
    for e in range(ELEMS):
        count[e] = 0
    for n in range(ELEMS * 4):
        own[n] = -1
        other[n] = 0
        other_edge[n] = 0
    for row in range(PAIRS):
        for first, second in ((0, 2), (2, 0)):
            e = pair[first, row]
            slot = e * 4 + count[e]
            own[slot] = pair[first + 1, row]
            other[slot] = pair[second, row]
            other_edge[slot] = pair[second + 1, row]
            count[e] = count[e] + 1


def chip_modes(j):
    chip = (lax.axis_index("span") >> 1) ^ j
    return pl.ds(pl.multiple_of(chip * 2 * MODES, 2 * MODES), 2 * MODES)


def metric_kernel(bound, pair, metric, pick, scale, columns, ready, rows, lines, square):
    me, part = lax.axis_index("span"), lax.axis_index("dom")
    rows[...] = jnp.zeros((16, 256), F32)
    for e in range(ELEMS):
        for j in range(4):
            at = e + 8 * (j // 2)
            lane = 128 * (j % 2)
            rows[at : at + 1, lane : lane + 81] = metric[j : j + 1, e * 81 : e * 81 + 81]
    rows_high, rows_low = split(rows[...])
    for s in range(4):
        here = pick[:, s * 128 : s * 128 + 128]
        size = dot(rows_high, here) + dot(rows_low, here)
        for n in range(16):
            scale[n * 4 + s] = size[n : n + 1, :]
    for n in range(16):
        lines[n] = rows[n : n + 1, :]
    square[...] = jnp.zeros((128, 128), F32)
    mine = bound[0, row_of(me, part)]
    for j in range(4):
        line = lines[mine + 8 * (j // 2)]
        square[j : j + 1, :] = line[:, 128 * (j % 2) : 128 * (j % 2) + 128]
    columns[...] = square[...].T
    ready[...] = jnp.full((8, 128), pair[0, 0], jnp.int32).astype(F32)


def pack_element(packed, e, core, here, there):
    for at, v in ((core, here), (1 - core, there)):
        rows = pl.ds(pl.multiple_of(at * MODES, MODES), MODES)
        for c in range(3):
            packed[e, rows, c * 81 : c * 81 + 81] = v[c, :, e * 81 : e * 81 + 81]
        packed[e, rows, 243:256] = jnp.zeros((MODES, 13), F32)


def column_flags(bound, core, flags):
    for e in range(ELEMS):
        flags[e] = 0
    for row in range(ROWS):
        flags[bound[0, core * ROWS + row]] = 1


def pack_kernel(bound, here, there, ready, packed, *rest):
    outs, flags = rest[:4], rest[4]
    me, part = lax.axis_index("span"), lax.axis_index("dom")
    core = me & 1
    column_flags(bound, core, flags)
    for e in range(ELEMS):
        pl.when(flags[e] == 1)(lambda e=e: pack_element(packed, e, core, here, there))
    for j in range(4):
        outs[j][...] = packed[bound[0, row_of(me ^ (2 * j), part)]]


def edge_kernel(bound, pair, done, here, there, scale, table, *rest):
    outs = rest[:4]
    packed, flags, count, own, other, other_edge = rest[4:]
    me, part = lax.axis_index("span"), lax.axis_index("dom")
    core = me & 1
    column_flags(bound, core, flags)
    list_pairs(pair, count, own, other, other_edge)

    def copy_element(e):
        packed[e] = done[e]

    for e in range(ELEMS):
        pl.when(flags[e] == 1)(lambda e=e: copy_element(e))
        pl.when(flags[e] == 0)(lambda e=e: pack_element(packed, e, core, here, there))
    lane = lax.broadcasted_iota(jnp.int32, (2 * MODES, 128), 1)
    for j in range(4):
        e = bound[0, row_of(me ^ (2 * j), part)]
        total = jnp.zeros((2 * MODES, 128), F32)
        for t in range(3):
            far, edge = other[e * 4 + t], other_edge[e * 4 + t]
            vh, vl = split(packed[far])
            high = table[edge, :, 0:256]
            value = dot(vh, high) + dot(vl, high) + dot(vh, table[edge, :, 256:512])
            value = (
                value[:, :128] * scale[far * 4 + edge]
                + value[:, 128:] * scale[(8 + far) * 4 + edge]
            )
            total = jnp.where((lane >= t * 42) & (lane < t * 42 + 42), value, total)
        outs[j][...] = total


def element_kernel(bound, *rest):
    blocks = rest[:4]
    columns, th, tl, dh, dl, gh, gl = rest[4:11]
    send, mine, u, q, g, modes, value, slope = rest[11:]
    me, part = lax.axis_index("span"), lax.axis_index("dom")
    for j in range(4):
        modes[chip_modes(j), :] = blocks[j][...]
    vh, vl = split(modes[...].T)
    value[0:256] = dot(vh, th[...]) + dot(vl, th[...]) + dot(vh, tl[...])
    slope[0:256] = dot(vh, dh[...]) + dot(vl, dh[...]) + dot(vh, dl[...])
    value[256:264] = jnp.zeros((8, NZ), F32)
    slope[256:264] = jnp.zeros((8, NZ), F32)
    third = value[162:250]
    for c in range(3):
        uh, ul = split(value[81 * c : 81 * c + 96])
        both = dot(gh[...], uh) + dot(gh[...], ul) + dot(gl[...], uh)
        fx, fe = both[:88], both[88:]
        g[c] = columns[0:88, 0:1] * fx + columns[0:88, 2:3] * fe
        g[3 + c] = columns[0:88, 1:2] * fx + columns[0:88, 3:4] * fe
        u[c] = value[81 * c : 81 * c + 88]
        q[c] = third * slope[81 * c : 81 * c + 88]
    base, step = edge_start(bound[1, row_of(me, part)])
    send[77:80] = jnp.zeros((3, NZ), F32)
    mine[77:80] = jnp.zeros((3, NZ), F32)
    order = [(g, f) for f in range(6)] + [(u, 0), (u, 1)] + [(q, c) for c in range(3)]
    for f, (ref, at) in enumerate(order):
        for i in range(7):
            line = ref[at, pl.ds(base + step * i, 1), :]
            mine[f * 7 + i : f * 7 + i + 1, :] = line
            send[f * 7 + 6 - i : f * 7 + 7 - i, :] = line


def term_kernel(bound, pair, *rest):
    blocks = rest[:4]
    th, tl, u, q, g, term, modes, count, own, other, other_edge = rest[4:]
    me, part = lax.axis_index("span"), lax.axis_index("dom")
    list_pairs(pair, count, own, other, other_edge)
    for j in range(4):
        modes[chip_modes(j), :] = blocks[j][...]
    eh, el = split(modes[...].T)
    planes = dot(eh, th[...]) + dot(el, th[...]) + dot(eh, tl[...])
    ph, pw = split(planes)
    e = bound[0, row_of(me, part)]
    lane = lax.broadcasted_iota(jnp.int32, (88, 128), 1)
    point = lax.broadcasted_iota(jnp.int32, (88, 128), 0)
    slot = jnp.where(lane < 42, 0, jnp.where(lane < 84, 1, 2))
    starts = []
    for t in range(3):
        edge = own[e * 4 + t]
        base, step = edge_start(edge)
        starts.append((jnp.where(edge < 0, -1000, base), step))
    base = jnp.where(slot == 0, starts[0][0], jnp.where(slot == 1, starts[1][0], starts[2][0]))
    step = jnp.where(slot == 0, starts[0][1], jnp.where(slot == 1, starts[1][1], starts[2][1]))
    place = lane - slot * 42
    takes = []
    for f in range(6):
        xy, c = f // 3, f % 3
        i = 6 - (place - (c * 14 + xy * 7))
        hit = (i >= 0) & (i <= 6) & (lane < 126) & (point == base + step * i)
        takes.append(jnp.where(hit, 0.5, 0.0))
    keep = 1.0 - jnp.sum(takes[0], axis=1, keepdims=True)
    take = jnp.concatenate(takes, axis=0).astype(BF)
    far = dot(take, ph) + dot(take, pw)
    for c in range(3):
        value = (
            u[0] * (g[c] * keep + far[c * 88 : c * 88 + 88])
            + u[1] * (g[3 + c] * keep + far[(3 + c) * 88 : (3 + c) * 88 + 88])
            + q[c]
        )
        term[81 * c : 81 * c + 81, :] = value[:81]
    term[243:256, :] = jnp.zeros((13, NZ), F32)


def spectra_kernel(term, th, tl, *rest):
    outs = rest[:4]
    (spec,) = rest[4:]
    wh, wl = split(term[...])
    along = ((1,), (1,))
    total = dot(th[...], wh, along) + dot(th[...], wl, along) + dot(tl[...], wh, along)
    slot = lax.broadcasted_iota(jnp.int32, (NZ, 256), 0)
    spec[...] = total * jnp.where(slot < 2, 1.0 / NZ, 2.0 / NZ)
    for j in range(4):
        outs[j][...] = spec[chip_modes(j), :]


def side_kernel(mine, other, th, tl, *rest):
    outs = rest[:4]
    value, spec = rest[4:]
    chip = lax.axis_index("span") >> 1
    m = [mine[f * 7 : f * 7 + 7, :] for f in range(11)]
    r = [other[f * 7 : f * 7 + 7, :] for f in range(11)]
    value[...] = jnp.zeros((32, NZ), F32)
    for c in range(3):
        gx = (m[c] + r[c]) * 0.5
        gy = (m[3 + c] + r[3 + c]) * 0.5
        value[c * 8 : c * 8 + 7, :] = (
            (m[6] * gx + m[7] * gy + m[8 + c]) + (r[6] * gx + r[7] * gy + r[8 + c])
        ) * 0.5
    vh, vl = split(value[...])
    along = ((1,), (1,))
    total = dot(vh, th[...], along) + dot(vl, th[...], along) + dot(vh, tl[...], along)
    slot = lax.broadcasted_iota(jnp.int32, (32, NZ), 1)
    total = total * jnp.where(slot < 2, 1.0 / NZ, 2.0 / NZ)
    for z in range(4):
        spec[z] = total[:, z * 128 : z * 128 + 128]
    for j in range(4):
        outs[j][...] = spec[chip ^ j]


def merge_kernel(bound, *rest):
    blocks, sides = rest[:4], rest[4:8]
    where, put, keep, cross, both = rest[8:]
    me, part = lax.axis_index("span"), lax.axis_index("dom")
    core = me & 1
    mine = pl.ds(pl.multiple_of(core * MODES, MODES), MODES)
    others = pl.ds(pl.multiple_of((1 - core) * MODES, MODES), MODES)
    across = ((0,), (0,))
    for j in range(4):
        edge = bound[1, row_of(me ^ (2 * j), part)]
        sh, sl = split(sides[j][...])
        place = put[edge]
        both[...] = (
            blocks[j][...] * (1.0 - 2.0 * where[pl.ds(edge, 1), :])
            + dot(sh, place, across)
            + dot(sl, place, across)
        )
        keep[j] = both[mine, :]
        cross[j] = both[others, :]


def settle_kernel(bound, pair, keep_blocks, cross_blocks, take, give, where, out, *rest):
    packed, edges, far, count, own, other, other_edge = rest
    me, part = lax.axis_index("span"), lax.axis_index("dom")
    list_pairs(pair, count, own, other, other_edge)
    for j in range(4):
        packed[bound[0, row_of(me ^ (2 * j), part)]] = keep_blocks[j]
        packed[bound[0, row_of(me ^ (2 * j + 1), part)]] = cross_blocks[j]
    ph, pw = split(packed[...].reshape(ELEMS * MODES, 256))
    edges[...] = (dot(ph, take[...]) + dot(pw, take[...])).reshape(ELEMS, MODES, 128)
    lane = lax.broadcasted_iota(jnp.int32, (MODES, 128), 1)
    for e in range(ELEMS):
        total = jnp.zeros((MODES, 128), F32)
        for t in range(3):
            edge = own[e * 4 + t]
            shift = (21 * (edge - other_edge[e * 4 + t]) + 128) & 127
            turned = pltpu.roll(edges[other[e * 4 + t]], shift, 1)
            low = edge * 21
            total = jnp.where((lane >= low) & (lane < low + 21) & (edge >= 0), turned, total)
        far[e] = total
    fh, fl = split(far[...].reshape(ELEMS * MODES, 128))
    given = dot(fh, give[...]) + dot(fl, give[...])
    for e in range(ELEMS):
        keep = jnp.ones((1, 256), F32)
        for t in range(3):
            edge = own[e * 4 + t]
            row = where[pl.ds(jnp.maximum(edge, 0), 1), :]
            keep = keep - jnp.where(edge >= 0, row, 0.0)
        done = packed[e] * keep + given[e * MODES : (e + 1) * MODES]
        for c in range(3):
            out[c, :, e * 81 : e * 81 + 81] = done[:, c * 81 : c * 81 + 81]


def spec_of(space):
    return pl.BlockSpec(memory_space=space)


def call(kernel, name, scalars, arrays, outs, scratch=(), weight=1000):
    shapes = [jax.ShapeDtypeStruct(shape, F32) for shape in outs]
    return pl.pallas_call(
        kernel,
        out_shape=shapes,
        in_specs=[spec_of(pltpu.SMEM)] * len(scalars)
        + [spec_of(pltpu.VMEM)] * len(arrays),
        out_specs=[spec_of(pltpu.VMEM)] * len(outs),
        scratch_shapes=list(scratch),
        compiler_params=pltpu.CompilerParams(vmem_limit_bytes=LIMIT),
        cost_estimate=pl.CostEstimate(flops=weight, bytes_accessed=weight, transcendentals=0),
        name=name,
    )(*scalars, *arrays)


def pair_scratch():
    return [pltpu.SMEM((n,), jnp.int32) for n in (ELEMS, ELEMS * 4, ELEMS * 4, ELEMS * 4)]


def between_chips(blocks):
    far = {
        j: lax.ppermute(blocks[j], "span", [(s, s ^ (2 * j)) for s in range(SPAN)])
        for j in (1, 2, 3)
    }
    return [blocks[0], far[1], far[2], far[3]]


def between_cores(block):
    return lax.ppermute(block, "span", [(s, s ^ 1) for s in range(SPAN)])


def side_swap(block, parts):
    def device(part, row, side):
        return ((row ^ (3 * (part & 1))) * 2 + side) * parts + part

    perm = []
    for part in range(parts):
        before = (part - 1) % parts
        for row in range(ROWS):
            perm.append((device(part, row, 0), device(before, row, 1)))
            perm.append((device(before, row, 1), device(part, row, 0)))
    return lax.ppermute(block, ("span", "dom"), perm)


def on_device(velocity_modes, metric, pair_table, bound_table):
    value, slope = span_tables()
    th, tl = halves(value)
    dh, dl = halves(slope)
    gh, gl = halves(gradient_table())
    edge_table, pick = edge_tables()
    take, give, where, put = settle_tables()
    chip, edge_chip = (2 * MODES, 256), (2 * MODES, 128)
    pair_table, bound_table = pair_table.T, bound_table.T
    flags = [pltpu.SMEM((ELEMS,), jnp.int32)]

    there = between_cores(velocity_modes)
    scale, columns, ready = call(
        metric_kernel,
        "metric",
        [bound_table, pair_table],
        [metric, pick],
        [(64, 1, 128), (128, 128), (8, 128)],
        [pltpu.VMEM((16, 256), F32), pltpu.VMEM((16, 1, 256), F32), pltpu.VMEM((128, 128), F32)],
        weight=8_000_000,
    )
    there, ready = lax.optimization_barrier((there, ready))
    packed, *blocks = call(
        pack_kernel,
        "pack",
        [bound_table],
        [velocity_modes, there, ready],
        [(ELEMS, 2 * MODES, 256)] + [chip] * 4,
        flags,
        weight=8_000_000,
    )
    blocks = between_chips(blocks)
    blocks[1], packed = lax.optimization_barrier((blocks[1], packed))
    edge_blocks = call(
        edge_kernel,
        "edges",
        [bound_table, pair_table],
        [packed, velocity_modes, there, scale, edge_table],
        [edge_chip] * 4,
        [pltpu.VMEM((ELEMS, 2 * MODES, 256), F32)] + flags + pair_scratch(),
        weight=8_000_000,
    )
    edge_blocks = between_chips(edge_blocks)
    blocks, edge_blocks[1] = lax.optimization_barrier((blocks, edge_blocks[1]))
    send, mine, u, q, g = call(
        element_kernel,
        "element",
        [bound_table],
        [*blocks, columns, th, tl, dh, dl, gh, gl],
        [(80, NZ), (80, NZ), (3, 88, NZ), (3, 88, NZ), (6, 88, NZ)],
        [pltpu.VMEM((NZ, 256), F32), pltpu.VMEM((264, NZ), F32), pltpu.VMEM((264, NZ), F32)],
    )
    other = side_swap(send, lax.axis_size("dom"))
    (term,) = call(
        term_kernel,
        "term",
        [bound_table, pair_table],
        [*edge_blocks, th, tl, u, q, g],
        [(256, NZ)],
        [pltpu.VMEM((NZ, 128), F32)] + pair_scratch(),
    )
    blocks = call(
        spectra_kernel, "spectra", [], [term, th, tl], [chip] * 4, [pltpu.VMEM((NZ, 256), F32)]
    )
    blocks = between_chips(blocks)
    sides = call(
        side_kernel,
        "side",
        [],
        [mine, other, th, tl],
        [(32, 128)] * 4,
        [pltpu.VMEM((32, NZ), F32), pltpu.VMEM((4, 32, 128), F32)],
    )
    sides = between_chips(sides)
    where = where.astype(np.float32)
    keep, cross = call(
        merge_kernel,
        "merge",
        [bound_table],
        [*blocks, *sides, where, halves(put)[0]],
        [(4, MODES, 256)] * 2,
        [pltpu.VMEM((2 * MODES, 256), F32)],
    )
    (out,) = call(
        settle_kernel,
        "settle",
        [bound_table, pair_table],
        [keep, between_cores(cross), halves(take)[0], halves(give)[0], where],
        [(3, MODES, ELEMS * PTS)],
        [
            pltpu.VMEM((ELEMS, MODES, 256), F32),
            pltpu.VMEM((ELEMS, MODES, 128), F32),
            pltpu.VMEM((ELEMS, MODES, 128), F32),
        ]
        + pair_scratch(),
    )
    return out


def solution(mesh):
    return jax.shard_map(
        on_device,
        mesh=mesh,
        in_specs=(P(None, "span", "dom"), P(None, "dom"), P("dom", None), P("dom", None)),
        out_specs=P(None, "span", "dom"),
        check_vma=False,
    )
```

```python
import jax
import jax.numpy as jnp
import ml_dtypes
import numpy as np
from jax import lax
from jax.experimental import pallas as pl
from jax.experimental.pallas import tpu as pltpu
from jax.sharding import PartitionSpec as P

NZ = 512
PTS = 81
ELEMS = 8
ROWS = 4
PAIRS = 10
SPAN = 8
MODES = NZ // SPAN
SPAN_RATE = 1.0 / 32.0
BF = jnp.bfloat16
F32 = jnp.float32
LIMIT = 48 * 1024 * 1024
LONG = 200_000_000


def legendre_rows(abscissa, node_count):
    legendre = np.zeros((node_count, node_count))
    legendre[:, 0] = 1.0
    legendre[:, 1] = abscissa
    for degree in range(2, node_count):
        legendre[:, degree] = (
            (2 * degree - 1) * abscissa * legendre[:, degree - 1]
            - (degree - 1) * legendre[:, degree - 2]
        ) / degree
    return legendre


def lobatto_matrix(order):
    node_count = order + 1
    abscissa = -np.cos(np.pi * np.arange(node_count) / order)
    for _ in range(60):
        legendre = legendre_rows(abscissa, node_count)
        abscissa = abscissa - (abscissa * legendre[:, order] - legendre[:, order - 1]) / (
            node_count * legendre[:, order]
        )
    legendre = legendre_rows(abscissa, node_count)
    end_values = legendre[:, order]
    spacing = abscissa[:, None] - abscissa[None, :] + np.eye(node_count)
    matrix = end_values[:, None] / (end_values[None, :] * spacing)
    matrix = matrix * (1.0 - np.eye(node_count))
    matrix[0, 0] = -order * node_count / 4.0
    matrix[order, order] = order * node_count / 4.0
    return matrix


def edge_points():
    positions = np.arange(9)
    outline = [positions, positions * 9 + 8, 72 + (8 - positions), (8 - positions) * 9]
    return np.stack(outline)[:, 1:8]


INSIDE = 53


def point_order():
    edges = edge_points().reshape(-1)
    inside = [point for point in range(PTS) if point not in set(edges.tolist())]
    return np.concatenate([inside, edges]).astype(int)


def lane_of(c, place):
    if place >= INSIDE:
        return 128 + 31 + 28 * c + place - INSIDE
    return 53 * c + place


def halves(table):
    high = table.astype(np.float32).astype(ml_dtypes.bfloat16)
    low = (table - high.astype(np.float64)).astype(np.float32).astype(ml_dtypes.bfloat16)
    return high, low


def span_tables():
    planes = np.arange(NZ)[None, :]
    slots = np.arange(NZ)[:, None]
    waves = np.where(slots == 1, NZ // 2, slots // 2)
    angles = (planes * waves % NZ) * (2.0 * np.pi / NZ)
    sine = (slots % 2 == 1) & (slots > 1)
    value = np.where(sine, np.sin(angles), np.cos(angles))
    rate = np.where(slots == 1, 0, waves) * SPAN_RATE
    slope = rate * np.where(sine, np.cos(angles), -np.sin(angles))
    return value, slope


def point_matrices():
    lobatto = lobatto_matrix(8)
    return np.kron(np.eye(9), lobatto), np.kron(lobatto, np.eye(9))


def gradient_table():
    along_xi, along_eta = point_matrices()
    order = point_order()
    table = np.zeros((176, 96))
    table[:81, :81] = along_xi[np.ix_(order, order)]
    table[88:169, :81] = along_eta[np.ix_(order, order)]
    return table


def order_table():
    order = point_order()
    table = np.zeros((288, 256))
    for c in range(3):
        for place in range(PTS):
            table[c * 96 + place, c * 81 + order[place]] = 1.0
    return table


def edge_tables():
    edges = edge_points()
    mats = point_matrices()
    table = np.zeros((256, 1024))
    pick = np.zeros((256, 512))
    for s in range(4):
        for t in range(3):
            for c in range(3):
                for xy in range(2):
                    for i in range(7):
                        lane = s * 128 + t * 42 + c * 14 + xy * 7 + i
                        for h in range(2):
                            table[c * 81 : c * 81 + 81, h * 512 + lane] = mats[h][edges[s, i]]
                        pick[xy * 128 + edges[s, i], lane] = 1.0
    high, low = halves(table)
    pick = halves(pick)[0]
    lanes = [slice(s * 128, s * 128 + 128) for s in range(4)]
    later = [slice(512 + s * 128, 640 + s * 128) for s in range(4)]
    return np.stack(
        [
            np.concatenate([high[:, n], high[:, m], low[:, n], low[:, m]], axis=1)
            for n, m in zip(lanes, later)
        ]
    ), pick


def settle_tables():
    order = point_order()
    take = np.zeros((128, 128))
    give = np.zeros((128, 384))
    where = np.zeros((8, 128))
    back = np.zeros((256, 384))
    for c in range(3):
        for place in range(PTS):
            back[lane_of(c, place), c * 128 + order[place]] = 1.0
        for s in range(4):
            for i in range(7):
                lane = s * 21 + c * 7 + i
                place = INSIDE + s * 7 + i
                take[lane_of(c, INSIDE + s * 7 + 6 - i) - 128, lane] = 1.0
                give[lane, c * 128 + order[place]] = 0.5
                where[s, lane_of(c, place) - 128] = 0.5
    return take, give, where, back


def row_of(place, part):
    return (place & 1) * ROWS + ((place >> 1) ^ (3 * (part & 1)))


def split(x):
    high = x.astype(BF)
    return high, (x - high.astype(F32)).astype(BF)


def dot(a, b, dims=((1,), (0,))):
    return lax.dot_general(a, b, (dims, ((), ())), preferred_element_type=F32)


def list_pairs(pair, count, own, other, other_edge):
    for e in range(ELEMS):
        count[e] = 0
    for n in range(ELEMS * 4):
        own[n] = -1
        other[n] = 0
        other_edge[n] = 0
    for row in range(PAIRS):
        for first, second in ((0, 2), (2, 0)):
            e = pair[first, row]
            slot = e * 4 + count[e]
            own[slot] = pair[first + 1, row]
            other[slot] = pair[second, row]
            other_edge[slot] = pair[second + 1, row]
            count[e] = count[e] + 1


def chip_modes(j):
    chip = (lax.axis_index("span") >> 1) ^ j
    return pl.ds(pl.multiple_of(chip * 2 * MODES, 2 * MODES), 2 * MODES)


def ready_kernel(bound, here, out):
    out[...] = here[0, 0:8, 0:128] + jnp.full((8, 128), bound[0, 0], jnp.int32).astype(F32)


def pack_element(packed, e, core, here, there):
    for at, v in ((core, here), (1 - core, there)):
        rows = pl.ds(pl.multiple_of(at * MODES, MODES), MODES)
        for c in range(3):
            packed[e, rows, c * 81 : c * 81 + 81] = v[c, :, e * 81 : e * 81 + 81]
        packed[e, rows, 243:256] = jnp.zeros((MODES, 13), F32)


def column_flags(bound, core, flags):
    for e in range(ELEMS):
        flags[e] = 0
    for row in range(ROWS):
        flags[bound[0, core * ROWS + row]] = 1


def pack_kernel(bound, here, there, ready, packed, *rest):
    outs, flags = rest[:4], rest[4]
    me, part = lax.axis_index("span"), lax.axis_index("dom")
    core = me & 1
    column_flags(bound, core, flags)
    for e in range(ELEMS):
        pl.when(flags[e] == 1)(lambda e=e: pack_element(packed, e, core, here, there))
    for j in range(4):
        outs[j][...] = packed[bound[0, row_of(me ^ (2 * j), part)]]


def edge_kernel(bound, pair, done, here, there, metric, pick, table, turn, columns, *rest):
    outs = rest[:4]
    packed, rows, lines, scale, square, flags, count, own, other, other_edge = rest[4:]
    me, part = lax.axis_index("span"), lax.axis_index("dom")
    core = me & 1
    column_flags(bound, core, flags)
    list_pairs(pair, count, own, other, other_edge)

    def copy_element(e):
        packed[e] = done[e]

    for e in range(ELEMS):
        pl.when(flags[e] == 1)(lambda e=e: copy_element(e))
        pl.when(flags[e] == 0)(lambda e=e: pack_element(packed, e, core, here, there))
    rows[...] = jnp.zeros((16, 256), F32)
    for e in range(ELEMS):
        for j in range(4):
            at = e + 8 * (j // 2)
            lane = 128 * (j % 2)
            rows[at : at + 1, lane : lane + 81] = metric[j : j + 1, e * 81 : e * 81 + 81]
    rows_high, rows_low = split(rows[...])
    for s in range(4):
        here_lanes = pick[:, s * 128 : s * 128 + 128]
        size = dot(rows_high, here_lanes) + dot(rows_low, here_lanes)
        for n in range(16):
            scale[n * 4 + s] = size[n : n + 1, :]
    for n in range(16):
        lines[n] = rows[n : n + 1, :]
    square[...] = jnp.zeros((128, 128), F32)
    mine = bound[0, row_of(me, part)]
    for j in range(4):
        line = lines[mine + 8 * (j // 2)]
        square[j : j + 1, :] = line[:, 128 * (j % 2) : 128 * (j % 2) + 128]
    high, low = split(square[...].T)
    columns[...] = dot(turn[0:96, 0:128], high) + dot(turn[0:96, 0:128], low)
    lane = lax.broadcasted_iota(jnp.int32, (2 * MODES, 128), 1)
    for j in range(4):
        e = bound[0, row_of(me ^ (2 * j), part)]
        total = jnp.zeros((2 * MODES, 128), F32)
        for t in range(3):
            far, edge = other[e * 4 + t], other_edge[e * 4 + t]
            vh, vl = split(packed[far])
            high = table[edge, :, 0:256]
            value = dot(vh, high) + dot(vl, high) + dot(vh, table[edge, :, 256:512])
            value = (
                value[:, :128] * scale[far * 4 + edge]
                + value[:, 128:] * scale[(8 + far) * 4 + edge]
            )
            total = jnp.where((lane >= t * 42) & (lane < t * 42 + 42), value, total)
        outs[j][...] = total


def element_kernel(bound, *rest):
    blocks = rest[:4]
    columns, turn, th, tl, dh, dl, gh, gl = rest[4:12]
    send, mine, u, q, g, modes = rest[12:]
    me, part = lax.axis_index("span"), lax.axis_index("dom")
    for j in range(4):
        modes[chip_modes(j), :] = blocks[j][...]
    vh, vl = split(modes[...].T)
    vh, vl = dot(turn[...], vh).astype(BF), dot(turn[...], vl).astype(BF)
    value = dot(vh, th[...]) + dot(vl, th[...]) + dot(vh, tl[...])
    slope = dot(vh, dh[...]) + dot(vl, dh[...]) + dot(vh, dl[...])
    uh, ul = split(value)
    third = value[192:280]
    for c in range(3):
        rows = slice(96 * c, 96 * c + 96)
        both = dot(gh[...], uh[rows]) + dot(gh[...], ul[rows]) + dot(gl[...], uh[rows])
        fx, fe = both[:88], both[88:]
        g[c] = columns[0:88, 0:1] * fx + columns[0:88, 2:3] * fe
        g[3 + c] = columns[0:88, 1:2] * fx + columns[0:88, 3:4] * fe
        u[c] = value[96 * c : 96 * c + 88]
        q[c] = third * slope[96 * c : 96 * c + 88]
    base = INSIDE + 7 * bound[1, row_of(me, part)]
    send[77:80] = jnp.zeros((3, NZ), F32)
    mine[77:80] = jnp.zeros((3, NZ), F32)
    order = [(g, f) for f in range(6)] + [(u, 0), (u, 1)] + [(q, c) for c in range(3)]
    for f, (ref, at) in enumerate(order):
        for i in range(7):
            line = ref[at, pl.ds(base + i, 1), :]
            mine[f * 7 + i : f * 7 + i + 1, :] = line
            send[f * 7 + 6 - i : f * 7 + 7 - i, :] = line


def to_modes(term, th, tl):
    wh, wl = split(term)
    along = ((1,), (1,))
    total = dot(th[...], wh, along) + dot(th[...], wl, along) + dot(tl[...], wh, along)
    slot = lax.broadcasted_iota(jnp.int32, total.shape, 0)
    return total * jnp.where(slot < 2, 1.0 / NZ, 2.0 / NZ)


def inside_kernel(u, q, g, th, tl, *rest):
    outs = rest[:4]
    term, spec = rest[4:]
    for c, count in ((0, 53), (1, 53), (2, 22)):
        value = u[0, 0:56] * g[c, 0:56] + u[1, 0:56] * g[3 + c, 0:56] + q[c, 0:56]
        term[53 * c : 53 * c + count, :] = value[:count]
    spec[...] = to_modes(term[...], th, tl)
    for j in range(4):
        outs[j][...] = spec[chip_modes(j), :]


def edge_term_kernel(bound, pair, *rest):
    blocks = rest[:4]
    th, tl, u, q, g, term, modes, count, own, other, other_edge = rest[4:]
    me, part = lax.axis_index("span"), lax.axis_index("dom")
    list_pairs(pair, count, own, other, other_edge)
    for j in range(4):
        modes[chip_modes(j), :] = blocks[j][...]
    eh, el = split(modes[...].T)
    planes = dot(eh, th[...]) + dot(el, th[...]) + dot(eh, tl[...])
    ph, pw = split(planes)
    e = bound[0, row_of(me, part)]
    lane = lax.broadcasted_iota(jnp.int32, (32, 128), 1)
    point = lax.broadcasted_iota(jnp.int32, (32, 128), 0)
    slot = jnp.where(lane < 42, 0, jnp.where(lane < 84, 1, 2))
    starts = []
    for t in range(3):
        edge = own[e * 4 + t]
        starts.append(jnp.where(edge < 0, -1000, 7 * edge))
    base = jnp.where(slot == 0, starts[0], jnp.where(slot == 1, starts[1], starts[2]))
    place = lane - slot * 42
    takes = []
    for f in range(6):
        xy, c = f // 3, f % 3
        i = 6 - (place - (c * 14 + xy * 7))
        hit = (i >= 0) & (i <= 6) & (lane < 126) & (point == base + i)
        takes.append(jnp.where(hit, 0.5, 0.0))
    keep = 1.0 - jnp.sum(takes[0], axis=1, keepdims=True)[:28]
    take = jnp.concatenate(takes, axis=0).astype(BF)
    far = dot(take, ph) + dot(take, pw)
    for c in range(3):
        u0, u1 = u[0, 53:81], u[1, 53:81]
        term[31 + 28 * c : 59 + 28 * c, :] = (
            u0 * (g[c, 53:81] * keep + far[c * 32 : c * 32 + 28])
            + u1 * (g[3 + c, 53:81] * keep + far[(3 + c) * 32 : (3 + c) * 32 + 28])
            + q[c, 53:81]
        )
    term[0:31, :] = u[0, 22:53] * g[2, 22:53] + u[1, 22:53] * g[5, 22:53] + q[2, 22:53]
    term[115:128, :] = jnp.zeros((13, NZ), F32)


def side_kernel(bound, term, mine, other, th, tl, *rest):
    outs = rest[:4]
    work, spec = rest[4:]
    me, part = lax.axis_index("span"), lax.axis_index("dom")
    work[...] = term[...]
    m = [mine[f * 7 : f * 7 + 7, :] for f in range(11)]
    r = [other[f * 7 : f * 7 + 7, :] for f in range(11)]
    base = 31 + 7 * bound[1, row_of(me, part)]
    for c in range(3):
        gx = (m[c] + r[c]) * 0.5
        gy = (m[3 + c] + r[3 + c]) * 0.5
        value = (
            (m[6] * gx + m[7] * gy + m[8 + c]) + (r[6] * gx + r[7] * gy + r[8 + c])
        ) * 0.5
        for i in range(7):
            work[pl.ds(base + 28 * c + i, 1), :] = value[i : i + 1, :]
    spec[...] = to_modes(work[...], th, tl)
    for j in range(4):
        outs[j][...] = spec[chip_modes(j), :]


def cut_kernel(*rest):
    blocks, cross = rest[:4], rest[4]
    others = pl.ds(pl.multiple_of((1 - (lax.axis_index("span") & 1)) * MODES, MODES), MODES)
    for j in range(4):
        cross[j] = blocks[j][others, :]


def settle_kernel(bound, pair, *rest):
    inside, edge = rest[:4], rest[4:8]
    cross, edge_cross, take, give, where, back, out = rest[8:15]
    packed, edges, far, count, own, other, other_edge = rest[15:]
    me, part = lax.axis_index("span"), lax.axis_index("dom")
    list_pairs(pair, count, own, other, other_edge)
    mine = pl.ds(pl.multiple_of((me & 1) * MODES, MODES), MODES)
    for j in range(4):
        e = bound[0, row_of(me ^ (2 * j), part)]
        packed[e, :, 0:128] = inside[j][mine, :]
        packed[e, :, 128:256] = edge[j][mine, :]
        e = bound[0, row_of(me ^ (2 * j + 1), part)]
        packed[e, :, 0:128] = cross[j]
        packed[e, :, 128:256] = edge_cross[j]
    ph, pw = split(packed[:, :, 128:256].reshape(ELEMS * MODES, 128))
    edges[...] = (dot(ph, take[...]) + dot(pw, take[...])).reshape(ELEMS, MODES, 128)
    lane = lax.broadcasted_iota(jnp.int32, (MODES, 128), 1)
    for e in range(ELEMS):
        total = jnp.zeros((MODES, 128), F32)
        keep = jnp.ones((1, 128), F32)
        for t in range(3):
            edge = own[e * 4 + t]
            shift = (21 * (edge - other_edge[e * 4 + t]) + 128) & 127
            turned = pltpu.roll(edges[other[e * 4 + t]], shift, 1)
            low = edge * 21
            total = jnp.where((lane >= low) & (lane < low + 21) & (edge >= 0), turned, total)
            row = where[pl.ds(jnp.maximum(edge, 0), 1), :]
            keep = keep - jnp.where(edge >= 0, row, 0.0)
        far[e] = total
        packed[e, :, 128:256] = packed[e, :, 128:256] * keep
    fh, fl = split(far[...].reshape(ELEMS * MODES, 128))
    ph, pw = split(packed[...].reshape(ELEMS * MODES, 256))
    done = (
        dot(ph, back[...]) + dot(pw, back[...]) + dot(fh, give[...]) + dot(fl, give[...])
    )
    for e in range(ELEMS):
        for c in range(3):
            out[c, :, e * 81 : e * 81 + 81] = done[e * MODES : (e + 1) * MODES, c * 128 : c * 128 + 81]


def spec_of(space):
    return pl.BlockSpec(memory_space=space)


def call(kernel, name, scalars, arrays, outs, scratch=(), weight=1000):
    shapes = [jax.ShapeDtypeStruct(shape, F32) for shape in outs]
    return pl.pallas_call(
        kernel,
        out_shape=shapes,
        in_specs=[spec_of(pltpu.SMEM)] * len(scalars)
        + [spec_of(pltpu.VMEM)] * len(arrays),
        out_specs=[spec_of(pltpu.VMEM)] * len(outs),
        scratch_shapes=list(scratch),
        compiler_params=pltpu.CompilerParams(vmem_limit_bytes=LIMIT),
        cost_estimate=pl.CostEstimate(flops=weight, bytes_accessed=weight, transcendentals=0),
        name=name,
    )(*scalars, *arrays)


def pair_scratch():
    return [pltpu.SMEM((n,), jnp.int32) for n in (ELEMS, ELEMS * 4, ELEMS * 4, ELEMS * 4)]


def between_chips(blocks, order=(3, 2, 1)):
    far = {
        j: lax.ppermute(blocks[j], "span", [(s, s ^ (2 * j)) for s in range(SPAN)])
        for j in order
    }
    return [blocks[0], far[1], far[2], far[3]]


def between_cores(block):
    return lax.ppermute(block, "span", [(s, s ^ 1) for s in range(SPAN)])


def side_swap(block, parts):
    def device(part, row, side):
        return ((row ^ (3 * (part & 1))) * 2 + side) * parts + part

    perm = []
    for part in range(parts):
        before = (part - 1) % parts
        for row in range(ROWS):
            perm.append((device(part, row, 0), device(before, row, 1)))
            perm.append((device(before, row, 1), device(part, row, 0)))
    return lax.ppermute(block, ("span", "dom"), perm)


def on_device(velocity_modes, metric, pair_table, bound_table):
    value, slope = span_tables()
    th, tl = halves(value)
    dh, dl = halves(slope)
    gh, gl = halves(gradient_table())
    edge_table, pick = edge_tables()
    take, give, where, back = settle_tables()
    turn = halves(order_table())[0]
    chip, edge_chip = (2 * MODES, 256), (2 * MODES, 128)
    pair_table, bound_table = pair_table.T, bound_table.T
    flags = [pltpu.SMEM((ELEMS,), jnp.int32)]

    there = between_cores(velocity_modes)
    (ready,) = call(
        ready_kernel, "ready", [bound_table], [velocity_modes], [(8, 128)], weight=LONG
    )
    there, ready = lax.optimization_barrier((there, ready))
    packed, *blocks = call(
        pack_kernel,
        "pack",
        [bound_table],
        [velocity_modes, there, ready],
        [(ELEMS, 2 * MODES, 256)] + [chip] * 4,
        flags,
        weight=LONG,
    )
    blocks = between_chips(blocks)
    blocks[3], packed = lax.optimization_barrier((blocks[3], packed))
    columns, *edge_blocks = call(
        edge_kernel,
        "edges",
        [bound_table, pair_table],
        [packed, velocity_modes, there, metric, pick, edge_table, turn],
        [(96, 128)] + [edge_chip] * 4,
        [
            pltpu.VMEM((ELEMS, 2 * MODES, 256), F32),
            pltpu.VMEM((16, 256), F32),
            pltpu.VMEM((16, 1, 256), F32),
            pltpu.VMEM((64, 1, 128), F32),
            pltpu.VMEM((128, 128), F32),
        ]
        + flags
        + pair_scratch(),
        weight=LONG,
    )
    edge_blocks = between_chips(edge_blocks)
    send, mine, u, q, g = call(
        element_kernel,
        "element",
        [bound_table],
        [*blocks, columns, turn, th, tl, dh, dl, gh, gl],
        [(80, NZ), (80, NZ), (3, 88, NZ), (3, 88, NZ), (6, 88, NZ)],
        [pltpu.VMEM((NZ, 256), F32)],
    )
    send, edge_blocks[1:3] = lax.optimization_barrier((send, edge_blocks[1:3]))
    other = side_swap(send, lax.axis_size("dom"))
    modes_scratch = pltpu.VMEM((NZ, 128), F32)
    term_scratch = pltpu.VMEM((128, NZ), F32)
    inside = call(
        inside_kernel, "inside", [], [u, q, g, th, tl], [edge_chip] * 4, [term_scratch, modes_scratch]
    )
    inside = between_chips(inside)
    (term,) = call(
        edge_term_kernel,
        "term",
        [bound_table, pair_table],
        [*edge_blocks, th, tl, u, q, g],
        [(128, NZ)],
        [modes_scratch] + pair_scratch(),
    )
    edge = call(
        side_kernel,
        "side",
        [bound_table],
        [term, mine, other, th, tl],
        [edge_chip] * 4,
        [term_scratch, modes_scratch],
    )
    edge = between_chips(edge)
    (cross,) = call(cut_kernel, "cut", [], inside, [(4, MODES, 128)])
    (edge_cross,) = call(cut_kernel, "cut_edge", [], edge, [(4, MODES, 128)])
    (out,) = call(
        settle_kernel,
        "settle",
        [bound_table, pair_table],
        [
            *inside,
            *edge,
            between_cores(cross),
            between_cores(edge_cross),
            *(halves(table)[0] for table in (take, give)),
            where.astype(np.float32),
            halves(back)[0],
        ],
        [(3, MODES, ELEMS * PTS)],
        [
            pltpu.VMEM((ELEMS, MODES, 256), F32),
            pltpu.VMEM((ELEMS, MODES, 128), F32),
            pltpu.VMEM((ELEMS, MODES, 128), F32),
        ]
        + pair_scratch(),
    )
    return out


def solution(mesh):
    return jax.shard_map(
        on_device,
        mesh=mesh,
        in_specs=(P(None, "span", "dom"), P(None, "dom"), P("dom", None), P("dom", None)),
        out_specs=P(None, "span", "dom"),
        check_vma=False,
    )
```

```python
import jax
import jax.numpy as jnp
import ml_dtypes
import numpy as np
from jax import lax
from jax.experimental import pallas as pl
from jax.experimental.pallas import tpu as pltpu
from jax.sharding import PartitionSpec as P

NZ = 512
PTS = 81
ELEMS = 8
ROWS = 4
PAIRS = 10
SPAN = 8
MODES = NZ // SPAN
SPAN_RATE = 1.0 / 32.0
BF = jnp.bfloat16
F32 = jnp.float32
LIMIT = 48 * 1024 * 1024
LONG = 200_000_000


def legendre_rows(abscissa, node_count):
    legendre = np.zeros((node_count, node_count))
    legendre[:, 0] = 1.0
    legendre[:, 1] = abscissa
    for degree in range(2, node_count):
        legendre[:, degree] = (
            (2 * degree - 1) * abscissa * legendre[:, degree - 1]
            - (degree - 1) * legendre[:, degree - 2]
        ) / degree
    return legendre


def lobatto_matrix(order):
    node_count = order + 1
    abscissa = -np.cos(np.pi * np.arange(node_count) / order)
    for _ in range(60):
        legendre = legendre_rows(abscissa, node_count)
        abscissa = abscissa - (abscissa * legendre[:, order] - legendre[:, order - 1]) / (
            node_count * legendre[:, order]
        )
    legendre = legendre_rows(abscissa, node_count)
    end_values = legendre[:, order]
    spacing = abscissa[:, None] - abscissa[None, :] + np.eye(node_count)
    matrix = end_values[:, None] / (end_values[None, :] * spacing)
    matrix = matrix * (1.0 - np.eye(node_count))
    matrix[0, 0] = -order * node_count / 4.0
    matrix[order, order] = order * node_count / 4.0
    return matrix


def edge_points():
    positions = np.arange(9)
    outline = [positions, positions * 9 + 8, 72 + (8 - positions), (8 - positions) * 9]
    return np.stack(outline)[:, 1:8]


INSIDE = 53


def point_order():
    edges = edge_points().reshape(-1)
    inside = [point for point in range(PTS) if point not in set(edges.tolist())]
    return np.concatenate([inside, edges]).astype(int)


def lane_of(c, place):
    if place >= INSIDE:
        return 128 + 31 + 28 * c + place - INSIDE
    return 53 * c + place


def halves(table):
    high = table.astype(np.float32).astype(ml_dtypes.bfloat16)
    low = (table - high.astype(np.float64)).astype(np.float32).astype(ml_dtypes.bfloat16)
    return high, low


def span_tables():
    planes = np.arange(NZ)[None, :]
    slots = np.arange(NZ)[:, None]
    waves = np.where(slots == 1, NZ // 2, slots // 2)
    angles = (planes * waves % NZ) * (2.0 * np.pi / NZ)
    sine = (slots % 2 == 1) & (slots > 1)
    value = np.where(sine, np.sin(angles), np.cos(angles))
    rate = np.where(slots == 1, 0, waves) * SPAN_RATE
    slope = rate * np.where(sine, np.cos(angles), -np.sin(angles))
    return value, slope


def point_matrices():
    lobatto = lobatto_matrix(8)
    return np.kron(np.eye(9), lobatto), np.kron(lobatto, np.eye(9))


def gradient_table():
    along_xi, along_eta = point_matrices()
    order = point_order()
    table = np.zeros((176, 96))
    table[:81, :81] = along_xi[np.ix_(order, order)]
    table[88:169, :81] = along_eta[np.ix_(order, order)]
    return table


def order_table():
    order = point_order()
    table = np.zeros((288, 256))
    for c in range(3):
        for place in range(PTS):
            table[c * 96 + place, c * 81 + order[place]] = 1.0
    return table


def rim_table():
    edges = edge_points()
    mats = point_matrices()
    table = np.zeros((4, 64, 256), ml_dtypes.bfloat16)
    for s in range(4):
        rows = np.zeros((32, 256))
        for c in range(3):
            rows[c * 8 : c * 8 + 7, c * 81 : c * 81 + 81] = mats[(s + 1) % 2][edges[s]]
        table[s, :32], table[s, 32:] = halves(rows)
    return table


def far_table():
    lobatto = lobatto_matrix(8)
    table = np.zeros((80, 64))
    for c in range(3):
        for i in range(7):
            table[c * 8 + i, c * 9 + i + 1] = 1.0
            table[24 + c * 8 + i, c * 9 : c * 9 + 9] = lobatto[i + 1]
            table[48 + c * 8 + i, 27 + c * 7 + i] = 1.0
    return table


def edge_tables():
    edges = edge_points()
    mats = point_matrices()
    table = np.zeros((256, 1024))
    pick = np.zeros((256, 512))
    for s in range(4):
        for t in range(3):
            for c in range(3):
                for xy in range(2):
                    for i in range(7):
                        lane = s * 128 + t * 42 + c * 14 + xy * 7 + i
                        for h in range(2):
                            table[c * 81 : c * 81 + 81, h * 512 + lane] = mats[h][edges[s, i]]
                        pick[xy * 128 + edges[s, i], lane] = 1.0
    high, low = halves(table)
    pick = halves(pick)[0]
    lanes = [slice(s * 128, s * 128 + 128) for s in range(4)]
    later = [slice(512 + s * 128, 640 + s * 128) for s in range(4)]
    return np.stack(
        [
            np.concatenate([high[:, n], high[:, m], low[:, n], low[:, m]], axis=1)
            for n, m in zip(lanes, later)
        ]
    ), pick


def settle_tables():
    order = point_order()
    take = np.zeros((128, 128))
    give = np.zeros((128, 384))
    where = np.zeros((8, 128))
    back = np.zeros((256, 384))
    for c in range(3):
        for place in range(PTS):
            back[lane_of(c, place), c * 128 + order[place]] = 1.0
        for s in range(4):
            for i in range(7):
                lane = s * 21 + c * 7 + i
                place = INSIDE + s * 7 + i
                take[lane_of(c, INSIDE + s * 7 + 6 - i) - 128, lane] = 1.0
                give[lane, c * 128 + order[place]] = 0.5
                where[s, lane_of(c, place) - 128] = 0.5
    return take, give, where, back


def row_of(place, part):
    return (place & 1) * ROWS + ((place >> 1) ^ (3 * (part & 1)))


def split(x):
    high = x.astype(BF)
    return high, (x - high.astype(F32)).astype(BF)


def dot(a, b, dims=((1,), (0,))):
    return lax.dot_general(a, b, (dims, ((), ())), preferred_element_type=F32)


def list_pairs(pair, count, own, other, other_edge):
    for e in range(ELEMS):
        count[e] = 0
    for n in range(ELEMS * 4):
        own[n] = -1
        other[n] = 0
        other_edge[n] = 0
    for row in range(PAIRS):
        for first, second in ((0, 2), (2, 0)):
            e = pair[first, row]
            slot = e * 4 + count[e]
            own[slot] = pair[first + 1, row]
            other[slot] = pair[second, row]
            other_edge[slot] = pair[second + 1, row]
            count[e] = count[e] + 1


def chip_modes(j):
    chip = (lax.axis_index("span") >> 1) ^ j
    return pl.ds(pl.multiple_of(chip * 2 * MODES, 2 * MODES), 2 * MODES)


def ready_kernel(bound, here, out):
    out[...] = here[0, 0:8, 0:128] + jnp.full((8, 128), bound[0, 0], jnp.int32).astype(F32)


def pack_element(packed, e, core, here, there):
    for at, v in ((core, here), (1 - core, there)):
        rows = pl.ds(pl.multiple_of(at * MODES, MODES), MODES)
        for c in range(3):
            packed[e, rows, c * 81 : c * 81 + 81] = v[c, :, e * 81 : e * 81 + 81]
        packed[e, rows, 243:256] = jnp.zeros((MODES, 13), F32)


def column_flags(bound, core, flags):
    for e in range(ELEMS):
        flags[e] = 0
    for row in range(ROWS):
        flags[bound[0, core * ROWS + row]] = 1


def pack_kernel(bound, here, there, ready, packed, *rest):
    outs, flags = rest[:4], rest[4]
    me, part = lax.axis_index("span"), lax.axis_index("dom")
    core = me & 1
    column_flags(bound, core, flags)
    for e in range(ELEMS):
        pl.when(flags[e] == 1)(lambda e=e: pack_element(packed, e, core, here, there))
    for j in range(4):
        outs[j][...] = packed[bound[0, row_of(me ^ (2 * j), part)]]


def edge_kernel(bound, pair, done, here, there, metric, pick, table, turn, columns, terms, *rest):
    outs = rest[:4]
    packed, rows, lines, scale, square, flags, count, own, other, other_edge = rest[4:]
    me, part = lax.axis_index("span"), lax.axis_index("dom")
    core = me & 1
    column_flags(bound, core, flags)
    list_pairs(pair, count, own, other, other_edge)

    def copy_element(e):
        packed[e] = done[e]

    for e in range(ELEMS):
        pl.when(flags[e] == 1)(lambda e=e: copy_element(e))
        pl.when(flags[e] == 0)(lambda e=e: pack_element(packed, e, core, here, there))
    rows[...] = jnp.zeros((16, 256), F32)
    for e in range(ELEMS):
        for j in range(4):
            at = e + 8 * (j // 2)
            lane = 128 * (j % 2)
            rows[at : at + 1, lane : lane + 81] = metric[j : j + 1, e * 81 : e * 81 + 81]
    rows_high, rows_low = split(rows[...])
    for s in range(4):
        here_lanes = pick[:, s * 128 : s * 128 + 128]
        size = dot(rows_high, here_lanes) + dot(rows_low, here_lanes)
        for n in range(16):
            scale[n * 4 + s] = size[n : n + 1, :]
    for n in range(16):
        lines[n] = rows[n : n + 1, :]
    square[...] = jnp.zeros((128, 128), F32)
    mine = bound[0, row_of(me, part)]
    for j in range(4):
        line = lines[mine + 8 * (j // 2)]
        square[j : j + 1, :] = line[:, 128 * (j % 2) : 128 * (j % 2) + 128]
    high, low = split(square[...].T)
    columns[...] = dot(turn[0:96, 0:128], high) + dot(turn[0:96, 0:128], low)
    side = bound[1, row_of(me, part)]
    along, across = scale[mine * 4 + side], scale[(8 + mine) * 4 + side]
    even = (side & 1) == 0
    terms[...] = jnp.zeros((8, 128), F32)
    terms[0:1, :] = jnp.where(side < 2, 1.0, -1.0) * jnp.where(even, along, across)
    terms[1:2, :] = jnp.where(even, across, along)
    lane = lax.broadcasted_iota(jnp.int32, (2 * MODES, 128), 1)
    for j in range(4):
        e = bound[0, row_of(me ^ (2 * j), part)]
        total = jnp.zeros((2 * MODES, 128), F32)
        for t in range(3):
            far, edge = other[e * 4 + t], other_edge[e * 4 + t]
            vh, vl = split(packed[far])
            high = table[edge, :, 0:256]
            value = dot(vh, high) + dot(vl, high) + dot(vh, table[edge, :, 256:512])
            value = (
                value[:, :128] * scale[far * 4 + edge]
                + value[:, 128:] * scale[(8 + far) * 4 + edge]
            )
            total = jnp.where((lane >= t * 42) & (lane < t * 42 + 42), value, total)
        outs[j][...] = total


def rim_kernel(bound, *rest):
    blocks = rest[:4]
    terms, table, send, high, low, modes, points = rest[4:]
    me, part = lax.axis_index("span"), lax.axis_index("dom")
    for j in range(4):
        modes[chip_modes(j), :] = blocks[j][...]
    points[...] = modes[...].T
    vh, vl = split(points[...])
    high[...] = vh
    low[...] = vl
    side = bound[1, row_of(me, part)]
    rows = dot(table[side], vh)
    across = rows[:32] + rows[32:] + dot(table[side, 0:32], vl)
    base = jnp.where(side == 0, 0, jnp.where(side == 1, 8, jnp.where(side == 2, 80, 72)))
    step = jnp.where(side == 0, 1, jnp.where(side == 1, 9, jnp.where(side == 2, -1, -9)))
    for c in range(3):
        for i in range(9):
            send[c * 9 + i : c * 9 + i + 1, :] = points[pl.ds(c * 81 + base + step * i, 1), :]
        send[27 + c * 7 : 34 + c * 7, :] = across[c * 8 : c * 8 + 7]
    send[48:56, :] = jnp.zeros((8, NZ), F32)
    send[48:56, 0:128] = terms[...]


def element_kernel(bound, high, low, columns, turn, th, tl, dh, dl, gh, gl, mine, u, q, g):
    me, part = lax.axis_index("span"), lax.axis_index("dom")
    vh, vl = dot(turn[...], high[...]).astype(BF), dot(turn[...], low[...]).astype(BF)
    value = dot(vh, th[...]) + dot(vl, th[...]) + dot(vh, tl[...])
    slope = dot(vh, dh[...]) + dot(vl, dh[...]) + dot(vh, dl[...])
    uh, ul = split(value)
    third = value[192:280]
    for c in range(3):
        rows = slice(96 * c, 96 * c + 96)
        both = dot(gh[...], uh[rows]) + dot(gh[...], ul[rows]) + dot(gl[...], uh[rows])
        fx, fe = both[:88], both[88:]
        g[c] = columns[0:88, 0:1] * fx + columns[0:88, 2:3] * fe
        g[3 + c] = columns[0:88, 1:2] * fx + columns[0:88, 3:4] * fe
        u[c] = value[96 * c : 96 * c + 88]
        q[c] = third * slope[96 * c : 96 * c + 88]
    base = INSIDE + 7 * bound[1, row_of(me, part)]
    mine[...] = jnp.zeros((88, NZ), F32)
    order = [(g, f) for f in range(6)] + [(u, 0), (u, 1)] + [(q, c) for c in range(3)]
    for f, (ref, at) in enumerate(order):
        for i in range(7):
            mine[f * 8 + 6 - i : f * 8 + 7 - i, :] = ref[at, pl.ds(base + i, 1), :]


def to_modes(term, th, tl):
    wh, wl = split(term)
    along = ((1,), (1,))
    total = dot(th[...], wh, along) + dot(th[...], wl, along) + dot(tl[...], wh, along)
    slot = lax.broadcasted_iota(jnp.int32, total.shape, 0)
    return total * jnp.where(slot < 2, 1.0 / NZ, 2.0 / NZ)


def inside_kernel(u, q, g, th, tl, *rest):
    outs = rest[:4]
    term, spec = rest[4:]
    for c, count in ((0, 53), (1, 53), (2, 22)):
        value = u[0, 0:56] * g[c, 0:56] + u[1, 0:56] * g[3 + c, 0:56] + q[c, 0:56]
        term[53 * c : 53 * c + count, :] = value[:count]
    spec[...] = to_modes(term[...], th, tl)
    for j in range(4):
        outs[j][...] = spec[chip_modes(j), :]


def edge_term_kernel(bound, pair, *rest):
    blocks = rest[:4]
    th, tl, u, q, g, term, modes, count, own, other, other_edge = rest[4:]
    me, part = lax.axis_index("span"), lax.axis_index("dom")
    list_pairs(pair, count, own, other, other_edge)
    for j in range(4):
        modes[chip_modes(j), :] = blocks[j][...]
    eh, el = split(modes[...].T)
    planes = dot(eh, th[...]) + dot(el, th[...]) + dot(eh, tl[...])
    ph, pw = split(planes)
    e = bound[0, row_of(me, part)]
    lane = lax.broadcasted_iota(jnp.int32, (32, 128), 1)
    point = lax.broadcasted_iota(jnp.int32, (32, 128), 0)
    slot = jnp.where(lane < 42, 0, jnp.where(lane < 84, 1, 2))
    starts = []
    for t in range(3):
        edge = own[e * 4 + t]
        starts.append(jnp.where(edge < 0, -1000, 7 * edge))
    base = jnp.where(slot == 0, starts[0], jnp.where(slot == 1, starts[1], starts[2]))
    place = lane - slot * 42
    takes = []
    for f in range(6):
        xy, c = f // 3, f % 3
        i = 6 - (place - (c * 14 + xy * 7))
        hit = (i >= 0) & (i <= 6) & (lane < 126) & (point == base + i)
        takes.append(jnp.where(hit, 0.5, 0.0))
    keep = 1.0 - jnp.sum(takes[0], axis=1, keepdims=True)[:28]
    take = jnp.concatenate(takes, axis=0).astype(BF)
    far = dot(take, ph) + dot(take, pw)
    for c in range(3):
        u0, u1 = u[0, 53:81], u[1, 53:81]
        term[31 + 28 * c : 59 + 28 * c, :] = (
            u0 * (g[c, 53:81] * keep + far[c * 32 : c * 32 + 28])
            + u1 * (g[3 + c, 53:81] * keep + far[(3 + c) * 32 : (3 + c) * 32 + 28])
            + q[c, 53:81]
        )
    term[0:31, :] = u[0, 22:53] * g[2, 22:53] + u[1, 22:53] * g[5, 22:53] + q[2, 22:53]
    term[115:128, :] = jnp.zeros((13, NZ), F32)


def whole_kernel(bound, pair, *rest):
    blocks = rest[:4]
    high, low, columns, turn, th, tl, dh, dl, gh, gl = rest[4:14]
    outs, term, mine = rest[14:18], rest[18], rest[19]
    u, q, g, inside_term, spec, modes = rest[20:26]
    pairs = rest[26:]
    element_kernel(bound, high, low, columns, turn, th, tl, dh, dl, gh, gl, mine, u, q, g)
    inside_kernel(u, q, g, th, tl, *outs, inside_term, spec)
    edge_term_kernel(bound, pair, *blocks, th, tl, u, q, g, term, modes, *pairs)


def side_kernel(bound, term, mine, other, table, th, tl, dh, dl, *rest):
    outs = rest[:4]
    work, spec, rows, square, turned = rest[4:]
    me, part = lax.axis_index("span"), lax.axis_index("dom")
    work[...] = term[...]
    rows[0:56] = other[...]
    rows[56:64] = jnp.zeros((8, NZ), F32)
    rh, rl = split(rows[...])
    xh, xl = split(dot(table[0], rh) + dot(table[0], rl) + dot(table[1], rh))
    value = dot(xh, th[...]) + dot(xl, th[...]) + dot(xh, tl[...])
    xh, xl = xh[:32], xl[:32]
    slope = dot(xh, dh[...]) + dot(xl, dh[...]) + dot(xh, dl[...])
    square[...] = jnp.zeros((128, 128), F32)
    square[0:8, :] = other[48:56, 0:128]
    turned[...] = square[...].T
    base = 31 + 7 * bound[1, row_of(me, part)]
    u0 = mine[48:56, :] + value[0:8]
    u1 = mine[56:64, :] + value[8:16]
    for c in range(3):
        along, across = value[24 + 8 * c : 32 + 8 * c], value[48 + 8 * c : 56 + 8 * c]
        gx = mine[8 * c : 8 * c + 8, :] + (turned[0:8, 0:1] * along + turned[0:8, 1:2] * across)
        gy = mine[24 + 8 * c : 32 + 8 * c, :] + (
            turned[7:15, 0:1] * along + turned[7:15, 1:2] * across
        )
        q = mine[64 + 8 * c : 72 + 8 * c, :] + value[16:24] * slope[8 * c : 8 * c + 8]
        mean = (u0 * gx + u1 * gy) * 0.25 + q * 0.5
        for i in range(7):
            work[pl.ds(base + 28 * c + 6 - i, 1), :] = mean[i : i + 1, :]
    spec[...] = to_modes(work[...], th, tl)
    for j in range(4):
        outs[j][...] = spec[chip_modes(j), :]


def cut_kernel(*rest):
    blocks, cross = rest[:4], rest[4]
    others = pl.ds(pl.multiple_of((1 - (lax.axis_index("span") & 1)) * MODES, MODES), MODES)
    for j in range(4):
        cross[j] = blocks[j][others, :]


def settle_kernel(bound, pair, *rest):
    inside, edge = rest[:4], rest[4:8]
    cross, edge_cross, take, give, where, back, out = rest[8:15]
    packed, edges, far, count, own, other, other_edge = rest[15:]
    me, part = lax.axis_index("span"), lax.axis_index("dom")
    list_pairs(pair, count, own, other, other_edge)
    mine = pl.ds(pl.multiple_of((me & 1) * MODES, MODES), MODES)
    for j in range(4):
        e = bound[0, row_of(me ^ (2 * j), part)]
        packed[e, :, 0:128] = inside[j][mine, :]
        packed[e, :, 128:256] = edge[j][mine, :]
        e = bound[0, row_of(me ^ (2 * j + 1), part)]
        packed[e, :, 0:128] = cross[j]
        packed[e, :, 128:256] = edge_cross[j]
    ph, pw = split(packed[:, :, 128:256].reshape(ELEMS * MODES, 128))
    edges[...] = (dot(ph, take[...]) + dot(pw, take[...])).reshape(ELEMS, MODES, 128)
    lane = lax.broadcasted_iota(jnp.int32, (MODES, 128), 1)
    for e in range(ELEMS):
        total = jnp.zeros((MODES, 128), F32)
        keep = jnp.ones((1, 128), F32)
        for t in range(3):
            edge = own[e * 4 + t]
            shift = (21 * (edge - other_edge[e * 4 + t]) + 128) & 127
            turned = pltpu.roll(edges[other[e * 4 + t]], shift, 1)
            low = edge * 21
            total = jnp.where((lane >= low) & (lane < low + 21) & (edge >= 0), turned, total)
            row = where[pl.ds(jnp.maximum(edge, 0), 1), :]
            keep = keep - jnp.where(edge >= 0, row, 0.0)
        far[e] = total
        packed[e, :, 128:256] = packed[e, :, 128:256] * keep
    fh, fl = split(far[...].reshape(ELEMS * MODES, 128))
    ph, pw = split(packed[...].reshape(ELEMS * MODES, 256))
    done = (
        dot(ph, back[...]) + dot(pw, back[...]) + dot(fh, give[...]) + dot(fl, give[...])
    )
    for e in range(ELEMS):
        for c in range(3):
            out[c, :, e * 81 : e * 81 + 81] = done[e * MODES : (e + 1) * MODES, c * 128 : c * 128 + 81]


def spec_of(space):
    return pl.BlockSpec(memory_space=space)


def call(kernel, name, scalars, arrays, outs, scratch=(), weight=1000):
    shapes = [
        shape if isinstance(shape, jax.ShapeDtypeStruct) else jax.ShapeDtypeStruct(shape, F32)
        for shape in outs
    ]
    return pl.pallas_call(
        kernel,
        out_shape=shapes,
        in_specs=[spec_of(pltpu.SMEM)] * len(scalars)
        + [spec_of(pltpu.VMEM)] * len(arrays),
        out_specs=[spec_of(pltpu.VMEM)] * len(outs),
        scratch_shapes=list(scratch),
        compiler_params=pltpu.CompilerParams(vmem_limit_bytes=LIMIT),
        cost_estimate=pl.CostEstimate(flops=weight, bytes_accessed=weight, transcendentals=0),
        name=name,
    )(*scalars, *arrays)


def pair_scratch():
    return [pltpu.SMEM((n,), jnp.int32) for n in (ELEMS, ELEMS * 4, ELEMS * 4, ELEMS * 4)]


def between_chips(blocks, order=(3, 2, 1)):
    far = {
        j: lax.ppermute(blocks[j], "span", [(s, s ^ (2 * j)) for s in range(SPAN)])
        for j in order
    }
    return [blocks[0], far[1], far[2], far[3]]


def between_cores(block):
    return lax.ppermute(block, "span", [(s, s ^ 1) for s in range(SPAN)])


def side_swap(block, parts):
    def device(part, row, side):
        return ((row ^ (3 * (part & 1))) * 2 + side) * parts + part

    perm = []
    for part in range(parts):
        before = (part - 1) % parts
        for row in range(ROWS):
            perm.append((device(part, row, 0), device(before, row, 1)))
            perm.append((device(before, row, 1), device(part, row, 0)))
    return lax.ppermute(block, ("span", "dom"), perm)


def on_device(velocity_modes, metric, pair_table, bound_table):
    value, slope = span_tables()
    th, tl = halves(value)
    dh, dl = halves(slope)
    gh, gl = halves(gradient_table())
    edge_table, pick = edge_tables()
    take, give, where, back = settle_tables()
    turn = halves(order_table())[0]
    chip, edge_chip = (2 * MODES, 256), (2 * MODES, 128)
    pair_table, bound_table = pair_table.T, bound_table.T
    flags = [pltpu.SMEM((ELEMS,), jnp.int32)]

    there = between_cores(velocity_modes)
    (ready,) = call(
        ready_kernel, "ready", [bound_table], [velocity_modes], [(8, 128)], weight=LONG
    )
    there, ready = lax.optimization_barrier((there, ready))
    packed, *blocks = call(
        pack_kernel,
        "pack",
        [bound_table],
        [velocity_modes, there, ready],
        [(ELEMS, 2 * MODES, 256)] + [chip] * 4,
        flags,
        weight=LONG,
    )
    blocks = between_chips(blocks)
    blocks[3], packed = lax.optimization_barrier((blocks[3], packed))
    columns, terms, *edge_blocks = call(
        edge_kernel,
        "edges",
        [bound_table, pair_table],
        [packed, velocity_modes, there, metric, pick, edge_table, turn],
        [(96, 128), (8, 128)] + [edge_chip] * 4,
        [
            pltpu.VMEM((ELEMS, 2 * MODES, 256), F32),
            pltpu.VMEM((16, 256), F32),
            pltpu.VMEM((16, 1, 256), F32),
            pltpu.VMEM((64, 1, 128), F32),
            pltpu.VMEM((128, 128), F32),
        ]
        + flags
        + pair_scratch(),
        weight=LONG,
    )
    edge_blocks = between_chips(edge_blocks)
    half = jax.ShapeDtypeStruct((256, NZ), BF)
    send, high, low = call(
        rim_kernel,
        "rim",
        [bound_table],
        [*blocks, terms, rim_table()],
        [(56, NZ), half, half],
        [pltpu.VMEM((NZ, 256), F32), pltpu.VMEM((256, NZ), F32)],
    )
    other = side_swap(send, lax.axis_size("dom"))
    modes_scratch = pltpu.VMEM((NZ, 128), F32)
    term_scratch = pltpu.VMEM((128, NZ), F32)
    *inside, term, mine = call(
        whole_kernel,
        "whole",
        [bound_table, pair_table],
        [*edge_blocks, high, low, columns, turn, th, tl, dh, dl, gh, gl],
        [edge_chip] * 4 + [(128, NZ), (88, NZ)],
        [
            pltpu.VMEM((3, 88, NZ), F32),
            pltpu.VMEM((3, 88, NZ), F32),
            pltpu.VMEM((6, 88, NZ), F32),
            term_scratch,
            modes_scratch,
            modes_scratch,
        ]
        + pair_scratch(),
    )
    inside = between_chips(inside)
    edge = call(
        side_kernel,
        "side",
        [bound_table],
        [term, mine, other, np.stack(halves(far_table())), th, tl, dh, dl],
        [edge_chip] * 4,
        [
            term_scratch,
            modes_scratch,
            pltpu.VMEM((64, NZ), F32),
            pltpu.VMEM((128, 128), F32),
            pltpu.VMEM((128, 128), F32),
        ],
    )
    edge = between_chips(edge)
    (cross,) = call(cut_kernel, "cut", [], inside, [(4, MODES, 128)])
    (edge_cross,) = call(cut_kernel, "cut_edge", [], edge, [(4, MODES, 128)])
    (out,) = call(
        settle_kernel,
        "settle",
        [bound_table, pair_table],
        [
            *inside,
            *edge,
            between_cores(cross),
            between_cores(edge_cross),
            *(halves(table)[0] for table in (take, give)),
            where.astype(np.float32),
            halves(back)[0],
        ],
        [(3, MODES, ELEMS * PTS)],
        [
            pltpu.VMEM((ELEMS, MODES, 256), F32),
            pltpu.VMEM((ELEMS, MODES, 128), F32),
            pltpu.VMEM((ELEMS, MODES, 128), F32),
        ]
        + pair_scratch(),
    )
    return out


def solution(mesh):
    return jax.shard_map(
        on_device,
        mesh=mesh,
        in_specs=(P(None, "span", "dom"), P(None, "dom"), P("dom", None), P("dom", None)),
        out_specs=P(None, "span", "dom"),
        check_vma=False,
    )
```

```python
import jax
import jax.numpy as jnp
import ml_dtypes
import numpy as np
from jax import lax
from jax.experimental import pallas as pl
from jax.experimental.pallas import tpu as pltpu
from jax.sharding import PartitionSpec as P

NZ = 512
HALF = 256
PTS = 81
ELEMS = 8
ROWS = 4
PAIRS = 10
SPAN = 8
MODES = NZ // SPAN
SPAN_RATE = 1.0 / 32.0
BF = jnp.bfloat16
F32 = jnp.float32
LIMIT = 48 * 1024 * 1024
LONG = 200_000_000


def legendre_rows(abscissa, node_count):
    legendre = np.zeros((node_count, node_count))
    legendre[:, 0] = 1.0
    legendre[:, 1] = abscissa
    for degree in range(2, node_count):
        legendre[:, degree] = (
            (2 * degree - 1) * abscissa * legendre[:, degree - 1]
            - (degree - 1) * legendre[:, degree - 2]
        ) / degree
    return legendre


def lobatto_matrix(order):
    node_count = order + 1
    abscissa = -np.cos(np.pi * np.arange(node_count) / order)
    for _ in range(60):
        legendre = legendre_rows(abscissa, node_count)
        abscissa = abscissa - (abscissa * legendre[:, order] - legendre[:, order - 1]) / (
            node_count * legendre[:, order]
        )
    legendre = legendre_rows(abscissa, node_count)
    end_values = legendre[:, order]
    spacing = abscissa[:, None] - abscissa[None, :] + np.eye(node_count)
    matrix = end_values[:, None] / (end_values[None, :] * spacing)
    matrix = matrix * (1.0 - np.eye(node_count))
    matrix[0, 0] = -order * node_count / 4.0
    matrix[order, order] = order * node_count / 4.0
    return matrix


def edge_points():
    positions = np.arange(9)
    outline = [positions, positions * 9 + 8, 72 + (8 - positions), (8 - positions) * 9]
    return np.stack(outline)[:, 1:8]


INSIDE = 53


def point_order():
    edges = edge_points().reshape(-1)
    inside = [point for point in range(PTS) if point not in set(edges.tolist())]
    return np.concatenate([inside, edges]).astype(int)


def lane_of(c, place):
    if place >= INSIDE:
        return 128 + 31 + 28 * c + place - INSIDE
    return 53 * c + place


def halves(table):
    high = table.astype(np.float32).astype(ml_dtypes.bfloat16)
    low = (table - high.astype(np.float64)).astype(np.float32).astype(ml_dtypes.bfloat16)
    return high, low


def span_tables():
    planes = np.arange(HALF)[None, :]
    waves = np.arange(HALF + 16)[:, None]
    angles = (planes * waves % NZ) * (2.0 * np.pi / NZ)
    cosines, sines = np.cos(angles), np.sin(angles)[:HALF]
    sines[0] = 1.0 - 2.0 * (np.arange(HALF) % 2)
    return cosines, sines


def point_matrices():
    lobatto = lobatto_matrix(8)
    return np.kron(np.eye(9), lobatto), np.kron(lobatto, np.eye(9))


def gradient_table():
    along_xi, along_eta = point_matrices()
    order = point_order()
    table = np.zeros((176, 96))
    table[:81, :81] = along_xi[np.ix_(order, order)]
    table[88:169, :81] = along_eta[np.ix_(order, order)]
    return table


def order_table():
    order = point_order()
    table = np.zeros((288, 256))
    for c in range(3):
        for place in range(PTS):
            table[c * 96 + place, c * 81 + order[place]] = 1.0
    return table


def rim_table():
    edges = edge_points()
    mats = point_matrices()
    table = np.zeros((4, 64, 256), ml_dtypes.bfloat16)
    for s in range(4):
        rows = np.zeros((32, 256))
        for c in range(3):
            rows[c * 8 : c * 8 + 7, c * 81 : c * 81 + 81] = mats[(s + 1) % 2][edges[s]]
        table[s, :32], table[s, 32:] = halves(rows)
    return table


def far_table():
    lobatto = lobatto_matrix(8)
    table = np.zeros((80, 64))
    for c in range(3):
        for i in range(7):
            table[c * 8 + i, c * 9 + i + 1] = 1.0
            table[24 + c * 8 + i, c * 9 : c * 9 + 9] = lobatto[i + 1]
            table[48 + c * 8 + i, 27 + c * 7 + i] = 1.0
    return table


def edge_tables():
    edges = edge_points()
    mats = point_matrices()
    table = np.zeros((256, 1024))
    pick = np.zeros((256, 512))
    for s in range(4):
        for t in range(3):
            for c in range(3):
                for xy in range(2):
                    for i in range(7):
                        lane = s * 128 + t * 42 + c * 14 + xy * 7 + i
                        for h in range(2):
                            table[c * 81 : c * 81 + 81, h * 512 + lane] = mats[h][edges[s, i]]
                        pick[xy * 128 + edges[s, i], lane] = 1.0
    high, low = halves(table)
    pick = halves(pick)[0]
    lanes = [slice(s * 128, s * 128 + 128) for s in range(4)]
    later = [slice(512 + s * 128, 640 + s * 128) for s in range(4)]
    return np.stack(
        [
            np.concatenate([high[:, n], high[:, m], low[:, n], low[:, m]], axis=1)
            for n, m in zip(lanes, later)
        ]
    ), pick


def settle_tables():
    order = point_order()
    take = np.zeros((128, 128))
    give = np.zeros((128, 384))
    where = np.zeros((8, 128))
    back = np.zeros((256, 384))
    for c in range(3):
        for place in range(PTS):
            back[lane_of(c, place), c * 128 + order[place]] = 1.0
        for s in range(4):
            for i in range(7):
                lane = s * 21 + c * 7 + i
                place = INSIDE + s * 7 + i
                take[lane_of(c, INSIDE + s * 7 + 6 - i) - 128, lane] = 1.0
                give[lane, c * 128 + order[place]] = 0.5
                where[s, lane_of(c, place) - 128] = 0.5
    return take, give, where, back


def row_of(place, part):
    return (place & 1) * ROWS + ((place >> 1) ^ (3 * (part & 1)))


def split(x):
    high = x.astype(BF)
    return high, (x - high.astype(F32)).astype(BF)


def dot(a, b, dims=((1,), (0,))):
    return lax.dot_general(a, b, (dims, ((), ())), preferred_element_type=F32)


def pick_slots(modes):
    even, odd = modes[pl.ds(0, HALF, stride=2), :], modes[pl.ds(1, HALF, stride=2), :]
    return even.T, odd.T


def to_planes(x, tables):
    ch, cl, sh, sl = tables
    high, low = split(x)
    ch, cl = ch[0:HALF], cl[0:HALF]
    sh, sl = sh[...], sl[...]
    even = dot(high[:, :HALF], ch) + dot(low[:, :HALF], ch) + dot(high[:, :HALF], cl)
    odd = dot(high[:, HALF:], sh) + dot(low[:, HALF:], sh) + dot(high[:, HALF:], sl)
    lane = lax.broadcasted_iota(jnp.int32, even.shape, 1)
    sign = jnp.where((lane & 1) == 0, 1.0, -1.0)
    lone = x[:, HALF : HALF + 1]
    middle = jnp.sum(x[:, :HALF] * sign, axis=1, keepdims=True) + lone
    mirror = jnp.where(lane == 0, middle, even - odd + (lone + lone) * sign)
    return jnp.concatenate([even + odd, mirror], axis=1)


def slope_slots(x):
    lane = lax.broadcasted_iota(jnp.int32, (x.shape[0], HALF), 1)
    rate = lane.astype(F32) * SPAN_RATE
    return jnp.concatenate([x[:, HALF:] * rate, -x[:, :HALF] * rate], axis=1)


def to_slots(term, tables, spec):
    ch, cl, sh, sl = tables
    first, mirror = term[:, :HALF], term[:, HALF:]
    lane = lax.broadcasted_iota(jnp.int32, first.shape, 1)
    eh, el = split(jnp.where(lane == 0, first, first + mirror))
    oh, ol = split(first - mirror)
    along = ((1,), (1,))
    even = dot(ch[...], eh, along) + dot(ch[...], el, along) + dot(cl[...], eh, along)
    odd = dot(sh[...], oh, along) + dot(sh[...], ol, along) + dot(sl[...], oh, along)
    row = lax.broadcasted_iota(jnp.int32, even.shape, 0)
    middle = mirror[:, 0:128].T[0:1, :]
    even = even + jnp.where((row & 1) == 0, 1.0, -1.0) * middle
    row = row[:HALF]
    lone = even[HALF : HALF + 1] * (1.0 / NZ)
    spec[pl.ds(0, HALF, stride=2), :] = even[:HALF] * jnp.where(row == 0, 1.0 / NZ, 2.0 / NZ)
    spec[pl.ds(1, HALF, stride=2), :] = jnp.where(row == 0, lone, odd * (2.0 / NZ))


def list_pairs(pair, count, own, other, other_edge):
    for e in range(ELEMS):
        count[e] = 0
    for n in range(ELEMS * 4):
        own[n] = -1
        other[n] = 0
        other_edge[n] = 0
    for row in range(PAIRS):
        for first, second in ((0, 2), (2, 0)):
            e = pair[first, row]
            slot = e * 4 + count[e]
            own[slot] = pair[first + 1, row]
            other[slot] = pair[second, row]
            other_edge[slot] = pair[second + 1, row]
            count[e] = count[e] + 1


def chip_modes(j):
    chip = (lax.axis_index("span") >> 1) ^ j
    return pl.ds(pl.multiple_of(chip * 2 * MODES, 2 * MODES), 2 * MODES)


def ready_kernel(bound, here, out):
    out[...] = here[0, 0:8, 0:128] + jnp.full((8, 128), bound[0, 0], jnp.int32).astype(F32)


def pack_element(packed, e, core, here, there):
    for at, v in ((core, here), (1 - core, there)):
        rows = pl.ds(pl.multiple_of(at * MODES, MODES), MODES)
        for c in range(3):
            packed[e, rows, c * 81 : c * 81 + 81] = v[c, :, e * 81 : e * 81 + 81]
        packed[e, rows, 243:256] = jnp.zeros((MODES, 13), F32)


def column_flags(bound, core, flags):
    for e in range(ELEMS):
        flags[e] = 0
    for row in range(ROWS):
        flags[bound[0, core * ROWS + row]] = 1


def pack_kernel(bound, here, there, ready, packed, *rest):
    outs, flags = rest[:4], rest[4]
    me, part = lax.axis_index("span"), lax.axis_index("dom")
    core = me & 1
    column_flags(bound, core, flags)
    for e in range(ELEMS):
        pl.when(flags[e] == 1)(lambda e=e: pack_element(packed, e, core, here, there))
    for j in range(4):
        outs[j][...] = packed[bound[0, row_of(me ^ (2 * j), part)]]


def edge_kernel(bound, pair, done, here, there, metric, pick, table, turn, columns, terms, *rest):
    outs = rest[:4]
    packed, rows, lines, scale, square, flags, count, own, other, other_edge = rest[4:]
    me, part = lax.axis_index("span"), lax.axis_index("dom")
    core = me & 1
    column_flags(bound, core, flags)
    list_pairs(pair, count, own, other, other_edge)

    def copy_element(e):
        packed[e] = done[e]

    for e in range(ELEMS):
        pl.when(flags[e] == 1)(lambda e=e: copy_element(e))
        pl.when(flags[e] == 0)(lambda e=e: pack_element(packed, e, core, here, there))
    rows[...] = jnp.zeros((16, 256), F32)
    for e in range(ELEMS):
        for j in range(4):
            at = e + 8 * (j // 2)
            lane = 128 * (j % 2)
            rows[at : at + 1, lane : lane + 81] = metric[j : j + 1, e * 81 : e * 81 + 81]
    rows_high, rows_low = split(rows[...])
    for s in range(4):
        here_lanes = pick[:, s * 128 : s * 128 + 128]
        size = dot(rows_high, here_lanes) + dot(rows_low, here_lanes)
        for n in range(16):
            scale[n * 4 + s] = size[n : n + 1, :]
    for n in range(16):
        lines[n] = rows[n : n + 1, :]
    square[...] = jnp.zeros((128, 128), F32)
    mine = bound[0, row_of(me, part)]
    for j in range(4):
        line = lines[mine + 8 * (j // 2)]
        square[j : j + 1, :] = line[:, 128 * (j % 2) : 128 * (j % 2) + 128]
    high, low = split(square[...].T)
    columns[...] = dot(turn[0:96, 0:128], high) + dot(turn[0:96, 0:128], low)
    side = bound[1, row_of(me, part)]
    along, across = scale[mine * 4 + side], scale[(8 + mine) * 4 + side]
    even = (side & 1) == 0
    terms[...] = jnp.zeros((8, 128), F32)
    terms[0:1, :] = jnp.where(side < 2, 1.0, -1.0) * jnp.where(even, along, across)
    terms[1:2, :] = jnp.where(even, across, along)
    lane = lax.broadcasted_iota(jnp.int32, (2 * MODES, 128), 1)
    for j in range(4):
        e = bound[0, row_of(me ^ (2 * j), part)]
        total = jnp.zeros((2 * MODES, 128), F32)
        for t in range(3):
            far, edge = other[e * 4 + t], other_edge[e * 4 + t]
            vh, vl = split(packed[far])
            high = table[edge, :, 0:256]
            value = dot(vh, high) + dot(vl, high) + dot(vh, table[edge, :, 256:512])
            value = (
                value[:, :128] * scale[far * 4 + edge]
                + value[:, 128:] * scale[(8 + far) * 4 + edge]
            )
            total = jnp.where((lane >= t * 42) & (lane < t * 42 + 42), value, total)
        outs[j][...] = total


def rim_kernel(bound, *rest):
    blocks = rest[:4]
    terms, table, send, high, low, modes, points = rest[4:]
    me, part = lax.axis_index("span"), lax.axis_index("dom")
    for j in range(4):
        for t in range(2):
            modes[t, chip_modes(j), :] = blocks[j][:, t * 128 : t * 128 + 128]
    for t in range(2):
        rows = slice(t * 128, t * 128 + 128)
        points[rows, 0:HALF], points[rows, HALF:] = pick_slots(modes.at[t])
    vh, vl = split(points[...])
    high[...] = vh
    low[...] = vl
    side = bound[1, row_of(me, part)]
    rows = dot(table[side], vh)
    across = rows[:32] + rows[32:] + dot(table[side, 0:32], vl)
    base = jnp.where(side == 0, 0, jnp.where(side == 1, 8, jnp.where(side == 2, 80, 72)))
    step = jnp.where(side == 0, 1, jnp.where(side == 1, 9, jnp.where(side == 2, -1, -9)))
    for c in range(3):
        for i in range(9):
            send[c * 9 + i : c * 9 + i + 1, :] = points[pl.ds(c * 81 + base + step * i, 1), :]
        send[27 + c * 7 : 34 + c * 7, :] = across[c * 8 : c * 8 + 7]
    send[48:56, :] = jnp.zeros((8, NZ), F32)
    send[48:56, 0:128] = terms[...]


def element_kernel(bound, high, low, columns, turn, tables, gh, gl, mine, u, q, g):
    me, part = lax.axis_index("span"), lax.axis_index("dom")
    slots = dot(turn[...], high[...]) + dot(turn[...], low[...])
    both = to_planes(jnp.concatenate([slots, slope_slots(slots)], axis=0), tables)
    value, slope = both[:288], both[288:]
    uh, ul = split(value)
    third = value[192:280]
    for c in range(3):
        rows = slice(96 * c, 96 * c + 96)
        both = dot(gh[...], uh[rows]) + dot(gh[...], ul[rows]) + dot(gl[...], uh[rows])
        fx, fe = both[:88], both[88:]
        g[c] = columns[0:88, 0:1] * fx + columns[0:88, 2:3] * fe
        g[3 + c] = columns[0:88, 1:2] * fx + columns[0:88, 3:4] * fe
        u[c] = value[96 * c : 96 * c + 88]
        q[c] = third * slope[96 * c : 96 * c + 88]
    base = INSIDE + 7 * bound[1, row_of(me, part)]
    mine[...] = jnp.zeros((88, NZ), F32)
    order = [(g, f) for f in range(6)] + [(u, 0), (u, 1)] + [(q, c) for c in range(3)]
    for f, (ref, at) in enumerate(order):
        for i in range(7):
            mine[f * 8 + 6 - i : f * 8 + 7 - i, :] = ref[at, pl.ds(base + i, 1), :]


def inside_kernel(u, q, g, tables, *rest):
    outs = rest[:4]
    term, spec = rest[4:]
    for c, count in ((0, 53), (1, 53), (2, 22)):
        value = u[0, 0:56] * g[c, 0:56] + u[1, 0:56] * g[3 + c, 0:56] + q[c, 0:56]
        term[53 * c : 53 * c + count, :] = value[:count]
    to_slots(term[...], tables, spec)
    for j in range(4):
        outs[j][...] = spec[chip_modes(j), :]


def edge_term_kernel(bound, pair, tables, *rest):
    blocks = rest[:4]
    u, q, g, term, modes, count, own, other, other_edge = rest[4:]
    me, part = lax.axis_index("span"), lax.axis_index("dom")
    list_pairs(pair, count, own, other, other_edge)
    for j in range(4):
        modes[chip_modes(j), :] = blocks[j][...]
    ph, pw = split(to_planes(jnp.concatenate(pick_slots(modes), axis=1), tables))
    e = bound[0, row_of(me, part)]
    lane = lax.broadcasted_iota(jnp.int32, (32, 128), 1)
    point = lax.broadcasted_iota(jnp.int32, (32, 128), 0)
    slot = jnp.where(lane < 42, 0, jnp.where(lane < 84, 1, 2))
    starts = []
    for t in range(3):
        edge = own[e * 4 + t]
        starts.append(jnp.where(edge < 0, -1000, 7 * edge))
    base = jnp.where(slot == 0, starts[0], jnp.where(slot == 1, starts[1], starts[2]))
    place = lane - slot * 42
    takes = []
    for f in range(6):
        xy, c = f // 3, f % 3
        i = 6 - (place - (c * 14 + xy * 7))
        hit = (i >= 0) & (i <= 6) & (lane < 126) & (point == base + i)
        takes.append(jnp.where(hit, 0.5, 0.0))
    keep = 1.0 - jnp.sum(takes[0], axis=1, keepdims=True)[:28]
    take = jnp.concatenate(takes, axis=0).astype(BF)
    far = dot(take, ph) + dot(take, pw)
    for c in range(3):
        u0, u1 = u[0, 53:81], u[1, 53:81]
        term[31 + 28 * c : 59 + 28 * c, :] = (
            u0 * (g[c, 53:81] * keep + far[c * 32 : c * 32 + 28])
            + u1 * (g[3 + c, 53:81] * keep + far[(3 + c) * 32 : (3 + c) * 32 + 28])
            + q[c, 53:81]
        )
    term[0:31, :] = u[0, 22:53] * g[2, 22:53] + u[1, 22:53] * g[5, 22:53] + q[2, 22:53]
    term[115:128, :] = jnp.zeros((13, NZ), F32)


def whole_kernel(bound, pair, *rest):
    blocks = rest[:4]
    high, low, columns, turn = rest[4:8]
    tables, (gh, gl) = rest[8:12], rest[12:14]
    outs, term, mine = rest[14:18], rest[18], rest[19]
    u, q, g, inside_term, spec, modes = rest[20:26]
    pairs = rest[26:]
    element_kernel(bound, high, low, columns, turn, tables, gh, gl, mine, u, q, g)
    inside_kernel(u, q, g, tables, *outs, inside_term, spec)
    edge_term_kernel(bound, pair, tables, *blocks, u, q, g, term, modes, *pairs)


def side_kernel(bound, term, mine, other, table, *rest):
    tables, outs = rest[:4], rest[4:8]
    work, spec, rows, square, turned = rest[8:]
    me, part = lax.axis_index("span"), lax.axis_index("dom")
    work[...] = term[...]
    rows[0:56] = other[...]
    rows[56:64] = jnp.zeros((8, NZ), F32)
    rh, rl = split(rows[...])
    near = dot(table[0], rh) + dot(table[0], rl) + dot(table[1], rh)
    value = to_planes(jnp.concatenate([near[0:72], slope_slots(near[0:24])], axis=0), tables)
    slope = value[72:96]
    square[...] = jnp.zeros((128, 128), F32)
    square[0:8, :] = other[48:56, 0:128]
    turned[...] = square[...].T
    base = 31 + 7 * bound[1, row_of(me, part)]
    u0 = mine[48:56, :] + value[0:8]
    u1 = mine[56:64, :] + value[8:16]
    for c in range(3):
        along, across = value[24 + 8 * c : 32 + 8 * c], value[48 + 8 * c : 56 + 8 * c]
        gx = mine[8 * c : 8 * c + 8, :] + (turned[0:8, 0:1] * along + turned[0:8, 1:2] * across)
        gy = mine[24 + 8 * c : 32 + 8 * c, :] + (
            turned[7:15, 0:1] * along + turned[7:15, 1:2] * across
        )
        q = mine[64 + 8 * c : 72 + 8 * c, :] + value[16:24] * slope[8 * c : 8 * c + 8]
        mean = (u0 * gx + u1 * gy) * 0.25 + q * 0.5
        for i in range(7):
            work[pl.ds(base + 28 * c + 6 - i, 1), :] = mean[i : i + 1, :]
    to_slots(work[...], tables, spec)
    for j in range(4):
        outs[j][...] = spec[chip_modes(j), :]


def cut_kernel(*rest):
    blocks, cross = rest[:4], rest[4]
    others = pl.ds(pl.multiple_of((1 - (lax.axis_index("span") & 1)) * MODES, MODES), MODES)
    for j in range(4):
        cross[j] = blocks[j][others, :]


def settle_kernel(bound, pair, *rest):
    inside, edge = rest[:4], rest[4:8]
    cross, edge_cross, take, give, where, back, out = rest[8:15]
    packed, edges, far, count, own, other, other_edge = rest[15:]
    me, part = lax.axis_index("span"), lax.axis_index("dom")
    list_pairs(pair, count, own, other, other_edge)
    mine = pl.ds(pl.multiple_of((me & 1) * MODES, MODES), MODES)
    for j in range(4):
        e = bound[0, row_of(me ^ (2 * j), part)]
        packed[e, :, 0:128] = inside[j][mine, :]
        packed[e, :, 128:256] = edge[j][mine, :]
        e = bound[0, row_of(me ^ (2 * j + 1), part)]
        packed[e, :, 0:128] = cross[j]
        packed[e, :, 128:256] = edge_cross[j]
    ph, pw = split(packed[:, :, 128:256].reshape(ELEMS * MODES, 128))
    edges[...] = (dot(ph, take[...]) + dot(pw, take[...])).reshape(ELEMS, MODES, 128)
    lane = lax.broadcasted_iota(jnp.int32, (MODES, 128), 1)
    for e in range(ELEMS):
        total = jnp.zeros((MODES, 128), F32)
        keep = jnp.ones((1, 128), F32)
        for t in range(3):
            edge = own[e * 4 + t]
            shift = (21 * (edge - other_edge[e * 4 + t]) + 128) & 127
            turned = pltpu.roll(edges[other[e * 4 + t]], shift, 1)
            low = edge * 21
            total = jnp.where((lane >= low) & (lane < low + 21) & (edge >= 0), turned, total)
            row = where[pl.ds(jnp.maximum(edge, 0), 1), :]
            keep = keep - jnp.where(edge >= 0, row, 0.0)
        far[e] = total
        packed[e, :, 128:256] = packed[e, :, 128:256] * keep
    fh, fl = split(far[...].reshape(ELEMS * MODES, 128))
    ph, pw = split(packed[...].reshape(ELEMS * MODES, 256))
    done = (
        dot(ph, back[...]) + dot(pw, back[...]) + dot(fh, give[...]) + dot(fl, give[...])
    )
    for e in range(ELEMS):
        for c in range(3):
            out[c, :, e * 81 : e * 81 + 81] = done[e * MODES : (e + 1) * MODES, c * 128 : c * 128 + 81]


def spec_of(space):
    return pl.BlockSpec(memory_space=space)


def call(kernel, name, scalars, arrays, outs, scratch=(), weight=1000):
    shapes = [
        shape if isinstance(shape, jax.ShapeDtypeStruct) else jax.ShapeDtypeStruct(shape, F32)
        for shape in outs
    ]
    return pl.pallas_call(
        kernel,
        out_shape=shapes,
        in_specs=[spec_of(pltpu.SMEM)] * len(scalars)
        + [spec_of(pltpu.VMEM)] * len(arrays),
        out_specs=[spec_of(pltpu.VMEM)] * len(outs),
        scratch_shapes=list(scratch),
        compiler_params=pltpu.CompilerParams(vmem_limit_bytes=LIMIT),
        cost_estimate=pl.CostEstimate(flops=weight, bytes_accessed=weight, transcendentals=0),
        name=name,
    )(*scalars, *arrays)


def pair_scratch():
    return [pltpu.SMEM((n,), jnp.int32) for n in (ELEMS, ELEMS * 4, ELEMS * 4, ELEMS * 4)]


def between_chips(blocks, order=(3, 2, 1)):
    far = {
        j: lax.ppermute(blocks[j], "span", [(s, s ^ (2 * j)) for s in range(SPAN)])
        for j in order
    }
    return [blocks[0], far[1], far[2], far[3]]


def between_cores(block):
    return lax.ppermute(block, "span", [(s, s ^ 1) for s in range(SPAN)])


def side_swap(block, parts):
    def device(part, row, side):
        return ((row ^ (3 * (part & 1))) * 2 + side) * parts + part

    perm = []
    for part in range(parts):
        before = (part - 1) % parts
        for row in range(ROWS):
            perm.append((device(part, row, 0), device(before, row, 1)))
            perm.append((device(before, row, 1), device(part, row, 0)))
    return lax.ppermute(block, ("span", "dom"), perm)


def on_device(velocity_modes, metric, pair_table, bound_table):
    cosines, sines = span_tables()
    tables = [*halves(cosines), *halves(sines)]
    gh, gl = halves(gradient_table())
    edge_table, pick = edge_tables()
    take, give, where, back = settle_tables()
    turn = halves(order_table())[0]
    chip, edge_chip = (2 * MODES, 256), (2 * MODES, 128)
    pair_table, bound_table = pair_table.T, bound_table.T
    flags = [pltpu.SMEM((ELEMS,), jnp.int32)]

    there = between_cores(velocity_modes)
    (ready,) = call(
        ready_kernel, "ready", [bound_table], [velocity_modes], [(8, 128)], weight=LONG
    )
    there, ready = lax.optimization_barrier((there, ready))
    packed, *blocks = call(
        pack_kernel,
        "pack",
        [bound_table],
        [velocity_modes, there, ready],
        [(ELEMS, 2 * MODES, 256)] + [chip] * 4,
        flags,
        weight=LONG,
    )
    blocks = between_chips(blocks)
    blocks[3], packed = lax.optimization_barrier((blocks[3], packed))
    columns, terms, *edge_blocks = call(
        edge_kernel,
        "edges",
        [bound_table, pair_table],
        [packed, velocity_modes, there, metric, pick, edge_table, turn],
        [(96, 128), (8, 128)] + [edge_chip] * 4,
        [
            pltpu.VMEM((ELEMS, 2 * MODES, 256), F32),
            pltpu.VMEM((16, 256), F32),
            pltpu.VMEM((16, 1, 256), F32),
            pltpu.VMEM((64, 1, 128), F32),
            pltpu.VMEM((128, 128), F32),
        ]
        + flags
        + pair_scratch(),
        weight=LONG,
    )
    edge_blocks = between_chips(edge_blocks)
    half = jax.ShapeDtypeStruct((256, NZ), BF)
    send, high, low = call(
        rim_kernel,
        "rim",
        [bound_table],
        [*blocks, terms, rim_table()],
        [(56, NZ), half, half],
        [pltpu.VMEM((2, NZ, 128), F32), pltpu.VMEM((256, NZ), F32)],
    )
    other = side_swap(send, lax.axis_size("dom"))
    modes_scratch = pltpu.VMEM((NZ, 128), F32)
    term_scratch = pltpu.VMEM((128, NZ), F32)
    *inside, term, mine = call(
        whole_kernel,
        "whole",
        [bound_table, pair_table],
        [*edge_blocks, high, low, columns, turn, *tables, gh, gl],
        [edge_chip] * 4 + [(128, NZ), (88, NZ)],
        [
            pltpu.VMEM((3, 88, NZ), F32),
            pltpu.VMEM((3, 88, NZ), F32),
            pltpu.VMEM((6, 88, NZ), F32),
            term_scratch,
            modes_scratch,
            modes_scratch,
        ]
        + pair_scratch(),
    )
    inside = between_chips(inside)
    edge = call(
        side_kernel,
        "side",
        [bound_table],
        [term, mine, other, np.stack(halves(far_table())), *tables],
        [edge_chip] * 4,
        [
            term_scratch,
            modes_scratch,
            pltpu.VMEM((64, NZ), F32),
            pltpu.VMEM((128, 128), F32),
            pltpu.VMEM((128, 128), F32),
        ],
    )
    edge = between_chips(edge)
    (cross,) = call(cut_kernel, "cut", [], inside, [(4, MODES, 128)])
    (edge_cross,) = call(cut_kernel, "cut_edge", [], edge, [(4, MODES, 128)])
    (out,) = call(
        settle_kernel,
        "settle",
        [bound_table, pair_table],
        [
            *inside,
            *edge,
            between_cores(cross),
            between_cores(edge_cross),
            *(halves(table)[0] for table in (take, give)),
            where.astype(np.float32),
            halves(back)[0],
        ],
        [(3, MODES, ELEMS * PTS)],
        [
            pltpu.VMEM((ELEMS, MODES, 256), F32),
            pltpu.VMEM((ELEMS, MODES, 128), F32),
            pltpu.VMEM((ELEMS, MODES, 128), F32),
        ]
        + pair_scratch(),
    )
    return out


def solution(mesh):
    return jax.shard_map(
        on_device,
        mesh=mesh,
        in_specs=(P(None, "span", "dom"), P(None, "dom"), P("dom", None), P("dom", None)),
        out_specs=P(None, "span", "dom"),
        check_vma=False,
    )
```

```python
import jax
import jax.numpy as jnp
import ml_dtypes
import numpy as np
from jax import lax
from jax.experimental import pallas as pl
from jax.experimental.pallas import tpu as pltpu
from jax.sharding import PartitionSpec as P

NZ = 512
HALF = 256
PTS = 81
ELEMS = 8
ROWS = 4
PAIRS = 10
SPAN = 8
MODES = NZ // SPAN
SPAN_RATE = 1.0 / 32.0
BF = jnp.bfloat16
F32 = jnp.float32
LIMIT = 48 * 1024 * 1024
LONG = 200_000_000


def legendre_rows(abscissa, node_count):
    legendre = np.zeros((node_count, node_count))
    legendre[:, 0] = 1.0
    legendre[:, 1] = abscissa
    for degree in range(2, node_count):
        legendre[:, degree] = (
            (2 * degree - 1) * abscissa * legendre[:, degree - 1]
            - (degree - 1) * legendre[:, degree - 2]
        ) / degree
    return legendre


def lobatto_matrix(order):
    node_count = order + 1
    abscissa = -np.cos(np.pi * np.arange(node_count) / order)
    for _ in range(60):
        legendre = legendre_rows(abscissa, node_count)
        abscissa = abscissa - (abscissa * legendre[:, order] - legendre[:, order - 1]) / (
            node_count * legendre[:, order]
        )
    legendre = legendre_rows(abscissa, node_count)
    end_values = legendre[:, order]
    spacing = abscissa[:, None] - abscissa[None, :] + np.eye(node_count)
    matrix = end_values[:, None] / (end_values[None, :] * spacing)
    matrix = matrix * (1.0 - np.eye(node_count))
    matrix[0, 0] = -order * node_count / 4.0
    matrix[order, order] = order * node_count / 4.0
    return matrix


def edge_points():
    positions = np.arange(9)
    outline = [positions, positions * 9 + 8, 72 + (8 - positions), (8 - positions) * 9]
    return np.stack(outline)[:, 1:8]


INSIDE = 53


def point_order():
    edges = edge_points().reshape(-1)
    inside = [point for point in range(PTS) if point not in set(edges.tolist())]
    return np.concatenate([inside, edges]).astype(int)


def lane_of(c, place):
    if place >= INSIDE:
        return 128 + 31 + 28 * c + place - INSIDE
    return 53 * c + place


def halves(table):
    high = table.astype(np.float32).astype(ml_dtypes.bfloat16)
    low = (table - high.astype(np.float64)).astype(np.float32).astype(ml_dtypes.bfloat16)
    return high, low


def span_tables():
    planes = np.arange(HALF)[None, :]
    waves = np.arange(HALF + 16)[:, None]
    angles = (planes * waves % NZ) * (2.0 * np.pi / NZ)
    cosines, sines = np.cos(angles), np.sin(angles)[:HALF]
    sines[0] = 1.0 - 2.0 * (np.arange(HALF) % 2)
    return cosines, sines


def point_matrices():
    lobatto = lobatto_matrix(8)
    return np.kron(np.eye(9), lobatto), np.kron(lobatto, np.eye(9))


def gradient_table():
    along_xi, along_eta = point_matrices()
    order = point_order()
    table = np.zeros((176, 96))
    table[:81, :81] = along_xi[np.ix_(order, order)]
    table[88:169, :81] = along_eta[np.ix_(order, order)]
    return table


def order_table():
    order = point_order()
    table = np.zeros((288, 256))
    for c in range(3):
        for place in range(PTS):
            table[c * 96 + place, c * 81 + order[place]] = 1.0
    return table


def rim_table():
    edges = edge_points()
    mats = point_matrices()
    table = np.zeros((4, 64, 256), ml_dtypes.bfloat16)
    for s in range(4):
        rows = np.zeros((32, 256))
        for c in range(3):
            rows[c * 8 : c * 8 + 7, c * 81 : c * 81 + 81] = mats[(s + 1) % 2][edges[s]]
        table[s, :32], table[s, 32:] = halves(rows)
    return table


def far_table():
    lobatto = lobatto_matrix(8)
    table = np.zeros((80, 64))
    for c in range(3):
        for i in range(7):
            table[c * 8 + i, c * 9 + i + 1] = 1.0
            table[24 + c * 8 + i, c * 9 : c * 9 + 9] = lobatto[i + 1]
            table[48 + c * 8 + i, 27 + c * 7 + i] = 1.0
    return table


def edge_tables():
    edges = edge_points()
    mats = point_matrices()
    table = np.zeros((256, 1024))
    pick = np.zeros((256, 512))
    for s in range(4):
        for t in range(3):
            for c in range(3):
                for xy in range(2):
                    for i in range(7):
                        lane = s * 128 + t * 42 + c * 14 + xy * 7 + i
                        for h in range(2):
                            table[c * 81 : c * 81 + 81, h * 512 + lane] = mats[h][edges[s, i]]
                        pick[xy * 128 + edges[s, i], lane] = 1.0
    high, low = halves(table)
    pick = halves(pick)[0]
    lanes = [slice(s * 128, s * 128 + 128) for s in range(4)]
    later = [slice(512 + s * 128, 640 + s * 128) for s in range(4)]
    return np.stack(
        [
            np.concatenate([high[:, n], high[:, m], low[:, n], low[:, m]], axis=1)
            for n, m in zip(lanes, later)
        ]
    ), pick


def settle_tables():
    order = point_order()
    take = np.zeros((128, 128))
    give = np.zeros((128, 384))
    where = np.zeros((8, 128))
    back = np.zeros((256, 384))
    for c in range(3):
        for place in range(PTS):
            back[lane_of(c, place), c * 128 + order[place]] = 1.0
        for s in range(4):
            for i in range(7):
                lane = s * 21 + c * 7 + i
                place = INSIDE + s * 7 + i
                take[lane_of(c, INSIDE + s * 7 + 6 - i) - 128, lane] = 1.0
                give[lane, c * 128 + order[place]] = 0.5
                where[s, lane_of(c, place) - 128] = 0.5
    return take, give, where, back


def row_of(place, part):
    return (place & 1) * ROWS + ((place >> 1) ^ (3 * (part & 1)))


def split(x):
    high = x.astype(BF)
    return high, (x - high.astype(F32)).astype(BF)


def dot(a, b, dims=((1,), (0,))):
    return lax.dot_general(a, b, (dims, ((), ())), preferred_element_type=F32)


def pick_slots(modes):
    even, odd = modes[pl.ds(0, HALF, stride=2), :], modes[pl.ds(1, HALF, stride=2), :]
    return even.T, odd.T


def to_planes(x, tables):
    ch, cl, sh, sl = tables
    high, low = split(x)
    ch, cl = ch[0:HALF], cl[0:HALF]
    sh, sl = sh[...], sl[...]
    even = dot(high[:, :HALF], ch) + dot(low[:, :HALF], ch) + dot(high[:, :HALF], cl)
    odd = dot(high[:, HALF:], sh) + dot(low[:, HALF:], sh) + dot(high[:, HALF:], sl)
    lane = lax.broadcasted_iota(jnp.int32, even.shape, 1)
    sign = jnp.where((lane & 1) == 0, 1.0, -1.0)
    lone = x[:, HALF : HALF + 1]
    middle = jnp.sum(x[:, :HALF] * sign, axis=1, keepdims=True) + lone
    mirror = jnp.where(lane == 0, middle, even - odd + (lone + lone) * sign)
    return jnp.concatenate([even + odd, mirror], axis=1)


def slope_slots(x):
    lane = lax.broadcasted_iota(jnp.int32, (x.shape[0], HALF), 1)
    rate = lane.astype(F32) * SPAN_RATE
    return jnp.concatenate([x[:, HALF:] * rate, -x[:, :HALF] * rate], axis=1)


def to_slots(term, tables, spec):
    ch, cl, sh, sl = tables
    first, mirror = term[:, :HALF], term[:, HALF:]
    lane = lax.broadcasted_iota(jnp.int32, first.shape, 1)
    eh, el = split(jnp.where(lane == 0, first, first + mirror))
    oh, ol = split(first - mirror)
    along = ((1,), (1,))
    even = dot(ch[...], eh, along) + dot(ch[...], el, along) + dot(cl[...], eh, along)
    odd = dot(sh[...], oh, along) + dot(sh[...], ol, along) + dot(sl[...], oh, along)
    row = lax.broadcasted_iota(jnp.int32, even.shape, 0)
    middle = mirror[:, 0:128].T[0:1, :]
    even = even + jnp.where((row & 1) == 0, 1.0, -1.0) * middle
    row = row[:HALF]
    lone = even[HALF : HALF + 1] * (1.0 / NZ)
    spec[pl.ds(0, HALF, stride=2), :] = even[:HALF] * jnp.where(row == 0, 1.0 / NZ, 2.0 / NZ)
    spec[pl.ds(1, HALF, stride=2), :] = jnp.where(row == 0, lone, odd * (2.0 / NZ))


def list_pairs(pair, count, own, other, other_edge):
    for e in range(ELEMS):
        count[e] = 0
    for n in range(ELEMS * 4):
        own[n] = -1
        other[n] = 0
        other_edge[n] = 0
    for row in range(PAIRS):
        for first, second in ((0, 2), (2, 0)):
            e = pair[first, row]
            slot = e * 4 + count[e]
            own[slot] = pair[first + 1, row]
            other[slot] = pair[second, row]
            other_edge[slot] = pair[second + 1, row]
            count[e] = count[e] + 1


def chip_modes(j):
    chip = (lax.axis_index("span") >> 1) ^ j
    return pl.ds(pl.multiple_of(chip * 2 * MODES, 2 * MODES), 2 * MODES)


def ready_kernel(bound, here, out):
    out[...] = here[0, 0:8, 0:128] + jnp.full((8, 128), bound[0, 0], jnp.int32).astype(F32)


def pack_element(packed, e, core, here, there):
    for at, v in ((core, here), (1 - core, there)):
        rows = pl.ds(pl.multiple_of(at * MODES, MODES), MODES)
        for c in range(3):
            packed[e, rows, c * 81 : c * 81 + 81] = v[c, :, e * 81 : e * 81 + 81]
        packed[e, rows, 243:256] = jnp.zeros((MODES, 13), F32)


def column_flags(bound, core, flags):
    for e in range(ELEMS):
        flags[e] = 0
    for row in range(ROWS):
        flags[bound[0, core * ROWS + row]] = 1


def pack_kernel(bound, here, there, ready, packed, *rest):
    outs, flags = rest[:4], rest[4]
    me, part = lax.axis_index("span"), lax.axis_index("dom")
    core = me & 1
    column_flags(bound, core, flags)
    for e in range(ELEMS):
        pl.when(flags[e] == 1)(lambda e=e: pack_element(packed, e, core, here, there))
    for j in range(4):
        outs[j][...] = packed[bound[0, row_of(me ^ (2 * j), part)]]


def metric_kernel(
    bound, done, here, there, metric, pick, turn, packed, scale, columns, terms, rows, lines, square, flags
):
    me, part = lax.axis_index("span"), lax.axis_index("dom")
    core = me & 1
    column_flags(bound, core, flags)

    def copy_element(e):
        packed[e] = done[e]

    for e in range(ELEMS):
        pl.when(flags[e] == 1)(lambda e=e: copy_element(e))
        pl.when(flags[e] == 0)(lambda e=e: pack_element(packed, e, core, here, there))
    rows[...] = jnp.zeros((16, 256), F32)
    for e in range(ELEMS):
        for j in range(4):
            at = e + 8 * (j // 2)
            lane = 128 * (j % 2)
            rows[at : at + 1, lane : lane + 81] = metric[j : j + 1, e * 81 : e * 81 + 81]
    rows_high, rows_low = split(rows[...])
    for s in range(4):
        here_lanes = pick[:, s * 128 : s * 128 + 128]
        size = dot(rows_high, here_lanes) + dot(rows_low, here_lanes)
        for n in range(16):
            scale[n * 4 + s] = size[n : n + 1, :]
    for n in range(16):
        lines[n] = rows[n : n + 1, :]
    square[...] = jnp.zeros((128, 128), F32)
    mine = bound[0, row_of(me, part)]
    for j in range(4):
        line = lines[mine + 8 * (j // 2)]
        square[j : j + 1, :] = line[:, 128 * (j % 2) : 128 * (j % 2) + 128]
    high, low = split(square[...].T)
    columns[...] = dot(turn[0:96, 0:128], high) + dot(turn[0:96, 0:128], low)
    side = bound[1, row_of(me, part)]
    along, across = scale[mine * 4 + side], scale[(8 + mine) * 4 + side]
    even = (side & 1) == 0
    terms[...] = jnp.zeros((8, 128), F32)
    terms[0:1, :] = jnp.where(side < 2, 1.0, -1.0) * jnp.where(even, along, across)
    terms[1:2, :] = jnp.where(even, across, along)


def edge_kernel(bound, pair, packed, scale, table, *rest):
    outs = rest[:4]
    count, own, other, other_edge = rest[4:]
    me, part = lax.axis_index("span"), lax.axis_index("dom")
    list_pairs(pair, count, own, other, other_edge)
    lane = lax.broadcasted_iota(jnp.int32, (2 * MODES, 128), 1)
    for j in range(4):
        e = bound[0, row_of(me ^ (2 * j), part)]
        total = jnp.zeros((2 * MODES, 128), F32)
        for t in range(3):
            far, edge = other[e * 4 + t], other_edge[e * 4 + t]
            vh, vl = split(packed[far])
            high = table[edge, :, 0:256]
            value = dot(vh, high) + dot(vl, high) + dot(vh, table[edge, :, 256:512])
            value = (
                value[:, :128] * scale[far * 4 + edge]
                + value[:, 128:] * scale[(8 + far) * 4 + edge]
            )
            total = jnp.where((lane >= t * 42) & (lane < t * 42 + 42), value, total)
        outs[j][...] = total


def rim_kernel(bound, *rest):
    blocks = rest[:4]
    terms, table, send, high, low, modes, points = rest[4:]
    me, part = lax.axis_index("span"), lax.axis_index("dom")
    for j in range(4):
        for t in range(2):
            modes[t, chip_modes(j), :] = blocks[j][:, t * 128 : t * 128 + 128]
    for t in range(2):
        rows = slice(t * 128, t * 128 + 128)
        points[rows, 0:HALF], points[rows, HALF:] = pick_slots(modes.at[t])
    vh, vl = split(points[...])
    high[...] = vh
    low[...] = vl
    side = bound[1, row_of(me, part)]
    rows = dot(table[side], vh)
    across = rows[:32] + rows[32:] + dot(table[side, 0:32], vl)
    base = jnp.where(side == 0, 0, jnp.where(side == 1, 8, jnp.where(side == 2, 80, 72)))
    step = jnp.where(side == 0, 1, jnp.where(side == 1, 9, jnp.where(side == 2, -1, -9)))
    for c in range(3):
        for i in range(9):
            send[c * 9 + i : c * 9 + i + 1, :] = points[pl.ds(c * 81 + base + step * i, 1), :]
        send[27 + c * 7 : 34 + c * 7, :] = across[c * 8 : c * 8 + 7]
    send[48:56, :] = jnp.zeros((8, NZ), F32)
    send[48:56, 0:128] = terms[...]


def element_kernel(bound, high, low, columns, turn, tables, gh, gl, mine, u, q, g):
    me, part = lax.axis_index("span"), lax.axis_index("dom")
    slots = dot(turn[...], high[...]) + dot(turn[...], low[...])
    both = to_planes(jnp.concatenate([slots, slope_slots(slots)], axis=0), tables)
    value, slope = both[:288], both[288:]
    uh, ul = split(value)
    third = value[192:280]
    for c in range(3):
        rows = slice(96 * c, 96 * c + 96)
        both = dot(gh[...], uh[rows]) + dot(gh[...], ul[rows]) + dot(gl[...], uh[rows])
        fx, fe = both[:88], both[88:]
        g[c] = columns[0:88, 0:1] * fx + columns[0:88, 2:3] * fe
        g[3 + c] = columns[0:88, 1:2] * fx + columns[0:88, 3:4] * fe
        u[c] = value[96 * c : 96 * c + 88]
        q[c] = third * slope[96 * c : 96 * c + 88]
    base = INSIDE + 7 * bound[1, row_of(me, part)]
    mine[...] = jnp.zeros((88, NZ), F32)
    order = [(g, f) for f in range(6)] + [(u, 0), (u, 1)] + [(q, c) for c in range(3)]
    for f, (ref, at) in enumerate(order):
        for i in range(7):
            mine[f * 8 + 6 - i : f * 8 + 7 - i, :] = ref[at, pl.ds(base + i, 1), :]


def inside_kernel(u, q, g, tables, *rest):
    outs = rest[:4]
    term, spec = rest[4:]
    for c, count in ((0, 53), (1, 53), (2, 22)):
        value = u[0, 0:56] * g[c, 0:56] + u[1, 0:56] * g[3 + c, 0:56] + q[c, 0:56]
        term[53 * c : 53 * c + count, :] = value[:count]
    to_slots(term[...], tables, spec)
    for j in range(4):
        outs[j][...] = spec[chip_modes(j), :]


def edge_term_kernel(bound, pair, tables, *rest):
    blocks = rest[:4]
    u, q, g, term, modes, count, own, other, other_edge = rest[4:]
    me, part = lax.axis_index("span"), lax.axis_index("dom")
    list_pairs(pair, count, own, other, other_edge)
    for j in range(4):
        modes[chip_modes(j), :] = blocks[j][...]
    ph, pw = split(to_planes(jnp.concatenate(pick_slots(modes), axis=1), tables))
    e = bound[0, row_of(me, part)]
    lane = lax.broadcasted_iota(jnp.int32, (32, 128), 1)
    point = lax.broadcasted_iota(jnp.int32, (32, 128), 0)
    slot = jnp.where(lane < 42, 0, jnp.where(lane < 84, 1, 2))
    starts = []
    for t in range(3):
        edge = own[e * 4 + t]
        starts.append(jnp.where(edge < 0, -1000, 7 * edge))
    base = jnp.where(slot == 0, starts[0], jnp.where(slot == 1, starts[1], starts[2]))
    place = lane - slot * 42
    takes = []
    for f in range(6):
        xy, c = f // 3, f % 3
        i = 6 - (place - (c * 14 + xy * 7))
        hit = (i >= 0) & (i <= 6) & (lane < 126) & (point == base + i)
        takes.append(jnp.where(hit, 0.5, 0.0))
    keep = 1.0 - jnp.sum(takes[0], axis=1, keepdims=True)[:28]
    take = jnp.concatenate(takes, axis=0).astype(BF)
    far = dot(take, ph) + dot(take, pw)
    for c in range(3):
        u0, u1 = u[0, 53:81], u[1, 53:81]
        term[31 + 28 * c : 59 + 28 * c, :] = (
            u0 * (g[c, 53:81] * keep + far[c * 32 : c * 32 + 28])
            + u1 * (g[3 + c, 53:81] * keep + far[(3 + c) * 32 : (3 + c) * 32 + 28])
            + q[c, 53:81]
        )
    term[0:31, :] = u[0, 22:53] * g[2, 22:53] + u[1, 22:53] * g[5, 22:53] + q[2, 22:53]
    term[115:128, :] = jnp.zeros((13, NZ), F32)


def whole_kernel(bound, pair, *rest):
    blocks = rest[:4]
    high, low, columns, turn = rest[4:8]
    tables, (gh, gl) = rest[8:12], rest[12:14]
    outs, term, mine = rest[14:18], rest[18], rest[19]
    u, q, g, inside_term, spec, modes = rest[20:26]
    pairs = rest[26:]
    element_kernel(bound, high, low, columns, turn, tables, gh, gl, mine, u, q, g)
    inside_kernel(u, q, g, tables, *outs, inside_term, spec)
    edge_term_kernel(bound, pair, tables, *blocks, u, q, g, term, modes, *pairs)


def side_kernel(bound, term, mine, other, table, *rest):
    tables, outs = rest[:4], rest[4:8]
    work, spec, rows, square, turned = rest[8:]
    me, part = lax.axis_index("span"), lax.axis_index("dom")
    work[...] = term[...]
    rows[0:56] = other[...]
    rows[56:64] = jnp.zeros((8, NZ), F32)
    rh, rl = split(rows[...])
    near = dot(table[0], rh) + dot(table[0], rl) + dot(table[1], rh)
    value = to_planes(jnp.concatenate([near[0:72], slope_slots(near[0:24])], axis=0), tables)
    slope = value[72:96]
    square[...] = jnp.zeros((128, 128), F32)
    square[0:8, :] = other[48:56, 0:128]
    turned[...] = square[...].T
    base = 31 + 7 * bound[1, row_of(me, part)]
    u0 = mine[48:56, :] + value[0:8]
    u1 = mine[56:64, :] + value[8:16]
    for c in range(3):
        along, across = value[24 + 8 * c : 32 + 8 * c], value[48 + 8 * c : 56 + 8 * c]
        gx = mine[8 * c : 8 * c + 8, :] + (turned[0:8, 0:1] * along + turned[0:8, 1:2] * across)
        gy = mine[24 + 8 * c : 32 + 8 * c, :] + (
            turned[7:15, 0:1] * along + turned[7:15, 1:2] * across
        )
        q = mine[64 + 8 * c : 72 + 8 * c, :] + value[16:24] * slope[8 * c : 8 * c + 8]
        mean = (u0 * gx + u1 * gy) * 0.25 + q * 0.5
        for i in range(7):
            work[pl.ds(base + 28 * c + 6 - i, 1), :] = mean[i : i + 1, :]
    to_slots(work[...], tables, spec)
    for j in range(4):
        outs[j][...] = spec[chip_modes(j), :]


def cut_kernel(*rest):
    blocks, cross = rest[:4], rest[4]
    others = pl.ds(pl.multiple_of((1 - (lax.axis_index("span") & 1)) * MODES, MODES), MODES)
    for j in range(4):
        cross[j] = blocks[j][others, :]


def settle_kernel(bound, pair, *rest):
    inside, edge = rest[:4], rest[4:8]
    cross, edge_cross, take, give, where, back, out = rest[8:15]
    packed, edges, far, count, own, other, other_edge = rest[15:]
    me, part = lax.axis_index("span"), lax.axis_index("dom")
    list_pairs(pair, count, own, other, other_edge)
    mine = pl.ds(pl.multiple_of((me & 1) * MODES, MODES), MODES)
    for j in range(4):
        e = bound[0, row_of(me ^ (2 * j), part)]
        packed[e, :, 0:128] = inside[j][mine, :]
        packed[e, :, 128:256] = edge[j][mine, :]
        e = bound[0, row_of(me ^ (2 * j + 1), part)]
        packed[e, :, 0:128] = cross[j]
        packed[e, :, 128:256] = edge_cross[j]
    ph, pw = split(packed[:, :, 128:256].reshape(ELEMS * MODES, 128))
    edges[...] = (dot(ph, take[...]) + dot(pw, take[...])).reshape(ELEMS, MODES, 128)
    lane = lax.broadcasted_iota(jnp.int32, (MODES, 128), 1)
    for e in range(ELEMS):
        total = jnp.zeros((MODES, 128), F32)
        keep = jnp.ones((1, 128), F32)
        for t in range(3):
            edge = own[e * 4 + t]
            shift = (21 * (edge - other_edge[e * 4 + t]) + 128) & 127
            turned = pltpu.roll(edges[other[e * 4 + t]], shift, 1)
            low = edge * 21
            total = jnp.where((lane >= low) & (lane < low + 21) & (edge >= 0), turned, total)
            row = where[pl.ds(jnp.maximum(edge, 0), 1), :]
            keep = keep - jnp.where(edge >= 0, row, 0.0)
        far[e] = total
        packed[e, :, 128:256] = packed[e, :, 128:256] * keep
    fh, fl = split(far[...].reshape(ELEMS * MODES, 128))
    ph, pw = split(packed[...].reshape(ELEMS * MODES, 256))
    done = (
        dot(ph, back[...]) + dot(pw, back[...]) + dot(fh, give[...]) + dot(fl, give[...])
    )
    for e in range(ELEMS):
        for c in range(3):
            out[c, :, e * 81 : e * 81 + 81] = done[e * MODES : (e + 1) * MODES, c * 128 : c * 128 + 81]


def spec_of(space):
    return pl.BlockSpec(memory_space=space)


def call(kernel, name, scalars, arrays, outs, scratch=(), weight=1000):
    shapes = [
        shape if isinstance(shape, jax.ShapeDtypeStruct) else jax.ShapeDtypeStruct(shape, F32)
        for shape in outs
    ]
    return pl.pallas_call(
        kernel,
        out_shape=shapes,
        in_specs=[spec_of(pltpu.SMEM)] * len(scalars)
        + [spec_of(pltpu.VMEM)] * len(arrays),
        out_specs=[spec_of(pltpu.VMEM)] * len(outs),
        scratch_shapes=list(scratch),
        compiler_params=pltpu.CompilerParams(vmem_limit_bytes=LIMIT),
        cost_estimate=pl.CostEstimate(flops=weight, bytes_accessed=weight, transcendentals=0),
        name=name,
    )(*scalars, *arrays)


def pair_scratch():
    return [pltpu.SMEM((n,), jnp.int32) for n in (ELEMS, ELEMS * 4, ELEMS * 4, ELEMS * 4)]


def between_chips(blocks, order=(3, 2, 1)):
    far = {
        j: lax.ppermute(blocks[j], "span", [(s, s ^ (2 * j)) for s in range(SPAN)])
        for j in order
    }
    return [blocks[0], far[1], far[2], far[3]]


def between_cores(block):
    return lax.ppermute(block, "span", [(s, s ^ 1) for s in range(SPAN)])


def side_swap(block, parts):
    def device(part, row, side):
        return ((row ^ (3 * (part & 1))) * 2 + side) * parts + part

    perm = []
    for part in range(parts):
        before = (part - 1) % parts
        for row in range(ROWS):
            perm.append((device(part, row, 0), device(before, row, 1)))
            perm.append((device(before, row, 1), device(part, row, 0)))
    return lax.ppermute(block, ("span", "dom"), perm)


def on_device(velocity_modes, metric, pair_table, bound_table):
    cosines, sines = span_tables()
    tables = [*halves(cosines), *halves(sines)]
    gh, gl = halves(gradient_table())
    edge_table, pick = edge_tables()
    take, give, where, back = settle_tables()
    turn = halves(order_table())[0]
    chip, edge_chip = (2 * MODES, 256), (2 * MODES, 128)
    pair_table, bound_table = pair_table.T, bound_table.T
    flags = [pltpu.SMEM((ELEMS,), jnp.int32)]

    there = between_cores(velocity_modes)
    (ready,) = call(
        ready_kernel, "ready", [bound_table], [velocity_modes], [(8, 128)], weight=LONG
    )
    there, ready = lax.optimization_barrier((there, ready))
    packed, *blocks = call(
        pack_kernel,
        "pack",
        [bound_table],
        [velocity_modes, there, ready],
        [(ELEMS, 2 * MODES, 256)] + [chip] * 4,
        flags,
        weight=LONG,
    )
    blocks = between_chips(blocks)
    packed, scale, columns, terms = call(
        metric_kernel,
        "metric",
        [bound_table],
        [packed, velocity_modes, there, metric, pick, turn],
        [(ELEMS, 2 * MODES, 256), (64, 1, 128), (96, 128), (8, 128)],
        [pltpu.VMEM((16, 256), F32), pltpu.VMEM((16, 1, 256), F32), pltpu.VMEM((128, 128), F32)]
        + flags,
        weight=LONG,
    )
    blocks[3], packed = lax.optimization_barrier((blocks[3], packed))
    edge_blocks = call(
        edge_kernel,
        "edges",
        [bound_table, pair_table],
        [packed, scale, edge_table],
        [edge_chip] * 4,
        pair_scratch(),
        weight=LONG,
    )
    edge_blocks = between_chips(edge_blocks)
    half = jax.ShapeDtypeStruct((256, NZ), BF)
    send, high, low = call(
        rim_kernel,
        "rim",
        [bound_table],
        [*blocks, terms, rim_table()],
        [(56, NZ), half, half],
        [pltpu.VMEM((2, NZ, 128), F32), pltpu.VMEM((256, NZ), F32)],
    )
    other = side_swap(send, lax.axis_size("dom"))
    modes_scratch = pltpu.VMEM((NZ, 128), F32)
    term_scratch = pltpu.VMEM((128, NZ), F32)
    *inside, term, mine = call(
        whole_kernel,
        "whole",
        [bound_table, pair_table],
        [*edge_blocks, high, low, columns, turn, *tables, gh, gl],
        [edge_chip] * 4 + [(128, NZ), (88, NZ)],
        [
            pltpu.VMEM((3, 88, NZ), F32),
            pltpu.VMEM((3, 88, NZ), F32),
            pltpu.VMEM((6, 88, NZ), F32),
            term_scratch,
            modes_scratch,
            modes_scratch,
        ]
        + pair_scratch(),
    )
    inside = between_chips(inside)
    edge = call(
        side_kernel,
        "side",
        [bound_table],
        [term, mine, other, np.stack(halves(far_table())), *tables],
        [edge_chip] * 4,
        [
            term_scratch,
            modes_scratch,
            pltpu.VMEM((64, NZ), F32),
            pltpu.VMEM((128, 128), F32),
            pltpu.VMEM((128, 128), F32),
        ],
    )
    edge = between_chips(edge)
    (cross,) = call(cut_kernel, "cut", [], inside, [(4, MODES, 128)])
    (edge_cross,) = call(cut_kernel, "cut_edge", [], edge, [(4, MODES, 128)])
    (out,) = call(
        settle_kernel,
        "settle",
        [bound_table, pair_table],
        [
            *inside,
            *edge,
            between_cores(cross),
            between_cores(edge_cross),
            *(halves(table)[0] for table in (take, give)),
            where.astype(np.float32),
            halves(back)[0],
        ],
        [(3, MODES, ELEMS * PTS)],
        [
            pltpu.VMEM((ELEMS, MODES, 256), F32),
            pltpu.VMEM((ELEMS, MODES, 128), F32),
            pltpu.VMEM((ELEMS, MODES, 128), F32),
        ]
        + pair_scratch(),
    )
    return out


def solution(mesh):
    return jax.shard_map(
        on_device,
        mesh=mesh,
        in_specs=(P(None, "span", "dom"), P(None, "dom"), P("dom", None), P("dom", None)),
        out_specs=P(None, "span", "dom"),
        check_vma=False,
    )
```

```python
import jax
import jax.numpy as jnp
import ml_dtypes
import numpy as np
from jax import lax
from jax.experimental import pallas as pl
from jax.experimental.pallas import tpu as pltpu
from jax.sharding import PartitionSpec as P

NZ = 512
HALF = 256
PTS = 81
ELEMS = 8
ROWS = 4
PAIRS = 10
SPAN = 8
MODES = NZ // SPAN
SPAN_RATE = 1.0 / 32.0
BF = jnp.bfloat16
F32 = jnp.float32
LIMIT = 48 * 1024 * 1024
LONG = 200_000_000


def legendre_rows(abscissa, node_count):
    legendre = np.zeros((node_count, node_count))
    legendre[:, 0] = 1.0
    legendre[:, 1] = abscissa
    for degree in range(2, node_count):
        legendre[:, degree] = (
            (2 * degree - 1) * abscissa * legendre[:, degree - 1]
            - (degree - 1) * legendre[:, degree - 2]
        ) / degree
    return legendre


def lobatto_matrix(order):
    node_count = order + 1
    abscissa = -np.cos(np.pi * np.arange(node_count) / order)
    for _ in range(60):
        legendre = legendre_rows(abscissa, node_count)
        abscissa = abscissa - (abscissa * legendre[:, order] - legendre[:, order - 1]) / (
            node_count * legendre[:, order]
        )
    legendre = legendre_rows(abscissa, node_count)
    end_values = legendre[:, order]
    spacing = abscissa[:, None] - abscissa[None, :] + np.eye(node_count)
    matrix = end_values[:, None] / (end_values[None, :] * spacing)
    matrix = matrix * (1.0 - np.eye(node_count))
    matrix[0, 0] = -order * node_count / 4.0
    matrix[order, order] = order * node_count / 4.0
    return matrix


def edge_points():
    positions = np.arange(9)
    outline = [positions, positions * 9 + 8, 72 + (8 - positions), (8 - positions) * 9]
    return np.stack(outline)[:, 1:8]


INSIDE = 53


def point_order():
    edges = edge_points().reshape(-1)
    inside = [point for point in range(PTS) if point not in set(edges.tolist())]
    return np.concatenate([inside, edges]).astype(int)


def lane_of(c, place):
    if place >= INSIDE:
        return 128 + 31 + 28 * c + place - INSIDE
    return 53 * c + place


def halves(table):
    high = table.astype(np.float32).astype(ml_dtypes.bfloat16)
    low = (table - high.astype(np.float64)).astype(np.float32).astype(ml_dtypes.bfloat16)
    return high, low


def span_tables():
    planes = np.arange(HALF)[None, :]
    waves = np.arange(HALF + 16)[:, None]
    angles = (planes * waves % NZ) * (2.0 * np.pi / NZ)
    cosines, sines = np.cos(angles), np.sin(angles)[:HALF]
    sines[0] = 1.0 - 2.0 * (np.arange(HALF) % 2)
    return cosines, sines


def point_matrices():
    lobatto = lobatto_matrix(8)
    return np.kron(np.eye(9), lobatto), np.kron(lobatto, np.eye(9))


def gradient_table():
    along_xi, along_eta = point_matrices()
    order = point_order()
    table = np.zeros((176, 96))
    table[:81, :81] = along_xi[np.ix_(order, order)]
    table[88:169, :81] = along_eta[np.ix_(order, order)]
    return table


def order_table():
    order = point_order()
    table = np.zeros((288, 256))
    for c in range(3):
        for place in range(PTS):
            table[c * 96 + place, c * 81 + order[place]] = 1.0
    return table


def rim_table():
    edges = edge_points()
    mats = point_matrices()
    table = np.zeros((4, 64, 256), ml_dtypes.bfloat16)
    for s in range(4):
        rows = np.zeros((32, 256))
        for c in range(3):
            rows[c * 8 : c * 8 + 7, c * 81 : c * 81 + 81] = mats[(s + 1) % 2][edges[s]]
        table[s, :32], table[s, 32:] = halves(rows)
    return table


def far_table():
    lobatto = lobatto_matrix(8)
    table = np.zeros((80, 64))
    for c in range(3):
        for i in range(7):
            table[c * 8 + i, c * 9 + i + 1] = 1.0
            table[24 + c * 8 + i, c * 9 : c * 9 + 9] = lobatto[i + 1]
            table[48 + c * 8 + i, 27 + c * 7 + i] = 1.0
    return table


def edge_tables():
    edges = edge_points()
    mats = point_matrices()
    table = np.zeros((256, 1024))
    pick = np.zeros((256, 512))
    for s in range(4):
        for t in range(3):
            for c in range(3):
                for xy in range(2):
                    for i in range(7):
                        lane = s * 128 + t * 42 + c * 14 + xy * 7 + i
                        for h in range(2):
                            table[c * 81 : c * 81 + 81, h * 512 + lane] = mats[h][edges[s, i]]
                        pick[xy * 128 + edges[s, i], lane] = 1.0
    high, low = halves(table)
    pick = halves(pick)[0]
    lanes = [slice(s * 128, s * 128 + 128) for s in range(4)]
    later = [slice(512 + s * 128, 640 + s * 128) for s in range(4)]
    return np.stack(
        [
            np.concatenate([high[:, n], high[:, m], low[:, n], low[:, m]], axis=1)
            for n, m in zip(lanes, later)
        ]
    ), pick


def settle_tables():
    order = point_order()
    take = np.zeros((128, 128))
    give = np.zeros((128, 384))
    where = np.zeros((8, 128))
    back = np.zeros((256, 384))
    for c in range(3):
        for place in range(PTS):
            back[lane_of(c, place), c * 128 + order[place]] = 1.0
        for s in range(4):
            for i in range(7):
                lane = s * 21 + c * 7 + i
                place = INSIDE + s * 7 + i
                take[lane_of(c, INSIDE + s * 7 + 6 - i) - 128, lane] = 1.0
                give[lane, c * 128 + order[place]] = 0.5
                where[s, lane_of(c, place) - 128] = 0.5
    return take, give, where, back


def row_of(place, part):
    return (place & 1) * ROWS + ((place >> 1) ^ (3 * (part & 1)))


def split(x):
    high = x.astype(BF)
    return high, (x - high.astype(F32)).astype(BF)


def dot(a, b, dims=((1,), (0,))):
    return lax.dot_general(a, b, (dims, ((), ())), preferred_element_type=F32)


def pick_slots(modes):
    even, odd = modes[pl.ds(0, HALF, stride=2), :], modes[pl.ds(1, HALF, stride=2), :]
    return even.T, odd.T


def to_planes(x, tables):
    ch, cl, sh, sl = tables
    high, low = split(x)
    ch, cl = ch[0:HALF], cl[0:HALF]
    sh, sl = sh[...], sl[...]
    even = dot(high[:, :HALF], ch) + dot(low[:, :HALF], ch) + dot(high[:, :HALF], cl)
    odd = dot(high[:, HALF:], sh) + dot(low[:, HALF:], sh) + dot(high[:, HALF:], sl)
    lane = lax.broadcasted_iota(jnp.int32, even.shape, 1)
    sign = jnp.where((lane & 1) == 0, 1.0, -1.0)
    lone = x[:, HALF : HALF + 1]
    middle = jnp.sum(x[:, :HALF] * sign, axis=1, keepdims=True) + lone
    mirror = jnp.where(lane == 0, middle, even - odd + (lone + lone) * sign)
    return jnp.concatenate([even + odd, mirror], axis=1)


def slope_slots(x):
    lane = lax.broadcasted_iota(jnp.int32, (x.shape[0], HALF), 1)
    rate = lane.astype(F32) * SPAN_RATE
    return jnp.concatenate([x[:, HALF:] * rate, -x[:, :HALF] * rate], axis=1)


def to_slots(term, tables, spec):
    ch, cl, sh, sl = tables
    first, mirror = term[:, :HALF], term[:, HALF:]
    lane = lax.broadcasted_iota(jnp.int32, first.shape, 1)
    eh, el = split(jnp.where(lane == 0, first, first + mirror))
    oh, ol = split(first - mirror)
    along = ((1,), (1,))
    even = dot(ch[...], eh, along) + dot(ch[...], el, along) + dot(cl[...], eh, along)
    odd = dot(sh[...], oh, along) + dot(sh[...], ol, along) + dot(sl[...], oh, along)
    row = lax.broadcasted_iota(jnp.int32, even.shape, 0)
    middle = mirror[:, 0:128].T[0:1, :]
    even = even + jnp.where((row & 1) == 0, 1.0, -1.0) * middle
    row = row[:HALF]
    lone = even[HALF : HALF + 1] * (1.0 / NZ)
    spec[pl.ds(0, HALF, stride=2), :] = even[:HALF] * jnp.where(row == 0, 1.0 / NZ, 2.0 / NZ)
    spec[pl.ds(1, HALF, stride=2), :] = jnp.where(row == 0, lone, odd * (2.0 / NZ))


def list_pairs(pair, count, own, other, other_edge):
    for e in range(ELEMS):
        count[e] = 0
    for n in range(ELEMS * 4):
        own[n] = -1
        other[n] = 0
        other_edge[n] = 0
    for row in range(PAIRS):
        for first, second in ((2, 4), (4, 2)):
            e = pair[first, row]
            slot = e * 4 + count[e]
            own[slot] = pair[first + 1, row]
            other[slot] = pair[second, row]
            other_edge[slot] = pair[second + 1, row]
            count[e] = count[e] + 1


def chip_modes(j):
    chip = (lax.axis_index("span") >> 1) ^ j
    return pl.ds(pl.multiple_of(chip * 2 * MODES, 2 * MODES), 2 * MODES)


def ready_kernel(bound, here, out):
    out[...] = here[0, 0:8, 0:128] + jnp.full((8, 128), bound[0, 0], jnp.int32).astype(F32)


def pack_element(packed, e, core, here, there):
    for at, v in ((core, here), (1 - core, there)):
        rows = pl.ds(pl.multiple_of(at * MODES, MODES), MODES)
        for c in range(3):
            packed[e, rows, c * 81 : c * 81 + 81] = v[c, :, e * 81 : e * 81 + 81]
        packed[e, rows, 243:256] = jnp.zeros((MODES, 13), F32)


def column_flags(bound, core, flags):
    for e in range(ELEMS):
        flags[e] = 0
    for row in range(ROWS):
        flags[bound[0, core * ROWS + row]] = 1


def pack_kernel(bound, here, there, ready, packed, *rest):
    outs, flags = rest[:4], rest[4]
    me, part = lax.axis_index("span"), lax.axis_index("dom")
    core = me & 1
    column_flags(bound, core, flags)
    for e in range(ELEMS):
        pl.when(flags[e] == 1)(lambda e=e: pack_element(packed, e, core, here, there))
    for j in range(4):
        outs[j][...] = packed[bound[0, row_of(me ^ (2 * j), part)]]


def metric_kernel(
    bound, done, here, there, metric, pick, turn, packed, scale, columns, terms, rows, lines, square, flags
):
    me, part = lax.axis_index("span"), lax.axis_index("dom")
    core = me & 1
    column_flags(bound, core, flags)

    def copy_element(e):
        packed[e] = done[e]

    for e in range(ELEMS):
        pl.when(flags[e] == 1)(lambda e=e: copy_element(e))
        pl.when(flags[e] == 0)(lambda e=e: pack_element(packed, e, core, here, there))
    rows[...] = jnp.zeros((16, 256), F32)
    for e in range(ELEMS):
        for j in range(4):
            at = e + 8 * (j // 2)
            lane = 128 * (j % 2)
            rows[at : at + 1, lane : lane + 81] = metric[j : j + 1, e * 81 : e * 81 + 81]
    rows_high, rows_low = split(rows[...])
    for s in range(4):
        here_lanes = pick[:, s * 128 : s * 128 + 128]
        size = dot(rows_high, here_lanes) + dot(rows_low, here_lanes)
        for n in range(16):
            scale[n * 4 + s] = size[n : n + 1, :]
    for n in range(16):
        lines[n] = rows[n : n + 1, :]
    square[...] = jnp.zeros((128, 128), F32)
    mine = bound[0, row_of(me, part)]
    for j in range(4):
        line = lines[mine + 8 * (j // 2)]
        square[j : j + 1, :] = line[:, 128 * (j % 2) : 128 * (j % 2) + 128]
    high, low = split(square[...].T)
    columns[...] = dot(turn[0:96, 0:128], high) + dot(turn[0:96, 0:128], low)
    side = bound[1, row_of(me, part)]
    along, across = scale[mine * 4 + side], scale[(8 + mine) * 4 + side]
    even = (side & 1) == 0
    terms[...] = jnp.zeros((8, 128), F32)
    terms[0:1, :] = jnp.where(side < 2, 1.0, -1.0) * jnp.where(even, along, across)
    terms[1:2, :] = jnp.where(even, across, along)


def edge_kernel(bound, pair, packed, scale, table, *rest):
    outs = rest[:4]
    count, own, other, other_edge = rest[4:]
    me, part = lax.axis_index("span"), lax.axis_index("dom")
    list_pairs(pair, count, own, other, other_edge)
    lane = lax.broadcasted_iota(jnp.int32, (2 * MODES, 128), 1)
    for j in range(4):
        e = bound[0, row_of(me ^ (2 * j), part)]
        total = jnp.zeros((2 * MODES, 128), F32)
        for t in range(3):
            far, edge = other[e * 4 + t], other_edge[e * 4 + t]
            vh, vl = split(packed[far])
            high = table[edge, :, 0:256]
            value = dot(vh, high) + dot(vl, high) + dot(vh, table[edge, :, 256:512])
            value = (
                value[:, :128] * scale[far * 4 + edge]
                + value[:, 128:] * scale[(8 + far) * 4 + edge]
            )
            total = jnp.where((lane >= t * 42) & (lane < t * 42 + 42), value, total)
        outs[j][...] = total


def rim_kernel(bound, *rest):
    blocks = rest[:4]
    terms, table, send, high, low, modes, points = rest[4:]
    me, part = lax.axis_index("span"), lax.axis_index("dom")
    for j in range(4):
        for t in range(2):
            modes[t, chip_modes(j), :] = blocks[j][:, t * 128 : t * 128 + 128]
    for t in range(2):
        rows = slice(t * 128, t * 128 + 128)
        points[rows, 0:HALF], points[rows, HALF:] = pick_slots(modes.at[t])
    vh, vl = split(points[...])
    high[...] = vh
    low[...] = vl
    side = bound[1, row_of(me, part)]
    rows = dot(table[side], vh)
    across = rows[:32] + rows[32:] + dot(table[side, 0:32], vl)
    base = jnp.where(side == 0, 0, jnp.where(side == 1, 8, jnp.where(side == 2, 80, 72)))
    step = jnp.where(side == 0, 1, jnp.where(side == 1, 9, jnp.where(side == 2, -1, -9)))
    for c in range(3):
        for i in range(9):
            send[c * 9 + i : c * 9 + i + 1, :] = points[pl.ds(c * 81 + base + step * i, 1), :]
        send[27 + c * 7 : 34 + c * 7, :] = across[c * 8 : c * 8 + 7]
    send[48:56, :] = jnp.zeros((8, NZ), F32)
    send[48:56, 0:128] = terms[...]


def element_kernel(bound, high, low, columns, turn, tables, gh, gl, mine, u, q, g):
    me, part = lax.axis_index("span"), lax.axis_index("dom")
    slots = dot(turn[...], high[...]) + dot(turn[...], low[...])
    both = to_planes(jnp.concatenate([slots, slope_slots(slots)], axis=0), tables)
    value, slope = both[:288], both[288:]
    uh, ul = split(value)
    third = value[192:280]
    for c in range(3):
        rows = slice(96 * c, 96 * c + 96)
        both = dot(gh[...], uh[rows]) + dot(gh[...], ul[rows]) + dot(gl[...], uh[rows])
        fx, fe = both[:88], both[88:]
        g[c] = columns[0:88, 0:1] * fx + columns[0:88, 2:3] * fe
        g[3 + c] = columns[0:88, 1:2] * fx + columns[0:88, 3:4] * fe
        u[c] = value[96 * c : 96 * c + 88]
        q[c] = third * slope[96 * c : 96 * c + 88]
    base = INSIDE + 7 * bound[1, row_of(me, part)]
    mine[...] = jnp.zeros((88, NZ), F32)
    order = [(g, f) for f in range(6)] + [(u, 0), (u, 1)] + [(q, c) for c in range(3)]
    for f, (ref, at) in enumerate(order):
        for i in range(7):
            mine[f * 8 + 6 - i : f * 8 + 7 - i, :] = ref[at, pl.ds(base + i, 1), :]


def inside_kernel(u, q, g, tables, *rest):
    outs = rest[:4]
    term, spec = rest[4:]
    for c, count in ((0, 53), (1, 53), (2, 22)):
        value = u[0, 0:56] * g[c, 0:56] + u[1, 0:56] * g[3 + c, 0:56] + q[c, 0:56]
        term[53 * c : 53 * c + count, :] = value[:count]
    to_slots(term[...], tables, spec)
    for j in range(4):
        outs[j][...] = spec[chip_modes(j), :]


def edge_term_kernel(bound, pair, tables, *rest):
    blocks = rest[:4]
    u, q, g, term, modes, count, own, other, other_edge = rest[4:]
    me, part = lax.axis_index("span"), lax.axis_index("dom")
    list_pairs(pair, count, own, other, other_edge)
    for j in range(4):
        modes[chip_modes(j), :] = blocks[j][...]
    ph, pw = split(to_planes(jnp.concatenate(pick_slots(modes), axis=1), tables))
    e = bound[0, row_of(me, part)]
    lane = lax.broadcasted_iota(jnp.int32, (32, 128), 1)
    point = lax.broadcasted_iota(jnp.int32, (32, 128), 0)
    slot = jnp.where(lane < 42, 0, jnp.where(lane < 84, 1, 2))
    starts = []
    for t in range(3):
        edge = own[e * 4 + t]
        starts.append(jnp.where(edge < 0, -1000, 7 * edge))
    base = jnp.where(slot == 0, starts[0], jnp.where(slot == 1, starts[1], starts[2]))
    place = lane - slot * 42
    takes = []
    for f in range(6):
        xy, c = f // 3, f % 3
        i = 6 - (place - (c * 14 + xy * 7))
        hit = (i >= 0) & (i <= 6) & (lane < 126) & (point == base + i)
        takes.append(jnp.where(hit, 0.5, 0.0))
    keep = 1.0 - jnp.sum(takes[0], axis=1, keepdims=True)[:28]
    take = jnp.concatenate(takes, axis=0).astype(BF)
    far = dot(take, ph) + dot(take, pw)
    for c in range(3):
        u0, u1 = u[0, 53:81], u[1, 53:81]
        term[31 + 28 * c : 59 + 28 * c, :] = (
            u0 * (g[c, 53:81] * keep + far[c * 32 : c * 32 + 28])
            + u1 * (g[3 + c, 53:81] * keep + far[(3 + c) * 32 : (3 + c) * 32 + 28])
            + q[c, 53:81]
        )
    term[0:31, :] = u[0, 22:53] * g[2, 22:53] + u[1, 22:53] * g[5, 22:53] + q[2, 22:53]
    term[115:128, :] = jnp.zeros((13, NZ), F32)


def whole_kernel(bound, pair, *rest):
    blocks = rest[:4]
    high, low, columns, turn = rest[4:8]
    tables, (gh, gl) = rest[8:12], rest[12:14]
    outs, term, mine = rest[14:18], rest[18], rest[19]
    u, q, g, inside_term, spec, modes = rest[20:26]
    pairs = rest[26:]
    element_kernel(bound, high, low, columns, turn, tables, gh, gl, mine, u, q, g)
    inside_kernel(u, q, g, tables, *outs, inside_term, spec)
    edge_term_kernel(bound, pair, tables, *blocks, u, q, g, term, modes, *pairs)


def side_kernel(bound, term, mine, other, table, *rest):
    tables, outs = rest[:4], rest[4:8]
    work, spec, rows, square, turned = rest[8:]
    me, part = lax.axis_index("span"), lax.axis_index("dom")
    work[...] = term[...]
    rows[0:56] = other[...]
    rows[56:64] = jnp.zeros((8, NZ), F32)
    rh, rl = split(rows[...])
    near = dot(table[0], rh) + dot(table[0], rl) + dot(table[1], rh)
    value = to_planes(jnp.concatenate([near[0:72], slope_slots(near[0:24])], axis=0), tables)
    slope = value[72:96]
    square[...] = jnp.zeros((128, 128), F32)
    square[0:8, :] = other[48:56, 0:128]
    turned[...] = square[...].T
    base = 31 + 7 * bound[1, row_of(me, part)]
    u0 = mine[48:56, :] + value[0:8]
    u1 = mine[56:64, :] + value[8:16]
    for c in range(3):
        along, across = value[24 + 8 * c : 32 + 8 * c], value[48 + 8 * c : 56 + 8 * c]
        gx = mine[8 * c : 8 * c + 8, :] + (turned[0:8, 0:1] * along + turned[0:8, 1:2] * across)
        gy = mine[24 + 8 * c : 32 + 8 * c, :] + (
            turned[7:15, 0:1] * along + turned[7:15, 1:2] * across
        )
        q = mine[64 + 8 * c : 72 + 8 * c, :] + value[16:24] * slope[8 * c : 8 * c + 8]
        mean = (u0 * gx + u1 * gy) * 0.25 + q * 0.5
        for i in range(7):
            work[pl.ds(base + 28 * c + 6 - i, 1), :] = mean[i : i + 1, :]
    to_slots(work[...], tables, spec)
    for j in range(4):
        outs[j][...] = spec[chip_modes(j), :]


def cut_kernel(*rest):
    blocks, cross = rest[:4], rest[4]
    others = pl.ds(pl.multiple_of((1 - (lax.axis_index("span") & 1)) * MODES, MODES), MODES)
    for j in range(4):
        cross[j] = blocks[j][others, :]


def settle_kernel(bound, pair, *rest):
    inside, edge = rest[:4], rest[4:8]
    cross, edge_cross, take, give, where, back, out = rest[8:15]
    packed, edges, far, count, own, other, other_edge = rest[15:]
    me, part = lax.axis_index("span"), lax.axis_index("dom")
    list_pairs(pair, count, own, other, other_edge)
    mine = pl.ds(pl.multiple_of((me & 1) * MODES, MODES), MODES)
    for j in range(4):
        e = bound[0, row_of(me ^ (2 * j), part)]
        packed[e, :, 0:128] = inside[j][mine, :]
        packed[e, :, 128:256] = edge[j][mine, :]
        e = bound[0, row_of(me ^ (2 * j + 1), part)]
        packed[e, :, 0:128] = cross[j]
        packed[e, :, 128:256] = edge_cross[j]
    ph, pw = split(packed[:, :, 128:256].reshape(ELEMS * MODES, 128))
    edges[...] = (dot(ph, take[...]) + dot(pw, take[...])).reshape(ELEMS, MODES, 128)
    lane = lax.broadcasted_iota(jnp.int32, (MODES, 128), 1)
    for e in range(ELEMS):
        total = jnp.zeros((MODES, 128), F32)
        keep = jnp.ones((1, 128), F32)
        for t in range(3):
            edge = own[e * 4 + t]
            shift = (21 * (edge - other_edge[e * 4 + t]) + 128) & 127
            turned = pltpu.roll(edges[other[e * 4 + t]], shift, 1)
            low = edge * 21
            total = jnp.where((lane >= low) & (lane < low + 21) & (edge >= 0), turned, total)
            row = where[pl.ds(jnp.maximum(edge, 0), 1), :]
            keep = keep - jnp.where(edge >= 0, row, 0.0)
        far[e] = total
        packed[e, :, 128:256] = packed[e, :, 128:256] * keep
    fh, fl = split(far[...].reshape(ELEMS * MODES, 128))
    ph, pw = split(packed[...].reshape(ELEMS * MODES, 256))
    done = (
        dot(ph, back[...]) + dot(pw, back[...]) + dot(fh, give[...]) + dot(fl, give[...])
    )
    for e in range(ELEMS):
        for c in range(3):
            out[c, :, e * 81 : e * 81 + 81] = done[e * MODES : (e + 1) * MODES, c * 128 : c * 128 + 81]


def spec_of(space):
    return pl.BlockSpec(memory_space=space)


def call(kernel, name, scalars, arrays, outs, scratch=(), weight=1000):
    shapes = [
        shape if isinstance(shape, jax.ShapeDtypeStruct) else jax.ShapeDtypeStruct(shape, F32)
        for shape in outs
    ]
    return pl.pallas_call(
        kernel,
        out_shape=shapes,
        in_specs=[spec_of(pltpu.SMEM)] * len(scalars)
        + [spec_of(pltpu.VMEM)] * len(arrays),
        out_specs=[spec_of(pltpu.VMEM)] * len(outs),
        scratch_shapes=list(scratch),
        compiler_params=pltpu.CompilerParams(vmem_limit_bytes=LIMIT),
        cost_estimate=pl.CostEstimate(flops=weight, bytes_accessed=weight, transcendentals=0),
        name=name,
    )(*scalars, *arrays)


def pair_scratch():
    return [pltpu.SMEM((n,), jnp.int32) for n in (ELEMS, ELEMS * 4, ELEMS * 4, ELEMS * 4)]


def between_chips(blocks, order=(3, 2, 1)):
    far = {
        j: lax.ppermute(blocks[j], "span", [(s, s ^ (2 * j)) for s in range(SPAN)])
        for j in order
    }
    return [blocks[0], far[1], far[2], far[3]]


def between_cores(block):
    return lax.ppermute(block, "span", [(s, s ^ 1) for s in range(SPAN)])


def side_swap(block, parts):
    def device(part, row, side):
        return ((row ^ (3 * (part & 1))) * 2 + side) * parts + part

    perm = []
    for part in range(parts):
        before = (part - 1) % parts
        for row in range(ROWS):
            perm.append((device(part, row, 0), device(before, row, 1)))
            perm.append((device(before, row, 1), device(part, row, 0)))
    return lax.ppermute(block, ("span", "dom"), perm)


def on_device(velocity_modes, metric, pair_table, bound_table):
    cosines, sines = span_tables()
    tables = [*halves(cosines), *halves(sines)]
    gh, gl = halves(gradient_table())
    edge_table, pick = edge_tables()
    take, give, where, back = settle_tables()
    turn = halves(order_table())[0]
    chip, edge_chip = (2 * MODES, 256), (2 * MODES, 128)
    side_rows = jnp.pad(bound_table.T, ((0, 0), (0, PAIRS - 2 * ROWS)))
    bound_table = pair_table = jnp.concatenate([side_rows, pair_table.T], axis=0)
    flags = [pltpu.SMEM((ELEMS,), jnp.int32)]

    there = between_cores(velocity_modes)
    (ready,) = call(
        ready_kernel, "ready", [bound_table], [velocity_modes], [(8, 128)], weight=LONG
    )
    there, ready = lax.optimization_barrier((there, ready))
    packed, *blocks = call(
        pack_kernel,
        "pack",
        [bound_table],
        [velocity_modes, there, ready],
        [(ELEMS, 2 * MODES, 256)] + [chip] * 4,
        flags,
        weight=LONG,
    )
    blocks = between_chips(blocks)
    packed, scale, columns, terms = call(
        metric_kernel,
        "metric",
        [bound_table],
        [packed, velocity_modes, there, metric, pick, turn],
        [(ELEMS, 2 * MODES, 256), (64, 1, 128), (96, 128), (8, 128)],
        [pltpu.VMEM((16, 256), F32), pltpu.VMEM((16, 1, 256), F32), pltpu.VMEM((128, 128), F32)]
        + flags,
        weight=LONG,
    )
    blocks[3], packed = lax.optimization_barrier((blocks[3], packed))
    edge_blocks = call(
        edge_kernel,
        "edges",
        [bound_table, pair_table],
        [packed, scale, edge_table],
        [edge_chip] * 4,
        pair_scratch(),
        weight=LONG,
    )
    edge_blocks = between_chips(edge_blocks)
    half = jax.ShapeDtypeStruct((256, NZ), BF)
    send, high, low = call(
        rim_kernel,
        "rim",
        [bound_table],
        [*blocks, terms, rim_table()],
        [(56, NZ), half, half],
        [pltpu.VMEM((2, NZ, 128), F32), pltpu.VMEM((256, NZ), F32)],
    )
    other = side_swap(send, lax.axis_size("dom"))
    modes_scratch = pltpu.VMEM((NZ, 128), F32)
    term_scratch = pltpu.VMEM((128, NZ), F32)
    *inside, term, mine = call(
        whole_kernel,
        "whole",
        [bound_table, pair_table],
        [*edge_blocks, high, low, columns, turn, *tables, gh, gl],
        [edge_chip] * 4 + [(128, NZ), (88, NZ)],
        [
            pltpu.VMEM((3, 88, NZ), F32),
            pltpu.VMEM((3, 88, NZ), F32),
            pltpu.VMEM((6, 88, NZ), F32),
            term_scratch,
            modes_scratch,
            modes_scratch,
        ]
        + pair_scratch(),
    )
    inside = between_chips(inside)
    edge = call(
        side_kernel,
        "side",
        [bound_table],
        [term, mine, other, np.stack(halves(far_table())), *tables],
        [edge_chip] * 4,
        [
            term_scratch,
            modes_scratch,
            pltpu.VMEM((64, NZ), F32),
            pltpu.VMEM((128, 128), F32),
            pltpu.VMEM((128, 128), F32),
        ],
    )
    edge = between_chips(edge)
    (cross,) = call(cut_kernel, "cut", [], inside, [(4, MODES, 128)])
    (edge_cross,) = call(cut_kernel, "cut_edge", [], edge, [(4, MODES, 128)])
    (out,) = call(
        settle_kernel,
        "settle",
        [bound_table, pair_table],
        [
            *inside,
            *edge,
            between_cores(cross),
            between_cores(edge_cross),
            *(halves(table)[0] for table in (take, give)),
            where.astype(np.float32),
            halves(back)[0],
        ],
        [(3, MODES, ELEMS * PTS)],
        [
            pltpu.VMEM((ELEMS, MODES, 256), F32),
            pltpu.VMEM((ELEMS, MODES, 128), F32),
            pltpu.VMEM((ELEMS, MODES, 128), F32),
        ]
        + pair_scratch(),
    )
    return out


def solution(mesh):
    return jax.shard_map(
        on_device,
        mesh=mesh,
        in_specs=(P(None, "span", "dom"), P(None, "dom"), P("dom", None), P("dom", None)),
        out_specs=P(None, "span", "dom"),
        check_vma=False,
    )
```

```python
import jax
import jax.numpy as jnp
import ml_dtypes
import numpy as np
from jax import lax
from jax.experimental import pallas as pl
from jax.experimental.pallas import tpu as pltpu
from jax.sharding import PartitionSpec as P

NZ = 512
HALF = 256
PTS = 81
ELEMS = 8
ROWS = 4
PAIRS = 10
SPAN = 8
MODES = NZ // SPAN
SPAN_RATE = 1.0 / 32.0
BF = jnp.bfloat16
F32 = jnp.float32
LIMIT = 48 * 1024 * 1024
LONG = 200_000_000


def legendre_rows(abscissa, node_count):
    legendre = np.zeros((node_count, node_count))
    legendre[:, 0] = 1.0
    legendre[:, 1] = abscissa
    for degree in range(2, node_count):
        legendre[:, degree] = (
            (2 * degree - 1) * abscissa * legendre[:, degree - 1]
            - (degree - 1) * legendre[:, degree - 2]
        ) / degree
    return legendre


def lobatto_matrix(order):
    node_count = order + 1
    abscissa = -np.cos(np.pi * np.arange(node_count) / order)
    for _ in range(60):
        legendre = legendre_rows(abscissa, node_count)
        abscissa = abscissa - (abscissa * legendre[:, order] - legendre[:, order - 1]) / (
            node_count * legendre[:, order]
        )
    legendre = legendre_rows(abscissa, node_count)
    end_values = legendre[:, order]
    spacing = abscissa[:, None] - abscissa[None, :] + np.eye(node_count)
    matrix = end_values[:, None] / (end_values[None, :] * spacing)
    matrix = matrix * (1.0 - np.eye(node_count))
    matrix[0, 0] = -order * node_count / 4.0
    matrix[order, order] = order * node_count / 4.0
    return matrix


def edge_points():
    positions = np.arange(9)
    outline = [positions, positions * 9 + 8, 72 + (8 - positions), (8 - positions) * 9]
    return np.stack(outline)[:, 1:8]


INSIDE = 53


def point_order():
    edges = edge_points().reshape(-1)
    inside = [point for point in range(PTS) if point not in set(edges.tolist())]
    return np.concatenate([inside, edges]).astype(int)


def lane_of(c, place):
    if place >= INSIDE:
        return 128 + 31 + 28 * c + place - INSIDE
    return 53 * c + place


def halves(table):
    high = table.astype(np.float32).astype(ml_dtypes.bfloat16)
    low = (table - high.astype(np.float64)).astype(np.float32).astype(ml_dtypes.bfloat16)
    return high, low


def span_tables():
    planes = np.arange(HALF)[None, :]
    waves = np.arange(HALF + 16)[:, None]
    angles = (planes * waves % NZ) * (2.0 * np.pi / NZ)
    cosines, sines = np.cos(angles), np.sin(angles)[:HALF]
    sines[0] = 1.0 - 2.0 * (np.arange(HALF) % 2)
    return cosines, sines


def point_matrices():
    lobatto = lobatto_matrix(8)
    return np.kron(np.eye(9), lobatto), np.kron(lobatto, np.eye(9))


def gradient_table():
    along_xi, along_eta = point_matrices()
    order = point_order()
    table = np.zeros((176, 96))
    table[:81, :81] = along_xi[np.ix_(order, order)]
    table[88:169, :81] = along_eta[np.ix_(order, order)]
    return table


def order_table():
    order = point_order()
    table = np.zeros((288, 256))
    for c in range(3):
        for place in range(PTS):
            table[c * 96 + place, c * 81 + order[place]] = 1.0
    return table


def rim_table():
    edges = edge_points()
    mats = point_matrices()
    table = np.zeros((4, 64, 256), ml_dtypes.bfloat16)
    for s in range(4):
        rows = np.zeros((32, 256))
        for c in range(3):
            rows[c * 8 : c * 8 + 7, c * 81 : c * 81 + 81] = mats[(s + 1) % 2][edges[s]]
        table[s, :32], table[s, 32:] = halves(rows)
    return table


def far_table():
    lobatto = lobatto_matrix(8)
    table = np.zeros((80, 64))
    for c in range(3):
        for i in range(7):
            table[c * 8 + i, c * 9 + i + 1] = 1.0
            table[24 + c * 8 + i, c * 9 : c * 9 + 9] = lobatto[i + 1]
            table[48 + c * 8 + i, 27 + c * 7 + i] = 1.0
    return table


def edge_tables():
    edges = edge_points()
    mats = point_matrices()
    table = np.zeros((256, 1024))
    pick = np.zeros((256, 512))
    for s in range(4):
        for t in range(3):
            for c in range(3):
                for xy in range(2):
                    for i in range(7):
                        lane = s * 128 + t * 42 + c * 14 + xy * 7 + i
                        for h in range(2):
                            table[c * 81 : c * 81 + 81, h * 512 + lane] = mats[h][edges[s, i]]
                        pick[xy * 128 + edges[s, i], lane] = 1.0
    high, low = halves(table)
    pick = halves(pick)[0]
    lanes = [slice(s * 128, s * 128 + 128) for s in range(4)]
    later = [slice(512 + s * 128, 640 + s * 128) for s in range(4)]
    return np.stack(
        [
            np.concatenate([high[:, n], high[:, m], low[:, n], low[:, m]], axis=1)
            for n, m in zip(lanes, later)
        ]
    ), pick


def settle_tables():
    order = point_order()
    take = np.zeros((128, 128))
    give = np.zeros((128, 384))
    where = np.zeros((8, 128))
    back = np.zeros((256, 384))
    for c in range(3):
        for place in range(PTS):
            back[lane_of(c, place), c * 128 + order[place]] = 1.0
        for s in range(4):
            for i in range(7):
                lane = s * 21 + c * 7 + i
                place = INSIDE + s * 7 + i
                take[lane_of(c, INSIDE + s * 7 + 6 - i) - 128, lane] = 1.0
                give[lane, c * 128 + order[place]] = 0.5
                where[s, lane_of(c, place) - 128] = 0.5
    return take, give, where, back


def row_of(place, part):
    return (place & 1) * ROWS + ((place >> 1) ^ (3 * (part & 1)))


def split(x):
    high = x.astype(BF)
    return high, (x - high.astype(F32)).astype(BF)


def dot(a, b, dims=((1,), (0,))):
    return lax.dot_general(a, b, (dims, ((), ())), preferred_element_type=F32)


def pick_slots(modes):
    even, odd = modes[pl.ds(0, HALF, stride=2), :], modes[pl.ds(1, HALF, stride=2), :]
    return even.T, odd.T


def to_planes(x, tables):
    ch, cl, sh, sl = tables
    high, low = split(x)
    ch, cl = ch[0:HALF], cl[0:HALF]
    sh, sl = sh[...], sl[...]
    even = dot(high[:, :HALF], ch) + dot(low[:, :HALF], ch) + dot(high[:, :HALF], cl)
    odd = dot(high[:, HALF:], sh) + dot(low[:, HALF:], sh) + dot(high[:, HALF:], sl)
    lane = lax.broadcasted_iota(jnp.int32, even.shape, 1)
    sign = jnp.where((lane & 1) == 0, 1.0, -1.0)
    lone = x[:, HALF : HALF + 1]
    middle = jnp.sum(x[:, :HALF] * sign, axis=1, keepdims=True) + lone
    mirror = jnp.where(lane == 0, middle, even - odd + (lone + lone) * sign)
    return jnp.concatenate([even + odd, mirror], axis=1)


def slope_slots(x):
    lane = lax.broadcasted_iota(jnp.int32, (x.shape[0], HALF), 1)
    rate = lane.astype(F32) * SPAN_RATE
    return jnp.concatenate([x[:, HALF:] * rate, -x[:, :HALF] * rate], axis=1)


def to_slots(term, tables, spec):
    ch, cl, sh, sl = tables
    first, mirror = term[:, :HALF], term[:, HALF:]
    lane = lax.broadcasted_iota(jnp.int32, first.shape, 1)
    eh, el = split(jnp.where(lane == 0, first, first + mirror))
    oh, ol = split(first - mirror)
    along = ((1,), (1,))
    even = dot(ch[...], eh, along) + dot(ch[...], el, along) + dot(cl[...], eh, along)
    odd = dot(sh[...], oh, along) + dot(sh[...], ol, along) + dot(sl[...], oh, along)
    row = lax.broadcasted_iota(jnp.int32, even.shape, 0)
    middle = mirror[:, 0:128].T[0:1, :]
    even = even + jnp.where((row & 1) == 0, 1.0, -1.0) * middle
    row = row[:HALF]
    lone = even[HALF : HALF + 1] * (1.0 / NZ)
    spec[pl.ds(0, HALF, stride=2), :] = even[:HALF] * jnp.where(row == 0, 1.0 / NZ, 2.0 / NZ)
    spec[pl.ds(1, HALF, stride=2), :] = jnp.where(row == 0, lone, odd * (2.0 / NZ))


def list_pairs(pair, count, own, other, other_edge):
    for e in range(ELEMS):
        count[e] = 0
    for n in range(ELEMS * 4):
        own[n] = -1
        other[n] = 0
        other_edge[n] = 0
    for row in range(PAIRS):
        for first, second in ((0, 2), (2, 0)):
            e = pair[first, row]
            slot = e * 4 + count[e]
            own[slot] = pair[first + 1, row]
            other[slot] = pair[second, row]
            other_edge[slot] = pair[second + 1, row]
            count[e] = count[e] + 1


def chip_modes(j):
    chip = (lax.axis_index("span") >> 1) ^ j
    return pl.ds(pl.multiple_of(chip * 2 * MODES, 2 * MODES), 2 * MODES)


def ready_kernel(bound, here, out):
    out[...] = here[0, 0:8, 0:128] + jnp.full((8, 128), bound[0, 0], jnp.int32).astype(F32)


def pack_element(packed, e, core, here, there):
    for at, v in ((core, here), (1 - core, there)):
        rows = pl.ds(pl.multiple_of(at * MODES, MODES), MODES)
        for c in range(3):
            packed[e, rows, c * 81 : c * 81 + 81] = v[c, :, e * 81 : e * 81 + 81]
        packed[e, rows, 243:256] = jnp.zeros((MODES, 13), F32)


def column_flags(bound, core, flags):
    for e in range(ELEMS):
        flags[e] = 0
    for row in range(ROWS):
        flags[bound[0, core * ROWS + row]] = 1


def pack_kernel(bound, here, there, ready, packed, *rest):
    outs, flags = rest[:4], rest[4]
    me, part = lax.axis_index("span"), lax.axis_index("dom")
    core = me & 1
    column_flags(bound, core, flags)
    for e in range(ELEMS):
        pl.when(flags[e] == 1)(lambda e=e: pack_element(packed, e, core, here, there))
    for j in range(4):
        outs[j][...] = packed[bound[0, row_of(me ^ (2 * j), part)]]


def metric_kernel(
    bound, done, here, there, metric, pick, turn, packed, scale, columns, terms, rows, lines, square, flags
):
    me, part = lax.axis_index("span"), lax.axis_index("dom")
    core = me & 1
    column_flags(bound, core, flags)

    def copy_element(e):
        packed[e] = done[e]

    for e in range(ELEMS):
        pl.when(flags[e] == 1)(lambda e=e: copy_element(e))
        pl.when(flags[e] == 0)(lambda e=e: pack_element(packed, e, core, here, there))
    rows[...] = jnp.zeros((16, 256), F32)
    for e in range(ELEMS):
        for j in range(4):
            at = e + 8 * (j // 2)
            lane = 128 * (j % 2)
            rows[at : at + 1, lane : lane + 81] = metric[j : j + 1, e * 81 : e * 81 + 81]
    rows_high, rows_low = split(rows[...])
    for s in range(4):
        here_lanes = pick[:, s * 128 : s * 128 + 128]
        size = dot(rows_high, here_lanes) + dot(rows_low, here_lanes)
        for n in range(16):
            scale[n * 4 + s] = size[n : n + 1, :]
    for n in range(16):
        lines[n] = rows[n : n + 1, :]
    square[...] = jnp.zeros((128, 128), F32)
    mine = bound[0, row_of(me, part)]
    for j in range(4):
        line = lines[mine + 8 * (j // 2)]
        square[j : j + 1, :] = line[:, 128 * (j % 2) : 128 * (j % 2) + 128]
    high, low = split(square[...].T)
    columns[...] = dot(turn[0:96, 0:128], high) + dot(turn[0:96, 0:128], low)
    side = bound[1, row_of(me, part)]
    along, across = scale[mine * 4 + side], scale[(8 + mine) * 4 + side]
    even = (side & 1) == 0
    terms[...] = jnp.zeros((8, 128), F32)
    terms[0:1, :] = jnp.where(side < 2, 1.0, -1.0) * jnp.where(even, along, across)
    terms[1:2, :] = jnp.where(even, across, along)


def edge_kernel(bound, pair, packed, scale, table, *rest):
    outs = rest[:4]
    count, own, other, other_edge = rest[4:]
    me, part = lax.axis_index("span"), lax.axis_index("dom")
    list_pairs(pair, count, own, other, other_edge)
    lane = lax.broadcasted_iota(jnp.int32, (2 * MODES, 128), 1)
    for j in range(4):
        e = bound[0, row_of(me ^ (2 * j), part)]
        total = jnp.zeros((2 * MODES, 128), F32)
        for t in range(3):
            far, edge = other[e * 4 + t], other_edge[e * 4 + t]
            vh, vl = split(packed[far])
            high = table[edge, :, 0:256]
            value = dot(vh, high) + dot(vl, high) + dot(vh, table[edge, :, 256:512])
            value = (
                value[:, :128] * scale[far * 4 + edge]
                + value[:, 128:] * scale[(8 + far) * 4 + edge]
            )
            total = jnp.where((lane >= t * 42) & (lane < t * 42 + 42), value, total)
        outs[j][...] = total


def rim_kernel(bound, *rest):
    blocks = rest[:4]
    terms, table, send, high, low, modes, points = rest[4:]
    me, part = lax.axis_index("span"), lax.axis_index("dom")
    for j in range(4):
        for t in range(2):
            modes[t, chip_modes(j), :] = blocks[j][:, t * 128 : t * 128 + 128]
    for t in range(2):
        rows = slice(t * 128, t * 128 + 128)
        points[rows, 0:HALF], points[rows, HALF:] = pick_slots(modes.at[t])
    vh, vl = split(points[...])
    high[...] = vh
    low[...] = vl
    side = bound[1, row_of(me, part)]
    rows = dot(table[side], vh)
    across = rows[:32] + rows[32:] + dot(table[side, 0:32], vl)
    base = jnp.where(side == 0, 0, jnp.where(side == 1, 8, jnp.where(side == 2, 80, 72)))
    step = jnp.where(side == 0, 1, jnp.where(side == 1, 9, jnp.where(side == 2, -1, -9)))
    for c in range(3):
        for i in range(9):
            send[c * 9 + i : c * 9 + i + 1, :] = points[pl.ds(c * 81 + base + step * i, 1), :]
        send[27 + c * 7 : 34 + c * 7, :] = across[c * 8 : c * 8 + 7]
    send[48:56, :] = jnp.zeros((8, NZ), F32)
    send[48:56, 0:128] = terms[...]


def element_kernel(bound, high, low, columns, turn, tables, gh, gl, mine, u, q, g, more):
    me, part = lax.axis_index("span"), lax.axis_index("dom")
    slots = dot(turn[...], high[...]) + dot(turn[...], low[...])
    every = to_planes(jnp.concatenate([slots, slope_slots(slots), more], axis=0), tables)
    value, slope, rest = every[:288], every[288:576], every[576:]
    uh, ul = split(value)
    third = value[192:280]
    for c in range(3):
        rows = slice(96 * c, 96 * c + 96)
        both = dot(gh[...], uh[rows]) + dot(gh[...], ul[rows]) + dot(gl[...], uh[rows])
        fx, fe = both[:88], both[88:]
        g[c] = columns[0:88, 0:1] * fx + columns[0:88, 2:3] * fe
        g[3 + c] = columns[0:88, 1:2] * fx + columns[0:88, 3:4] * fe
        u[c] = value[96 * c : 96 * c + 88]
        q[c] = third * slope[96 * c : 96 * c + 88]
    base = INSIDE + 7 * bound[1, row_of(me, part)]
    mine[...] = jnp.zeros((88, NZ), F32)
    order = [(g, f) for f in range(6)] + [(u, 0), (u, 1)] + [(q, c) for c in range(3)]
    for f, (ref, at) in enumerate(order):
        for i in range(7):
            mine[f * 8 + 6 - i : f * 8 + 7 - i, :] = ref[at, pl.ds(base + i, 1), :]
    return rest


def inside_kernel(u, q, g, tables, *rest):
    outs = rest[:4]
    term, spec = rest[4:]
    for c, count in ((0, 53), (1, 53), (2, 22)):
        value = u[0, 0:56] * g[c, 0:56] + u[1, 0:56] * g[3 + c, 0:56] + q[c, 0:56]
        term[53 * c : 53 * c + count, :] = value[:count]
    to_slots(term[...], tables, spec)
    for j in range(4):
        outs[j][...] = spec[chip_modes(j), :]


def edge_term_kernel(bound, pair, planes, *rest):
    u, q, g, term, count, own, other, other_edge = rest
    me, part = lax.axis_index("span"), lax.axis_index("dom")
    list_pairs(pair, count, own, other, other_edge)
    ph, pw = split(planes)
    e = bound[0, row_of(me, part)]
    lane = lax.broadcasted_iota(jnp.int32, (32, 128), 1)
    point = lax.broadcasted_iota(jnp.int32, (32, 128), 0)
    slot = jnp.where(lane < 42, 0, jnp.where(lane < 84, 1, 2))
    starts = []
    for t in range(3):
        edge = own[e * 4 + t]
        starts.append(jnp.where(edge < 0, -1000, 7 * edge))
    base = jnp.where(slot == 0, starts[0], jnp.where(slot == 1, starts[1], starts[2]))
    place = lane - slot * 42
    takes = []
    for f in range(6):
        xy, c = f // 3, f % 3
        i = 6 - (place - (c * 14 + xy * 7))
        hit = (i >= 0) & (i <= 6) & (lane < 126) & (point == base + i)
        takes.append(jnp.where(hit, 0.5, 0.0))
    keep = 1.0 - jnp.sum(takes[0], axis=1, keepdims=True)[:28]
    take = jnp.concatenate(takes, axis=0).astype(BF)
    far = dot(take, ph) + dot(take, pw)
    for c in range(3):
        u0, u1 = u[0, 53:81], u[1, 53:81]
        term[31 + 28 * c : 59 + 28 * c, :] = (
            u0 * (g[c, 53:81] * keep + far[c * 32 : c * 32 + 28])
            + u1 * (g[3 + c, 53:81] * keep + far[(3 + c) * 32 : (3 + c) * 32 + 28])
            + q[c, 53:81]
        )
    term[0:31, :] = u[0, 22:53] * g[2, 22:53] + u[1, 22:53] * g[5, 22:53] + q[2, 22:53]
    term[115:128, :] = jnp.zeros((13, NZ), F32)


def whole_kernel(bound, pair, *rest):
    blocks = rest[:4]
    high, low, columns, turn = rest[4:8]
    tables, (gh, gl) = rest[8:12], rest[12:14]
    outs, term, mine = rest[14:18], rest[18], rest[19]
    u, q, g, inside_term, spec, modes = rest[20:26]
    pairs = rest[26:]
    for j in range(4):
        modes[chip_modes(j), :] = blocks[j][...]
    more = jnp.concatenate(pick_slots(modes), axis=1)
    planes = element_kernel(bound, high, low, columns, turn, tables, gh, gl, mine, u, q, g, more)
    inside_kernel(u, q, g, tables, *outs, inside_term, spec)
    edge_term_kernel(bound, pair, planes, u, q, g, term, *pairs)


def side_kernel(bound, term, mine, other, table, *rest):
    tables, outs = rest[:4], rest[4:8]
    work, spec, rows, square, turned = rest[8:]
    me, part = lax.axis_index("span"), lax.axis_index("dom")
    work[...] = term[...]
    rows[0:56] = other[...]
    rows[56:64] = jnp.zeros((8, NZ), F32)
    rh, rl = split(rows[...])
    near = dot(table[0], rh) + dot(table[0], rl) + dot(table[1], rh)
    value = to_planes(jnp.concatenate([near[0:72], slope_slots(near[0:24])], axis=0), tables)
    slope = value[72:96]
    square[...] = jnp.zeros((128, 128), F32)
    square[0:8, :] = other[48:56, 0:128]
    turned[...] = square[...].T
    base = 31 + 7 * bound[1, row_of(me, part)]
    u0 = mine[48:56, :] + value[0:8]
    u1 = mine[56:64, :] + value[8:16]
    for c in range(3):
        along, across = value[24 + 8 * c : 32 + 8 * c], value[48 + 8 * c : 56 + 8 * c]
        gx = mine[8 * c : 8 * c + 8, :] + (turned[0:8, 0:1] * along + turned[0:8, 1:2] * across)
        gy = mine[24 + 8 * c : 32 + 8 * c, :] + (
            turned[7:15, 0:1] * along + turned[7:15, 1:2] * across
        )
        q = mine[64 + 8 * c : 72 + 8 * c, :] + value[16:24] * slope[8 * c : 8 * c + 8]
        mean = (u0 * gx + u1 * gy) * 0.25 + q * 0.5
        for i in range(7):
            work[pl.ds(base + 28 * c + 6 - i, 1), :] = mean[i : i + 1, :]
    to_slots(work[...], tables, spec)
    for j in range(4):
        outs[j][...] = spec[chip_modes(j), :]


def cut_kernel(*rest):
    blocks, cross = rest[:4], rest[4]
    others = pl.ds(pl.multiple_of((1 - (lax.axis_index("span") & 1)) * MODES, MODES), MODES)
    for j in range(4):
        cross[j] = blocks[j][others, :]


def settle_kernel(bound, pair, *rest):
    inside, edge = rest[:4], rest[4:8]
    cross, edge_cross, take, give, where, back, out = rest[8:15]
    packed, edges, far, count, own, other, other_edge = rest[15:]
    me, part = lax.axis_index("span"), lax.axis_index("dom")
    list_pairs(pair, count, own, other, other_edge)
    mine = pl.ds(pl.multiple_of((me & 1) * MODES, MODES), MODES)
    for j in range(4):
        e = bound[0, row_of(me ^ (2 * j), part)]
        packed[e, :, 0:128] = inside[j][mine, :]
        packed[e, :, 128:256] = edge[j][mine, :]
        e = bound[0, row_of(me ^ (2 * j + 1), part)]
        packed[e, :, 0:128] = cross[j]
        packed[e, :, 128:256] = edge_cross[j]
    ph, pw = split(packed[:, :, 128:256].reshape(ELEMS * MODES, 128))
    edges[...] = (dot(ph, take[...]) + dot(pw, take[...])).reshape(ELEMS, MODES, 128)
    lane = lax.broadcasted_iota(jnp.int32, (MODES, 128), 1)
    for e in range(ELEMS):
        total = jnp.zeros((MODES, 128), F32)
        keep = jnp.ones((1, 128), F32)
        for t in range(3):
            edge = own[e * 4 + t]
            shift = (21 * (edge - other_edge[e * 4 + t]) + 128) & 127
            turned = pltpu.roll(edges[other[e * 4 + t]], shift, 1)
            low = edge * 21
            total = jnp.where((lane >= low) & (lane < low + 21) & (edge >= 0), turned, total)
            row = where[pl.ds(jnp.maximum(edge, 0), 1), :]
            keep = keep - jnp.where(edge >= 0, row, 0.0)
        far[e] = total
        packed[e, :, 128:256] = packed[e, :, 128:256] * keep
    fh, fl = split(far[...].reshape(ELEMS * MODES, 128))
    ph, pw = split(packed[...].reshape(ELEMS * MODES, 256))
    done = (
        dot(ph, back[...]) + dot(pw, back[...]) + dot(fh, give[...]) + dot(fl, give[...])
    )
    for e in range(ELEMS):
        for c in range(3):
            out[c, :, e * 81 : e * 81 + 81] = done[e * MODES : (e + 1) * MODES, c * 128 : c * 128 + 81]


def spec_of(space):
    return pl.BlockSpec(memory_space=space)


def call(kernel, name, scalars, arrays, outs, scratch=(), weight=1000):
    shapes = [
        shape if isinstance(shape, jax.ShapeDtypeStruct) else jax.ShapeDtypeStruct(shape, F32)
        for shape in outs
    ]
    return pl.pallas_call(
        kernel,
        out_shape=shapes,
        in_specs=[spec_of(pltpu.SMEM)] * len(scalars)
        + [spec_of(pltpu.VMEM)] * len(arrays),
        out_specs=[spec_of(pltpu.VMEM)] * len(outs),
        scratch_shapes=list(scratch),
        compiler_params=pltpu.CompilerParams(vmem_limit_bytes=LIMIT),
        cost_estimate=pl.CostEstimate(flops=weight, bytes_accessed=weight, transcendentals=0),
        name=name,
    )(*scalars, *arrays)


def pair_scratch():
    return [pltpu.SMEM((n,), jnp.int32) for n in (ELEMS, ELEMS * 4, ELEMS * 4, ELEMS * 4)]


def between_chips(blocks, order=(3, 2, 1)):
    far = {
        j: lax.ppermute(blocks[j], "span", [(s, s ^ (2 * j)) for s in range(SPAN)])
        for j in order
    }
    return [blocks[0], far[1], far[2], far[3]]


def between_cores(block):
    return lax.ppermute(block, "span", [(s, s ^ 1) for s in range(SPAN)])


def side_swap(block, parts):
    def device(part, row, side):
        return ((row ^ (3 * (part & 1))) * 2 + side) * parts + part

    perm = []
    for part in range(parts):
        before = (part - 1) % parts
        for row in range(ROWS):
            perm.append((device(part, row, 0), device(before, row, 1)))
            perm.append((device(before, row, 1), device(part, row, 0)))
    return lax.ppermute(block, ("span", "dom"), perm)


def on_device(velocity_modes, metric, pair_table, bound_table):
    cosines, sines = span_tables()
    tables = [*halves(cosines), *halves(sines)]
    gh, gl = halves(gradient_table())
    edge_table, pick = edge_tables()
    take, give, where, back = settle_tables()
    turn = halves(order_table())[0]
    chip, edge_chip = (2 * MODES, 256), (2 * MODES, 128)
    pair_table, bound_table = pair_table.T, bound_table.T
    flags = [pltpu.SMEM((ELEMS,), jnp.int32)]

    there = between_cores(velocity_modes)
    (ready,) = call(
        ready_kernel, "ready", [bound_table], [velocity_modes], [(8, 128)], weight=LONG
    )
    there, ready = lax.optimization_barrier((there, ready))
    packed, *blocks = call(
        pack_kernel,
        "pack",
        [bound_table],
        [velocity_modes, there, ready],
        [(ELEMS, 2 * MODES, 256)] + [chip] * 4,
        flags,
        weight=LONG,
    )
    blocks = between_chips(blocks)
    packed, scale, columns, terms = call(
        metric_kernel,
        "metric",
        [bound_table],
        [packed, velocity_modes, there, metric, pick, turn],
        [(ELEMS, 2 * MODES, 256), (64, 1, 128), (96, 128), (8, 128)],
        [pltpu.VMEM((16, 256), F32), pltpu.VMEM((16, 1, 256), F32), pltpu.VMEM((128, 128), F32)]
        + flags,
        weight=LONG,
    )
    blocks[3], packed = lax.optimization_barrier((blocks[3], packed))
    edge_blocks = call(
        edge_kernel,
        "edges",
        [bound_table, pair_table],
        [packed, scale, edge_table],
        [edge_chip] * 4,
        pair_scratch(),
        weight=LONG,
    )
    edge_blocks = between_chips(edge_blocks)
    half = jax.ShapeDtypeStruct((256, NZ), BF)
    send, high, low = call(
        rim_kernel,
        "rim",
        [bound_table],
        [*blocks, terms, rim_table()],
        [(56, NZ), half, half],
        [pltpu.VMEM((2, NZ, 128), F32), pltpu.VMEM((256, NZ), F32)],
    )
    other = side_swap(send, lax.axis_size("dom"))
    modes_scratch = pltpu.VMEM((NZ, 128), F32)
    term_scratch = pltpu.VMEM((128, NZ), F32)
    *inside, term, mine = call(
        whole_kernel,
        "whole",
        [bound_table, pair_table],
        [*edge_blocks, high, low, columns, turn, *tables, gh, gl],
        [edge_chip] * 4 + [(128, NZ), (88, NZ)],
        [
            pltpu.VMEM((3, 88, NZ), F32),
            pltpu.VMEM((3, 88, NZ), F32),
            pltpu.VMEM((6, 88, NZ), F32),
            term_scratch,
            modes_scratch,
            modes_scratch,
        ]
        + pair_scratch(),
    )
    inside = between_chips(inside)
    edge = call(
        side_kernel,
        "side",
        [bound_table],
        [term, mine, other, np.stack(halves(far_table())), *tables],
        [edge_chip] * 4,
        [
            term_scratch,
            modes_scratch,
            pltpu.VMEM((64, NZ), F32),
            pltpu.VMEM((128, 128), F32),
            pltpu.VMEM((128, 128), F32),
        ],
    )
    edge = between_chips(edge)
    (cross,) = call(cut_kernel, "cut", [], inside, [(4, MODES, 128)])
    (edge_cross,) = call(cut_kernel, "cut_edge", [], edge, [(4, MODES, 128)])
    (out,) = call(
        settle_kernel,
        "settle",
        [bound_table, pair_table],
        [
            *inside,
            *edge,
            between_cores(cross),
            between_cores(edge_cross),
            *(halves(table)[0] for table in (take, give)),
            where.astype(np.float32),
            halves(back)[0],
        ],
        [(3, MODES, ELEMS * PTS)],
        [
            pltpu.VMEM((ELEMS, MODES, 256), F32),
            pltpu.VMEM((ELEMS, MODES, 128), F32),
            pltpu.VMEM((ELEMS, MODES, 128), F32),
        ]
        + pair_scratch(),
    )
    return out


def solution(mesh):
    return jax.shard_map(
        on_device,
        mesh=mesh,
        in_specs=(P(None, "span", "dom"), P(None, "dom"), P("dom", None), P("dom", None)),
        out_specs=P(None, "span", "dom"),
        check_vma=False,
    )
```
